128 devices in a mesh: front: 4 (over x), row: 4 (over z), col: 8 (over y, core).
Axes of the slice: x: 4, y: 4, z: 4, core: 2. Of those that a mesh axis runs over, the one named last changes fastest.
Arguments:
- tiles: float32 [4096, 256, 256], P(('front', 'row', 'col')), may hold values from -6 to 6
- dest: int32 [4096, 1], P(('front', 'row', 'col')), may hold values from 0 to 15; in each aligned block of 32 rows (0 to 31, 32 to 63, ...) at most 4 rows name the same one
- block_row: int32 [4096], P(('front', 'row', 'col')), may hold values from 0 to 9
- block_col: int32 [4096], P(('front', 'row', 'col')), may hold values from 0 to 4
- rows_from: int32 [4096, 256], P(('front', 'row', 'col')), may hold values from 0 to 255, each once within a row
- cols_from: int32 [4096, 256], P(('front', 'row', 'col')), may hold values from 0 to 255, each once within a row
- initial: float32 [4, 10240, 512], P('front', 'row', 'col'), may hold values from -6 to 60, as said below
- pattern: int32 [4, 2, 40], P('front'), may hold values 0 or 1
Outputs:
- factored: float32 [4, 10240, 10240], P('front', 'row', 'col')
The draws below stay inside these ranges and needn't reach their ends.
Inputs may be any that keep to these rules, and one draw needn't show every extreme that they name: `dest`: in the rows of one device no destination is named by more than 4 tiles, a bound that some block reaches. `rows_from`: each row is a permutation. `cols_from`: each row is a permutation. `initial`: the first 512 rows form a symmetric block whose diagonal entries exceed the sum of magnitudes of the other entries in their rows.
All inputs are finite; a program needn't handle non-finite values. No bound on the sum of `pattern` on one device may be relied on, other than what follows from the above.
Results may differ from the reference program's by a relative error of at most 0.0001.
Values sent between devices are 32-bit elements; how exact they have to be, the bound alone decides.
No kernel may reach another device: no remote copies, remote signals or barrier semaphores. Data moves between devices by JAX's collectives and lax.ppermute only.
A program may use at most 192 MiB of HBM per device.

```python
import math
import jax
import jax.numpy as jnp
import numpy as np
from jax import lax

ORDER = 10240
BS = 256
NPANEL = 2
CAP = 4
CB_DEV = 32
FRONTS = 4
TILES = 4096
NBLK = 40
PIV = 512
N_FRONT = 4
N_ROW = 4
N_COL = 8


def draw_initial(key, part):
    key = jax.random.fold_in(key, 7)
    keys = jax.random.split(key, 3)
    spread = jax.random.uniform(keys[0], (FRONTS, PIV, PIV), jnp.float32, -0.5, 0.5) / 16.0
    below = jnp.clip(jax.random.normal(keys[1], (FRONTS, ORDER - PIV, PIV), jnp.float32), -6.0, 6.0)
    diag = jax.random.uniform(keys[2], (FRONTS, PIV), jnp.float32, 40.0, 60.0)
    sym = (spread + jnp.swapaxes(spread, 1, 2)) * 0.5
    eye = jnp.eye(PIV, dtype=jnp.float32)
    pivot = sym * (1.0 - eye) + eye * diag[:, :, None]
    return jnp.concatenate([pivot, below], axis=1)


def place_ends(drawn, own_key, least, high):
    spot = [jax.random.randint(jax.random.fold_in(own_key, axis), (), 0, length) for axis, length in enumerate(drawn.shape)]
    widest = drawn.shape.index(max(drawn.shape))
    neighbour = spot[:widest] + [(spot[widest] + 1) % drawn.shape[widest]] + spot[widest + 1:]
    return drawn.at[tuple(spot)].set(least).at[tuple(neighbour)].set(high)


def block_scale(stream_key, shape, pieces, smallest, high):
    def one(dim, parts):
        draws = jax.random.uniform(jax.random.fold_in(jax.random.fold_in(stream_key, 6), dim), (parts,), jnp.float32, smallest / len(pieces), high / len(pieces))
        return jnp.repeat(jnp.exp(draws), shape[dim] // parts).reshape((-1,) + (1,) * (len(shape) - dim - 1))

    level = one(*pieces[0])
    for cut in pieces[1:]:
        level = level * one(*cut)
    return level


def shared_out(own_key, own, number, rows, count, top, bound, lean):
    ranking = jax.random.permutation(own_key, count)
    packed, ordinary = load_shares(count, rows * top, bound, lean, True), load_shares(count, rows * top, bound, lean, False)
    places = jnp.arange(count)

    def named(tallies, offset_by):
        used = int((tallies > 0).sum())
        fixed = max(1, used // 4)
        passed = fixed + (places - fixed + offset_by * (used - fixed)) % max(1, count - fixed)
        return jnp.zeros((count,), jnp.int32).at[ranking[jnp.where(places < fixed, places, passed)]].set(jnp.asarray(tallies, jnp.int32))

    tallies = jnp.where(number % 4 == 0, named(packed, number // 4), named(ordinary, number - number // 4 - 1))
    mixed = jax.random.permutation(jax.random.fold_in(own, 3), count)
    source_of, taker = mixed[0:count // 2 * 2:2], mixed[1:count // 2 * 2:2]
    room = jnp.minimum(tallies[source_of] - 1, bound - tallies[taker]) // 2
    room = jnp.where((source_of == ranking[0]) | (taker == ranking[0]) | (tallies[taker] == 0), 0, jnp.maximum(room, 0))
    passed = jax.random.randint(jax.random.fold_in(own, 4), (count // 2,), 0, 1 << 20) % (room + 1)
    tallies = tallies.at[source_of].add(-passed).at[taker].add(passed)
    items = jnp.searchsorted(jnp.cumsum(tallies), jnp.arange(rows * top), side="right").astype(jnp.int32)
    table = items.reshape(top, rows).T
    table = table[jax.random.permutation(jax.random.fold_in(own, 1), rows)]
    offset_by = jax.random.randint(jax.random.fold_in(own, 2), (rows, 1), 0, top)
    return jnp.take_along_axis(table, (jnp.arange(top)[None, :] + offset_by) % top, axis=1)


def load_shares(count, total, limit, skew, full):
    portions = [(1 << 20) // math.isqrt(grade ** skew) + 1 for grade in range(1, count + 1)]
    largest = limit if full else min(limit, max(-(-total // count), total * portions[0] // sum(portions)))
    least = 1 if total - largest >= count - 1 else 0
    given, spare = [largest] + [least] * (count - 1), total - largest - least * (count - 1)
    while spare > 0:
        free = [i for i in range(1, count) if given[i] < largest] or [i for i in range(1, count) if given[i] < limit]
        pool, remaining = sum([portions[i] for i in free]), spare
        for i in free:
            addition = min(limit - given[i], max(1, remaining * portions[i] // pool), spare)
            given[i] = given[i] + addition
            spare = spare - addition
    return np.array(given)


def gaussian(own_key, dims, width, bound, cuts=(), held_as=jnp.bfloat16):
    loudness = block_scale(own_key, dims, cuts, -0.22, 0.18) if cuts else 1.0
    array = jax.random.normal(own_key, dims, jnp.float32) * width * loudness
    return jnp.minimum(jnp.maximum(array, -bound), bound).astype(held_as)


def setup_inputs(seed: int = 0) -> dict:
    streams_of = jax.random.split(jax.random.key(seed), 9)
    tiles = gaussian(streams_of[0], (TILES, BS, BS), 1.0, 6.0, ((0, 128),), jnp.float32)
    dest_keys = jax.random.split(jax.random.fold_in(streams_of[1], 1), TILES // CB_DEV)
    dest_turns = jax.random.permutation(jax.random.fold_in(streams_of[1], 3), TILES // CB_DEV)
    dest = jax.vmap(lambda own, number: shared_out(jax.random.fold_in(streams_of[1], 2), own, number, CB_DEV, N_FRONT * N_ROW, 1, CAP, 2))(dest_keys, dest_turns).reshape((TILES, 1))
    block_row = place_ends(jax.random.randint(streams_of[2], (TILES,), 0, ORDER // (N_ROW * BS)), jax.random.fold_in(streams_of[2], 1), 0, (ORDER // (N_ROW * BS)) - 1).astype(jnp.int32)
    block_col = place_ends(jax.random.randint(streams_of[3], (TILES,), 0, ORDER // (N_COL * BS)), jax.random.fold_in(streams_of[3], 1), 0, (ORDER // (N_COL * BS)) - 1).astype(jnp.int32)
    rows_from = jax.vmap(lambda own: jax.random.permutation(own, BS))(jax.random.split(streams_of[4], TILES)).reshape((TILES, BS)).astype(jnp.int32)
    cols_from = jax.vmap(lambda own: jax.random.permutation(own, BS))(jax.random.split(streams_of[5], TILES)).reshape((TILES, BS)).astype(jnp.int32)
    initial = draw_initial(jax.random.fold_in(streams_of[8], 71), 0)
    pattern = place_ends((jax.random.randint(streams_of[7], (FRONTS, NPANEL, NBLK), 0, 3) < 2).astype(jnp.int32), jax.random.fold_in(streams_of[7], 1), 0, 1)
    return {"tiles": tiles, "dest": dest, "block_row": block_row, "block_col": block_col, "rows_from": rows_from, "cols_from": cols_from, "initial": initial, "pattern": pattern}


HIGH = lax.Precision.HIGHEST

def lower_sym(block):
    return jnp.tril(block) + jnp.tril(block, -1).T

def reference(tiles, dest, block_row, block_col, rows_from, cols_from, initial, pattern):
    row_span = ORDER // N_ROW
    col_span = ORDER // N_COL
    row_blocks = row_span // BS
    lead = PIV // BS
    moved = jnp.take_along_axis(tiles, rows_from[:, :, None], axis=1)
    moved = jnp.take_along_axis(moved, cols_from[:, None, :], axis=2)
    target = dest[:, 0]
    parent = (target // N_ROW).astype(jnp.int32)
    owner_row = target % N_ROW
    local_row = jnp.where(owner_row == 0, lead + block_row % (row_blocks - lead), block_row)
    sender_col = jnp.arange(TILES, dtype=jnp.int32) // CB_DEV % N_COL
    top = (owner_row * row_span + local_row * BS).astype(jnp.int32)
    left = (sender_col * col_span + block_col * BS).astype(jnp.int32)
    fronts = jnp.zeros((FRONTS, ORDER, ORDER), jnp.float32)

    def place(index, acc):
        start = (parent[index], top[index], left[index])
        current = lax.dynamic_slice(acc, start, (1, BS, BS))
        return lax.dynamic_update_slice(acc, current + moved[index][None], start)
    fronts = lax.fori_loop(0, TILES, place, fronts)
    glob = jnp.arange(ORDER, dtype=jnp.int32)
    results = []
    for front in range(FRONTS):
        whole = fronts[front].at[:, :PIV].add(initial[front])
        for panel in range(NPANEL):
            low = panel * BS
            factor = jnp.linalg.cholesky(lower_sym(whole[low:low + BS, low:low + BS]))
            solved = lax.linalg.triangular_solve(factor, whole[:, low:low + BS], left_side=False, lower=True, transpose_a=True)
            flags = jnp.repeat(pattern[front, panel], BS)
            keep = (glob >= low + BS) & (flags == 1)
            rows = jnp.where(keep[:, None], solved, jnp.zeros_like(solved))
            whole = whole - jnp.dot(rows, rows.T, precision=HIGH)
            column = rows.at[low:low + BS].set(factor)
            whole = whole.at[:, low:low + BS].set(column)
        upper = (glob[:, None] < PIV) & (glob[None, :] >= PIV)
        results.append(jnp.where(upper, jnp.zeros_like(whole), whole))
    return jnp.stack(results)
```

```python
import jax
import jax.numpy as jnp
from jax import lax
from jax.experimental import pallas as pl
from jax.experimental.pallas import tpu as pltpu
from jax.sharding import PartitionSpec as P

ORDER = 10240
BS = 256
CAP = 4
PIV = 512
STRIPS = (64, 64, 64, 64)
OFFSETS = tuple(sum(STRIPS[:q]) for q in range(len(STRIPS)))
NSTRIP = len(STRIPS)
RING = 8

HIGH = lax.Precision.HIGHEST
f32, bf16, i32 = jnp.float32, jnp.bfloat16, jnp.int32


def lower_sym(block):
    return jnp.tril(block) + jnp.tril(block, -1).T


def permute_kernel(slot_ref, tile_ref, rows_ref, cols_ref, *out_refs):
    tile = tile_ref[0]
    high = tile.astype(bf16)
    rest = tile - high.astype(f32)
    mid = rest.astype(bf16)
    low = (rest - mid.astype(f32)).astype(bf16)
    place = lax.broadcasted_iota(i32, (BS, BS), 0)
    pick_rows = jnp.where(place == rows_ref[0], 1.0, 0.0).astype(bf16)
    pick_cols = jnp.where(place == cols_ref[0], 1.0, 0.0).astype(bf16)
    parts = jnp.concatenate([high, mid, low], axis=1)
    moved = lax.dot_general(
        pick_rows, parts, (((0,), (0,)), ((), ())), preferred_element_type=f32
    ).astype(bf16)
    out = jnp.dot(moved[:, :BS], pick_cols, preferred_element_type=f32)
    out = out + jnp.dot(moved[:, BS : 2 * BS], pick_cols, preferred_element_type=f32)
    out = out + jnp.dot(moved[:, 2 * BS :], pick_cols, preferred_element_type=f32)
    for q, out_ref in enumerate(out_refs):
        out_ref[0] = out[OFFSETS[q] : OFFSETS[q] + STRIPS[q]]


def permute(slot, tiles, rows_from, cols_from, slots):
    count = tiles.shape[0]
    return pl.pallas_call(
        permute_kernel,
        grid_spec=pltpu.PrefetchScalarGridSpec(
            num_scalar_prefetch=1,
            grid=(count,),
            in_specs=[
                pl.BlockSpec((1, BS, BS), lambda t, slot: (t, 0, 0)),
                pl.BlockSpec((1, 1, BS), lambda t, slot: (t, 0, 0)),
                pl.BlockSpec((1, 1, BS), lambda t, slot: (t, 0, 0)),
            ],
            out_specs=[
                pl.BlockSpec((1, h, BS), lambda t, slot: (slot[t], 0, 0)) for h in STRIPS
            ],
        ),
        out_shape=[jax.ShapeDtypeStruct((slots, h, BS), f32) for h in STRIPS],
        compiler_params=pltpu.CompilerParams(vmem_limit_bytes=32 << 20),
        cost_estimate=pl.CostEstimate(
            flops=12 * count * BS**3, bytes_accessed=8 * count * BS * BS, transcendentals=0
        ),
        name="permute_tiles",
    )(slot, tiles, rows_from[:, None, :], cols_from[:, None, :])


def slab_kernel(height, meta, initial_ref, in_ref, out_ref, ring, sems):
    total = meta[128]

    def copy(g):
        return pltpu.make_async_copy(in_ref.at[meta[g]], ring.at[g % RING], sems.at[g % RING])

    for g in range(RING):

        @pl.when(g < total)
        def _():
            copy(g).start()

    out_ref[...] = initial_ref[...]

    @pl.loop(0, total)
    def _(g):
        copy(g).wait()
        spot = meta[64 + g]
        cols = pl.ds(pl.multiple_of((spot % 2) * BS, BS), BS)
        out_ref[spot // 2, :, cols] += ring[g % RING]

        @pl.when(g + RING < total)
        def _():
            copy(g + RING).start()


def slab_strip(meta, initial, incoming, height):
    blocks = initial.shape[0]
    return pl.pallas_call(
        lambda *refs: slab_kernel(height, *refs),
        grid_spec=pltpu.PrefetchScalarGridSpec(
            num_scalar_prefetch=1,
            grid=(1,),
            in_specs=[
                pl.BlockSpec((blocks, height, PIV), lambda i, meta: (0, 0, 0)),
                pl.BlockSpec(memory_space=pl.ANY),
            ],
            out_specs=pl.BlockSpec((blocks, height, PIV), lambda i, meta: (0, 0, 0)),
            scratch_shapes=[
                pltpu.VMEM((RING, height, BS), f32),
                pltpu.SemaphoreType.DMA((RING,)),
            ],
        ),
        out_shape=jax.ShapeDtypeStruct((blocks, height, PIV), f32),
        compiler_params=pltpu.CompilerParams(vmem_limit_bytes=32 << 20),
        cost_estimate=pl.CostEstimate(
            flops=0, bytes_accessed=12 * blocks * height * PIV, transcendentals=0
        ),
        name="slab_strip",
    )(meta, initial, incoming)


def halves(x):
    high = x.astype(bf16)
    return high, (x - high.astype(f32)).astype(bf16)


def nt(a, b):
    return lax.dot_general(a, b, (((1,), (1,)), ((), ())), preferred_element_type=f32)


def final_kernel(col_blocks, *refs):
    meta = refs[0]
    slab = refs[1 : 1 + NSTRIP]
    across = refs[1 + NSTRIP : 1 + 2 * NSTRIP]
    first_inv, second_inv, cross, first_factor, second_factor = refs[1 + 2 * NSTRIP : 6 + 2 * NSTRIP]
    incoming = refs[6 + 2 * NSTRIP : 6 + 3 * NSTRIP]
    out_ref, a_high, a_low, ring, sems = refs[6 + 3 * NSTRIP :]
    b = pl.program_id(0)
    total = meta[138]

    def copies(g):
        return [
            pltpu.make_async_copy(
                incoming[q].at[meta[g]],
                ring.at[g % RING, pl.ds(OFFSETS[q], STRIPS[q])],
                sems.at[g % RING, q],
            )
            for q in range(NSTRIP)
        ]

    def solve(block, keep_first, keep_second):
        one = jnp.dot(block[:, :BS], first_inv[...], precision=HIGH, preferred_element_type=f32)
        one = jnp.where(keep_first == 1, one, 0.0)
        two = jnp.dot(block[:, BS:], second_inv[...], precision=HIGH, preferred_element_type=f32)
        two = two - jnp.dot(one, cross[...], precision=HIGH, preferred_element_type=f32)
        return one, jnp.where(keep_second == 1, two, 0.0)

    @pl.when(b == 0)
    def _():
        for g in range(RING):

            @pl.when(g < total)
            def _():
                for c in copies(g):
                    c.start()

        for cb in range(col_blocks):
            block = jnp.concatenate([ref[cb] for ref in across], axis=0)
            one, two = solve(block, meta[159 + cb], meta[164 + cb])
            high, low = halves(jnp.concatenate([one, two], axis=1))
            a_high[cb * BS : (cb + 1) * BS] = high
            a_low[cb * BS : (cb + 1) * BS] = low

    one, two = solve(
        jnp.concatenate([ref[0] for ref in slab], axis=0), meta[139 + b], meta[149 + b]
    )
    top = meta[169] == 1
    high, low = halves(
        jnp.where(jnp.logical_and(top, b < 2), 0.0, jnp.concatenate([one, two], axis=1))
    )
    for cb in range(col_blocks):
        rows = slice(cb * BS, (cb + 1) * BS)
        product = nt(high, a_high[rows]) + (nt(high, a_low[rows]) + nt(low, a_high[rows]))
        out_ref[:, rows] = -product

    @pl.loop(meta[128 + b], meta[129 + b])
    def _(g):
        for c in copies(g):
            c.wait()
        cols = pl.ds(pl.multiple_of(meta[64 + g] * BS, BS), BS)
        out_ref[:, cols] += ring[g % RING]

        @pl.when(g + RING < total)
        def _():
            for c in copies(g + RING):
                c.start()

    @pl.when(meta[170] == 1)
    def _():
        out_ref[:, :BS] = jnp.where(jnp.logical_and(top, b == 0), first_factor[...], one)
        out_ref[:, BS:PIV] = jnp.where(jnp.logical_and(top, b == 1), second_factor[...], two)


def final(meta, slab, across, mats, incoming, row_blocks, col_blocks):
    whole = pl.BlockSpec((BS, BS), lambda b, meta: (0, 0))
    return pl.pallas_call(
        lambda *refs: final_kernel(col_blocks, *refs),
        grid_spec=pltpu.PrefetchScalarGridSpec(
            num_scalar_prefetch=1,
            grid=(row_blocks,),
            in_specs=[pl.BlockSpec((1, h, PIV), lambda b, meta: (b, 0, 0)) for h in STRIPS]
            + [pl.BlockSpec((col_blocks, h, PIV), lambda b, meta: (0, 0, 0)) for h in STRIPS]
            + [whole] * 5
            + [pl.BlockSpec(memory_space=pl.ANY)] * NSTRIP,
            out_specs=pl.BlockSpec((BS, col_blocks * BS), lambda b, meta: (b, 0)),
            scratch_shapes=[
                pltpu.VMEM((col_blocks * BS, PIV), bf16),
                pltpu.VMEM((col_blocks * BS, PIV), bf16),
                pltpu.VMEM((RING, BS, BS), f32),
                pltpu.SemaphoreType.DMA((RING, NSTRIP)),
            ],
        ),
        out_shape=jax.ShapeDtypeStruct((row_blocks * BS, col_blocks * BS), f32),
        compiler_params=pltpu.CompilerParams(vmem_limit_bytes=48 << 20),
        cost_estimate=pl.CostEstimate(
            flops=6 * row_blocks * col_blocks * BS * BS * PIV,
            bytes_accessed=4 * 2 * row_blocks * col_blocks * BS * BS,
            transcendentals=0,
        ),
        name="place_and_update",
    )(meta, *slab, *across, *mats, *incoming)


def factors(corner, keep):
    first = jnp.linalg.cholesky(lower_sym(corner[:BS, :BS]))
    eye = jnp.eye(BS, dtype=f32)
    first_inv = lax.linalg.triangular_solve(first, eye, left_side=True, lower=True)
    below = jnp.dot(corner[BS:, :BS], first_inv.T, precision=HIGH)
    below = jnp.where(keep, below, jnp.zeros_like(below))
    rest = corner[BS:, BS:] - jnp.dot(below, below.T, precision=HIGH)
    second = jnp.linalg.cholesky(lower_sym(rest))
    second_inv = lax.linalg.triangular_solve(second, eye, left_side=True, lower=True)
    cross = jnp.dot(below.T, second_inv.T, precision=HIGH)
    return first_inv.T, second_inv.T, cross, first, second


def spread_col(x, my_col):
    arrived = [lax.ppermute(x, "col", [(0, to)]) for to in (2, 6, 4)]
    even = jnp.where(my_col == 0, x, arrived[0] + arrived[1] + arrived[2])
    odd = lax.ppermute(even, "col", [(c, c + 1) for c in (0, 2, 4, 6)])
    return jnp.where(my_col % 2 == 0, even, odd)


def spread_row(x, my_row, my_col, n_row, n_col):
    half = x.shape[0] // 2
    own = lax.dynamic_slice_in_dim(x, (my_col % 2) * half, half, 0)
    out = own
    for step in range(1, n_row):
        pairs = [
            ((c // 2) * n_col + c, ((c // 2 + step) % n_row) * n_col + c) for c in range(n_col)
        ]
        got = lax.ppermute(own, ("row", "col"), pairs)
        out = jnp.where((my_row - my_col // 2) % n_row == step, got, out)
    return out


def ordered(key, valid, span):
    count = key.shape[0]
    key = jnp.where(valid, key, span)
    index = jnp.arange(count, dtype=i32)
    ahead = (key[None, :] < key[:, None]) | (
        (key[None, :] == key[:, None]) & (index[None, :] < index[:, None])
    )
    rank = jnp.sum(ahead.astype(i32), axis=1)
    chosen = rank[None, :] == index[:, None]
    order = jnp.sum(jnp.where(chosen, index[None, :], 0), axis=1)
    return order, jnp.sum(jnp.where(chosen, key[None, :], 0), axis=1), key


def body(tiles, dest, block_row, block_col, rows_from, cols_from, initial, pattern):
    n_front = lax.axis_size("front")
    n_row = lax.axis_size("row")
    n_col = lax.axis_size("col")
    my_row = lax.axis_index("row")
    my_col = lax.axis_index("col")
    row_blocks = ORDER // n_row // BS
    col_blocks = ORDER // n_col // BS
    lead = PIV // BS
    slots = n_front * n_row * CAP
    target = dest[:, 0]
    owner_row = target % n_row
    local_row = jnp.where(owner_row == 0, lead + block_row % (row_blocks - lead), block_row)
    block_id = local_row * col_blocks + block_col
    same = (target[:, None] == target[None, :]).astype(i32)
    slot = target * CAP + jnp.sum(jnp.tril(same, -1), axis=1)
    choose = jnp.arange(slots, dtype=i32)[:, None] == slot[None, :]
    labels = jnp.where(
        jnp.any(choose, axis=1), jnp.sum(jnp.where(choose, block_id[None, :], 0), axis=1), -1
    )
    names = lax.all_to_all(labels, ("front", "row"), split_axis=0, concat_axis=0, tiled=True)
    outgoing = permute(slot, tiles, rows_from, cols_from, slots)
    incoming = [
        lax.all_to_all(part, ("front", "row"), split_axis=0, concat_axis=0, tiled=True)
        for part in outgoing
    ]
    valid = names >= 0
    order, sorted_id, key = ordered(names, valid, row_blocks * col_blocks)
    bounds = jnp.arange(row_blocks + 1, dtype=i32)[:, None] * col_blocks
    starts = jnp.sum((key[None, :] < bounds).astype(i32), axis=1)
    in_slab = valid & (names % col_blocks < lead) & (my_col == 0)
    slab_key = (names // col_blocks) * lead + names % col_blocks
    slab_order, slab_id, _ = ordered(slab_key, in_slab, row_blocks * lead)
    slab_meta = jnp.concatenate([slab_order, slab_id, jnp.sum(in_slab.astype(i32))[None]])

    def kept(first_block, count):
        blocks = first_block + jnp.arange(count, dtype=i32)
        flags = lax.dynamic_slice_in_dim(pattern[0], first_block, count, axis=1)
        ahead = blocks[None, :] > jnp.arange(2, dtype=i32)[:, None]
        return jnp.where(ahead, flags, 0).reshape(-1)

    meta = jnp.concatenate(
        [
            order,
            sorted_id % col_blocks,
            starts,
            kept(my_row * row_blocks, row_blocks),
            kept(my_col * col_blocks, col_blocks),
            (my_row == 0).astype(i32)[None],
            (my_col == 0).astype(i32)[None],
        ]
    )

    pivot = jnp.where(my_row == 0, initial[0, :PIV], 0.0)
    corner = lax.all_gather(lax.psum(pivot, "row"), "col", axis=1, tiled=True)
    mats = factors(corner, pattern[0, 0, 1] == 1)
    columns = lax.all_gather(initial[0], "col", axis=1, tiled=True)
    columns = columns.reshape(row_blocks, BS, PIV)

    slab, across = [], []
    for q in range(NSTRIP):
        rows = slice(OFFSETS[q], OFFSETS[q] + STRIPS[q])
        strip = slab_strip(slab_meta, columns[:, rows], incoming[q], STRIPS[q])
        strip = spread_col(strip, my_col)
        slab.append(strip)
        across.append(spread_row(strip, my_row, my_col, n_row, n_col))
    return final(meta, slab, across, mats, incoming, row_blocks, col_blocks)[None]


def solution(mesh):
    placed = (
        P(("front", "row", "col"), None, None),
        P(("front", "row", "col"), None),
        P(("front", "row", "col")),
        P(("front", "row", "col")),
        P(("front", "row", "col"), None),
        P(("front", "row", "col"), None),
        P("front", "row", "col"),
        P("front", None, None),
    )
    return jax.shard_map(
        body, mesh=mesh, in_specs=placed, out_specs=P("front", "row", "col"), check_vma=False
    )
```

```python
import jax
import jax.numpy as jnp
from jax import lax
from jax.experimental import pallas as pl
from jax.experimental.pallas import tpu as pltpu
from jax.sharding import PartitionSpec as P

ORDER = 10240
BS = 256
CAP = 4
PIV = 512
STRIPS = (64, 64, 64, 32, 32)
OFFSETS = tuple(sum(STRIPS[:q]) for q in range(len(STRIPS)))
NSTRIP = len(STRIPS)
RING = 8

HIGH = lax.Precision.HIGHEST
f32, bf16, i32 = jnp.float32, jnp.bfloat16, jnp.int32


def lower_sym(block):
    return jnp.tril(block) + jnp.tril(block, -1).T


def permute_kernel(first, heights, slot_ref, tile_ref, rows_ref, cols_ref, *out_refs):
    tile = tile_ref[0]
    high = tile.astype(bf16)
    rest = tile - high.astype(f32)
    mid = rest.astype(bf16)
    low = (rest - mid.astype(f32)).astype(bf16)
    parts = jnp.concatenate([high, mid, low], axis=1)
    count = sum(heights)
    half = BS // 2
    wanted = jnp.transpose(jnp.broadcast_to(rows_ref[0], (half, BS)))[first : first + count]
    lane = lax.broadcasted_iota(i32, (count, half), 1)
    pick_rows = jnp.concatenate(
        [jnp.where(wanted == lane + k * half, 1.0, 0.0) for k in range(2)], axis=1
    ).astype(bf16)
    place = lax.broadcasted_iota(i32, (BS, BS), 0)
    pick_cols = jnp.where(place == cols_ref[0], 1.0, 0.0).astype(bf16)
    moved = jnp.dot(pick_rows, parts, preferred_element_type=f32).astype(bf16)
    out = jnp.dot(moved[:, :BS], pick_cols, preferred_element_type=f32)
    out = out + jnp.dot(moved[:, BS : 2 * BS], pick_cols, preferred_element_type=f32)
    out = out + jnp.dot(moved[:, 2 * BS :], pick_cols, preferred_element_type=f32)
    at = 0
    for out_ref, h in zip(out_refs, heights, strict=True):
        out_ref[0] = out[at : at + h]
        at += h


def permute(slot, tiles, rows_from, cols_from, slots, first, heights):
    count = tiles.shape[0]
    return pl.pallas_call(
        lambda *refs: permute_kernel(first, heights, *refs),
        grid_spec=pltpu.PrefetchScalarGridSpec(
            num_scalar_prefetch=1,
            grid=(count,),
            in_specs=[
                pl.BlockSpec((1, BS, BS), lambda t, slot: (t, 0, 0)),
                pl.BlockSpec((1, 1, BS), lambda t, slot: (t, 0, 0)),
                pl.BlockSpec((1, 1, BS), lambda t, slot: (t, 0, 0)),
            ],
            out_specs=[
                pl.BlockSpec((1, h, BS), lambda t, slot: (slot[t], 0, 0)) for h in heights
            ],
        ),
        out_shape=[jax.ShapeDtypeStruct((slots, h, BS), f32) for h in heights],
        compiler_params=pltpu.CompilerParams(vmem_limit_bytes=58 << 20),
        cost_estimate=pl.CostEstimate(
            flops=12 * count * BS * BS * sum(heights),
            bytes_accessed=4 * count * BS * (BS + sum(heights)),
            transcendentals=0,
        ),
        name="permute_tiles",
    )(slot, tiles, rows_from[:, None, :], cols_from[:, None, :])


def slab_kernel(first, height, meta, initial_ref, in_ref, out_ref, ring, sems, initial_sem):
    total = meta[128]

    def copy(g):
        return pltpu.make_async_copy(in_ref.at[meta[g]], ring.at[g % RING], sems.at[g % RING])

    begin = pltpu.make_async_copy(initial_ref.at[:, pl.ds(first, height)], out_ref, initial_sem)
    begin.start()
    for g in range(RING):

        @pl.when(g < total)
        def _():
            copy(g).start()

    begin.wait()

    @pl.loop(0, total)
    def _(g):
        copy(g).wait()
        spot = meta[64 + g]
        cols = pl.ds(pl.multiple_of((spot % 2) * BS, BS), BS)
        out_ref[spot // 2, :, cols] += ring[g % RING]

        @pl.when(g + RING < total)
        def _():
            copy(g + RING).start()


def slab_strip(meta, initial, incoming, first, height):
    blocks = initial.shape[0]
    return pl.pallas_call(
        lambda *refs: slab_kernel(first, height, *refs),
        grid_spec=pltpu.PrefetchScalarGridSpec(
            num_scalar_prefetch=1,
            grid=(1,),
            in_specs=[pl.BlockSpec(memory_space=pl.ANY)] * 2,
            out_specs=pl.BlockSpec((blocks, height, PIV), lambda i, meta: (0, 0, 0)),
            scratch_shapes=[
                pltpu.VMEM((RING, height, BS), f32),
                pltpu.SemaphoreType.DMA((RING,)),
                pltpu.SemaphoreType.DMA(()),
            ],
        ),
        out_shape=jax.ShapeDtypeStruct((blocks, height, PIV), f32),
        compiler_params=pltpu.CompilerParams(vmem_limit_bytes=32 << 20),
        cost_estimate=pl.CostEstimate(
            flops=0, bytes_accessed=12 * blocks * height * PIV, transcendentals=0
        ),
        name="slab_strip",
    )(meta, initial, incoming)


def halves(x):
    high = x.astype(bf16)
    return high, (x - high.astype(f32)).astype(bf16)


def nt(a, b):
    return lax.dot_general(a, b, (((1,), (1,)), ((), ())), preferred_element_type=f32)


def final_kernel(col_blocks, *refs):
    meta = refs[0]
    slab = refs[1 : 1 + NSTRIP]
    across = refs[1 + NSTRIP : 1 + 2 * NSTRIP]
    first_inv, second_inv, cross, first_factor, second_factor = refs[1 + 2 * NSTRIP : 6 + 2 * NSTRIP]
    incoming = refs[6 + 2 * NSTRIP : 6 + 3 * NSTRIP]
    out_ref, a_high, a_low, ring, sems = refs[6 + 3 * NSTRIP :]
    b = pl.program_id(0)
    total = meta[138]

    def copies(g):
        return [
            pltpu.make_async_copy(
                incoming[q].at[meta[g]],
                ring.at[g % RING, pl.ds(OFFSETS[q], STRIPS[q])],
                sems.at[g % RING, q],
            )
            for q in range(NSTRIP)
        ]

    def solve(block, keep_first, keep_second):
        one = jnp.dot(block[:, :BS], first_inv[...], precision=HIGH, preferred_element_type=f32)
        one = jnp.where(keep_first == 1, one, 0.0)
        two = jnp.dot(block[:, BS:], second_inv[...], precision=HIGH, preferred_element_type=f32)
        two = two - jnp.dot(one, cross[...], precision=HIGH, preferred_element_type=f32)
        return one, jnp.where(keep_second == 1, two, 0.0)

    @pl.when(b == 0)
    def _():
        for g in range(RING):

            @pl.when(g < total)
            def _():
                for c in copies(g):
                    c.start()

        for cb in range(col_blocks):
            block = jnp.concatenate([ref[cb] for ref in across], axis=0)
            one, two = solve(block, meta[159 + cb], meta[164 + cb])
            high, low = halves(jnp.concatenate([one, two], axis=1))
            a_high[cb * BS : (cb + 1) * BS] = high
            a_low[cb * BS : (cb + 1) * BS] = low

    one, two = solve(
        jnp.concatenate([ref[0] for ref in slab], axis=0), meta[139 + b], meta[149 + b]
    )
    top = meta[169] == 1
    high, low = halves(
        jnp.where(jnp.logical_and(top, b < 2), 0.0, jnp.concatenate([one, two], axis=1))
    )
    for cb in range(col_blocks):
        rows = slice(cb * BS, (cb + 1) * BS)
        product = nt(high, a_high[rows]) + (nt(high, a_low[rows]) + nt(low, a_high[rows]))
        out_ref[:, rows] = -product

    @pl.loop(meta[128 + b], meta[129 + b])
    def _(g):
        for c in copies(g):
            c.wait()
        cols = pl.ds(pl.multiple_of(meta[64 + g] * BS, BS), BS)
        out_ref[:, cols] += ring[g % RING]

        @pl.when(g + RING < total)
        def _():
            for c in copies(g + RING):
                c.start()

    @pl.when(meta[170] == 1)
    def _():
        out_ref[:, :BS] = jnp.where(jnp.logical_and(top, b == 0), first_factor[...], one)
        out_ref[:, BS:PIV] = jnp.where(jnp.logical_and(top, b == 1), second_factor[...], two)


def final(meta, slab, across, mats, incoming, row_blocks, col_blocks):
    whole = pl.BlockSpec((BS, BS), lambda b, meta: (0, 0))
    return pl.pallas_call(
        lambda *refs: final_kernel(col_blocks, *refs),
        grid_spec=pltpu.PrefetchScalarGridSpec(
            num_scalar_prefetch=1,
            grid=(row_blocks,),
            in_specs=[pl.BlockSpec((1, h, PIV), lambda b, meta: (b, 0, 0)) for h in STRIPS]
            + [pl.BlockSpec((col_blocks, h, PIV), lambda b, meta: (0, 0, 0)) for h in STRIPS]
            + [whole] * 5
            + [pl.BlockSpec(memory_space=pl.ANY)] * NSTRIP,
            out_specs=pl.BlockSpec((BS, col_blocks * BS), lambda b, meta: (b, 0)),
            scratch_shapes=[
                pltpu.VMEM((col_blocks * BS, PIV), bf16),
                pltpu.VMEM((col_blocks * BS, PIV), bf16),
                pltpu.VMEM((RING, BS, BS), f32),
                pltpu.SemaphoreType.DMA((RING, NSTRIP)),
            ],
        ),
        out_shape=jax.ShapeDtypeStruct((row_blocks * BS, col_blocks * BS), f32),
        compiler_params=pltpu.CompilerParams(vmem_limit_bytes=48 << 20),
        cost_estimate=pl.CostEstimate(
            flops=6 * row_blocks * col_blocks * BS * BS * PIV,
            bytes_accessed=4 * 2 * row_blocks * col_blocks * BS * BS,
            transcendentals=0,
        ),
        name="place_and_update",
    )(meta, *slab, *across, *mats, *incoming)


def dot(a, b):
    return jnp.dot(a, b, precision=HIGH)


def inverse(lower):
    size = lower.shape[0]
    eye = jnp.eye(size, dtype=f32)
    scale = jnp.sum(lower * eye, axis=0)
    power = eye - lower / scale[None, :]
    out = eye + power
    for _ in range(6):
        power = dot(power, power)
        out = out + dot(power, out)
    return out / scale[:, None]


def panel(block):
    half = BS // 2
    first = jnp.linalg.cholesky(lower_sym(block[:half, :half]))
    first_inv = inverse(first)
    below = dot(block[half:, :half], first_inv.T)
    second = jnp.linalg.cholesky(lower_sym(block[half:, half:] - dot(below, below.T)))
    second_inv = inverse(second)
    across = -dot(second_inv, dot(below, first_inv))
    zero = jnp.zeros((half, half), f32)
    factor = jnp.block([[first, zero], [below, second]])
    return factor, jnp.block([[first_inv.T, across.T], [zero, second_inv.T]])


def spread_col(x, my_col):
    arrived = [lax.ppermute(x, "col", [(0, to)]) for to in (2, 6, 4)]
    even = jnp.where(my_col == 0, x, arrived[0] + arrived[1] + arrived[2])
    odd = lax.ppermute(even, "col", [(c, c + 1) for c in (0, 2, 4, 6)])
    return jnp.where(my_col % 2 == 0, even, odd)


def spread_row(x, my_row, my_col, n_row, n_col):
    half = x.shape[0] // 2
    own = lax.dynamic_slice_in_dim(x, (my_col % 2) * half, half, 0)

    def pairs(start, stop):
        return [
            ((c // 2 + start[c % 2]) % n_row * n_col + c, (c // 2 + stop) % n_row * n_col + c)
            for c in range(n_col)
        ]

    step = (my_row - my_col // 2) % n_row
    after = lax.ppermute(own, ("row", "col"), pairs((0, 0), 1))
    before = lax.ppermute(own, ("row", "col"), pairs((0, 0), -1))
    near = jnp.where(step == 0, own, jnp.where(step == 1, after, before))
    far = lax.ppermute(near, ("row", "col"), pairs((1, -1), 2))
    return jnp.where(step == 2, far, near)


def ordered(key, valid, span):
    count = key.shape[0]
    key = jnp.where(valid, key, span)
    index = jnp.arange(count, dtype=i32)
    ahead = (key[None, :] < key[:, None]) | (
        (key[None, :] == key[:, None]) & (index[None, :] < index[:, None])
    )
    rank = jnp.sum(ahead.astype(i32), axis=1)
    chosen = rank[None, :] == index[:, None]
    order = jnp.sum(jnp.where(chosen, index[None, :], 0), axis=1)
    return order, jnp.sum(jnp.where(chosen, key[None, :], 0), axis=1), key


def body(tiles, dest, block_row, block_col, rows_from, cols_from, initial, pattern):
    n_front = lax.axis_size("front")
    n_row = lax.axis_size("row")
    n_col = lax.axis_size("col")
    my_row = lax.axis_index("row")
    my_col = lax.axis_index("col")
    row_blocks = ORDER // n_row // BS
    col_blocks = ORDER // n_col // BS
    lead = PIV // BS
    slots = n_front * n_row * CAP
    target = dest[:, 0]
    owner_row = target % n_row
    local_row = jnp.where(owner_row == 0, lead + block_row % (row_blocks - lead), block_row)
    block_id = local_row * col_blocks + block_col
    same = (target[:, None] == target[None, :]).astype(i32)
    slot = target * CAP + jnp.sum(jnp.tril(same, -1), axis=1)
    choose = jnp.arange(slots, dtype=i32)[:, None] == slot[None, :]
    labels = jnp.where(
        jnp.any(choose, axis=1), jnp.sum(jnp.where(choose, block_id[None, :], 0), axis=1), -1
    )
    names = lax.all_to_all(labels, ("front", "row"), split_axis=0, concat_axis=0, tiled=True)
    valid = names >= 0
    order, sorted_id, key = ordered(names, valid, row_blocks * col_blocks)
    bounds = jnp.arange(row_blocks + 1, dtype=i32)[:, None] * col_blocks
    starts = jnp.sum((key[None, :] < bounds).astype(i32), axis=1)
    in_slab = valid & (names % col_blocks < lead) & (my_col == 0)
    slab_key = (names // col_blocks) * lead + names % col_blocks
    slab_order, slab_id, _ = ordered(slab_key, in_slab, row_blocks * lead)
    slab_meta = jnp.concatenate([slab_order, slab_id, jnp.sum(in_slab.astype(i32))[None]])

    def kept(first_block, count):
        blocks = first_block + jnp.arange(count, dtype=i32)
        flags = lax.dynamic_slice_in_dim(pattern[0], first_block, count, axis=1)
        ahead = blocks[None, :] > jnp.arange(2, dtype=i32)[:, None]
        return jnp.where(ahead, flags, 0).reshape(-1)

    meta = jnp.concatenate(
        [
            order,
            sorted_id % col_blocks,
            starts,
            kept(my_row * row_blocks, row_blocks),
            kept(my_col * col_blocks, col_blocks),
            (my_row == 0).astype(i32)[None],
            (my_col == 0).astype(i32)[None],
        ]
    )

    corner = lax.all_gather(initial[0, :PIV], ("row", "col"), axis=0)[:n_col]
    corner = corner.transpose(1, 0, 2).reshape(PIV, PIV)
    columns = lax.all_gather(initial[0], "col", axis=1, tiled=True)
    columns = columns.reshape(row_blocks, BS, PIV)

    def send(part):
        return lax.all_to_all(part, ("front", "row"), split_axis=0, concat_axis=0, tiled=True)

    outgoing = permute(slot, tiles, rows_from, cols_from, slots, 0, STRIPS[:1])
    outgoing += permute(slot, tiles, rows_from, cols_from, slots, STRIPS[0], STRIPS[1:])
    incoming, slab, across = [], [], []

    def collect(q):
        strip = slab_strip(slab_meta, columns, incoming[q], OFFSETS[q], STRIPS[q])
        slab.append(spread_col(strip, my_col))
        across.append(spread_row(slab[q], my_row, my_col, n_row, n_col))

    incoming.append(send(outgoing[0]))
    incoming.append(send(outgoing[1]))
    collect(0)
    first, first_inv = panel(corner[:BS, :BS])
    below = dot(corner[BS:, :BS], first_inv)
    below = jnp.where(pattern[0, 0, 1] == 1, below, jnp.zeros_like(below))
    rest = corner[BS:, BS:] - dot(below, below.T)
    part, slab[0], rest = lax.optimization_barrier((outgoing[2], slab[0], rest))
    incoming.append(send(part))
    collect(1)
    second, second_inv = panel(rest)
    cross = dot(below.T, second_inv)
    mats = (first_inv, second_inv, cross, first, second)
    part, slab[1], across[0], mats = lax.optimization_barrier((outgoing[3], slab[1], across[0], mats))
    incoming.append(send(part))
    collect(2)
    part, across[1] = lax.optimization_barrier((outgoing[4], across[1]))
    incoming.append(send(part))
    collect(3)
    collect(4)
    return final(meta, slab, across, mats, incoming, row_blocks, col_blocks)[None]


def solution(mesh):
    placed = (
        P(("front", "row", "col"), None, None),
        P(("front", "row", "col"), None),
        P(("front", "row", "col")),
        P(("front", "row", "col")),
        P(("front", "row", "col"), None),
        P(("front", "row", "col"), None),
        P("front", "row", "col"),
        P("front", None, None),
    )
    return jax.shard_map(
        body, mesh=mesh, in_specs=placed, out_specs=P("front", "row", "col"), check_vma=False
    )
```

```python
import jax
import jax.numpy as jnp
from jax import lax
from jax.experimental import pallas as pl
from jax.experimental.pallas import tpu as pltpu
from jax.sharding import PartitionSpec as P

ORDER = 10240
BS = 256
CAP = 4
PIV = 512
STRIP = 32
NSTRIP = BS // STRIP
PARTS = (2, 3, 3)
OFFSETS = tuple(sum(PARTS[:q]) for q in range(len(PARTS)))
NPART = len(PARTS)
GROUP = 8
RING = 8

HIGH = lax.Precision.HIGHEST
f32, bf16, i32 = jnp.float32, jnp.bfloat16, jnp.int32


def lower_sym(block):
    return jnp.tril(block) + jnp.tril(block, -1).T


def permute_kernel(slot_ref, tile_ref, rows_ref, cols_ref, *refs):
    strip_refs, part_refs = refs[:NSTRIP], refs[NSTRIP : NSTRIP + NPART]
    hold, strip_sems, part_sems = refs[NSTRIP + NPART :]
    step = pl.program_id(0)
    half = BS // 2
    lane = lax.broadcasted_iota(i32, (BS, half), 1)
    place = lax.broadcasted_iota(i32, (BS, BS), 0)

    def move(g, carry):
        t = step * GROUP + g
        tile = tile_ref[g]
        high = tile.astype(bf16)
        rest = tile - high.astype(f32)
        mid = rest.astype(bf16)
        low = (rest - mid.astype(f32)).astype(bf16)
        parts = jnp.concatenate([high, mid, low], axis=1)
        wanted = jnp.transpose(jnp.broadcast_to(rows_ref[g], (half, BS)))
        pick_rows = jnp.concatenate(
            [jnp.where(wanted == lane + k * half, 1.0, 0.0) for k in range(2)], axis=1
        ).astype(bf16)
        pick_cols = jnp.where(place == cols_ref[g], 1.0, 0.0).astype(bf16)
        moved = jnp.dot(pick_rows, parts, preferred_element_type=f32).astype(bf16)
        out = jnp.dot(moved[:, :BS], pick_cols, preferred_element_type=f32)
        out = out + jnp.dot(moved[:, BS : 2 * BS], pick_cols, preferred_element_type=f32)
        out = out + jnp.dot(moved[:, 2 * BS :], pick_cols, preferred_element_type=f32)
        hold[t] = out.reshape(NSTRIP, STRIP, BS)
        for k in range(NSTRIP):
            pltpu.make_async_copy(hold.at[t, k], strip_refs[k].at[t], strip_sems.at[t]).start()
        for q in range(NPART):
            pltpu.make_async_copy(
                hold.at[t, pl.ds(OFFSETS[q], PARTS[q])],
                part_refs[q].at[slot_ref[t]],
                part_sems.at[t],
            ).start()
        return carry

    lax.fori_loop(0, GROUP, move, 0, unroll=2)

    @pl.when(step == pl.num_programs(0) - 1)
    def _():
        def finish(t, carry):
            pltpu.make_async_copy(hold.at[t], hold.at[t], strip_sems.at[t]).wait()
            pltpu.make_async_copy(hold.at[t], hold.at[t], part_sems.at[t]).wait()
            return carry

        lax.fori_loop(0, hold.shape[0], finish, 0)


def permute(slot, tiles, rows_from, cols_from, slots):
    count = tiles.shape[0]
    out = pl.pallas_call(
        permute_kernel,
        grid_spec=pltpu.PrefetchScalarGridSpec(
            num_scalar_prefetch=1,
            grid=(count // GROUP,),
            in_specs=[
                pl.BlockSpec((GROUP, BS, BS), lambda t, slot: (t, 0, 0)),
                pl.BlockSpec((GROUP, 1, BS), lambda t, slot: (t, 0, 0)),
                pl.BlockSpec((GROUP, 1, BS), lambda t, slot: (t, 0, 0)),
            ],
            out_specs=[pl.BlockSpec(memory_space=pl.ANY)] * (NSTRIP + NPART),
            scratch_shapes=[
                pltpu.VMEM((count, NSTRIP, STRIP, BS), f32),
                pltpu.SemaphoreType.DMA((count,)),
                pltpu.SemaphoreType.DMA((count,)),
            ],
        ),
        out_shape=[jax.ShapeDtypeStruct((count, STRIP, BS), f32)] * NSTRIP
        + [jax.ShapeDtypeStruct((slots, n, STRIP, BS), f32) for n in PARTS],
        compiler_params=pltpu.CompilerParams(vmem_limit_bytes=58 << 20),
        cost_estimate=pl.CostEstimate(
            flops=12 * count * BS**3, bytes_accessed=12 * count * BS * BS, transcendentals=0
        ),
        name="permute_tiles",
    )(slot, tiles, rows_from[:, None, :], cols_from[:, None, :])
    return out[:NSTRIP], out[NSTRIP:]


def slot_kernel(count, meta, *refs):
    sources, (out_ref, sems) = refs[:NSTRIP], refs[NSTRIP:]
    for c in range(NSTRIP):

        @pl.when(meta[count] == c)
        def _():
            def begin(t, carry):
                pltpu.make_async_copy(sources[c].at[t], out_ref.at[meta[t]], sems.at[t]).start()
                return carry

            lax.fori_loop(0, count, begin, 0)

    def finish(t, carry):
        pltpu.make_async_copy(sources[0].at[t], out_ref.at[meta[t]], sems.at[t]).wait()
        return carry

    lax.fori_loop(0, count, finish, 0)


def slot_strips(meta, sources, slots):
    count = sources[0].shape[0]
    return pl.pallas_call(
        lambda *refs: slot_kernel(count, *refs),
        grid_spec=pltpu.PrefetchScalarGridSpec(
            num_scalar_prefetch=1,
            grid=(1,),
            in_specs=[pl.BlockSpec(memory_space=pl.ANY)] * NSTRIP,
            out_specs=pl.BlockSpec(memory_space=pl.ANY),
            scratch_shapes=[pltpu.SemaphoreType.DMA((count,))],
        ),
        out_shape=jax.ShapeDtypeStruct((slots, STRIP, BS), f32),
        compiler_params=pltpu.CompilerParams(vmem_limit_bytes=58 << 20),
        cost_estimate=pl.CostEstimate(
            flops=0, bytes_accessed=8 * count * STRIP * BS, transcendentals=0
        ),
        name="slot_strips",
    )(meta, *sources)


def slab_kernel(meta, initial_ref, in_ref, out_ref, ring, sems):
    total = meta[128]

    def copy(g):
        return pltpu.make_async_copy(in_ref.at[meta[g]], ring.at[g % RING], sems.at[g % RING])

    for g in range(RING):

        @pl.when(g < total)
        def _():
            copy(g).start()

    out_ref[...] = initial_ref[...]

    @pl.loop(0, total)
    def _(g):
        copy(g).wait()
        spot = meta[64 + g]
        cols = pl.ds(pl.multiple_of((spot % 2) * BS, BS), BS)
        out_ref[spot // 2, :, cols] += ring[g % RING]

        @pl.when(g + RING < total)
        def _():
            copy(g + RING).start()


def slab_strip(meta, initial, incoming):
    spec = pl.BlockSpec(initial.shape, lambda i, meta: (0, 0, 0))
    return pl.pallas_call(
        slab_kernel,
        grid_spec=pltpu.PrefetchScalarGridSpec(
            num_scalar_prefetch=1,
            grid=(1,),
            in_specs=[spec, pl.BlockSpec(memory_space=pl.ANY)],
            out_specs=spec,
            scratch_shapes=[
                pltpu.VMEM((RING, STRIP, BS), f32),
                pltpu.SemaphoreType.DMA((RING,)),
            ],
        ),
        out_shape=jax.ShapeDtypeStruct(initial.shape, f32),
        compiler_params=pltpu.CompilerParams(vmem_limit_bytes=32 << 20),
        cost_estimate=pl.CostEstimate(
            flops=0, bytes_accessed=12 * initial.size, transcendentals=0
        ),
        name="slab_strip",
    )(meta, initial, incoming)


def halves(x):
    high = x.astype(bf16)
    return high, (x - high.astype(f32)).astype(bf16)


def nt(a, b):
    return lax.dot_general(a, b, (((1,), (1,)), ((), ())), preferred_element_type=f32)


def final_kernel(col_blocks, *refs):
    meta = refs[0]
    slab, across, first_inv, second_inv, cross, first_factor, second_factor = refs[1:8]
    incoming = refs[8 : 8 + NPART]
    out_ref, a_high, a_low, ring, sems = refs[8 + NPART :]
    b = pl.program_id(0)
    total = meta[138]

    def copies(g):
        return [
            pltpu.make_async_copy(
                incoming[q].at[meta[g]],
                ring.at[g % RING, pl.ds(OFFSETS[q], PARTS[q])],
                sems.at[g % RING, q],
            )
            for q in range(NPART)
        ]

    def solve(block, keep_first, keep_second):
        one = jnp.dot(block[:, :BS], first_inv[...], precision=HIGH, preferred_element_type=f32)
        one = jnp.where(keep_first == 1, one, 0.0)
        two = jnp.dot(block[:, BS:], second_inv[...], precision=HIGH, preferred_element_type=f32)
        two = two - jnp.dot(one, cross[...], precision=HIGH, preferred_element_type=f32)
        return one, jnp.where(keep_second == 1, two, 0.0)

    @pl.when(b == 0)
    def _():
        for g in range(RING):

            @pl.when(g < total)
            def _():
                for c in copies(g):
                    c.start()

        for cb in range(col_blocks):
            block = across[:, cb].reshape(BS, PIV)
            one, two = solve(block, meta[159 + cb], meta[164 + cb])
            high, low = halves(jnp.concatenate([one, two], axis=1))
            a_high[cb * BS : (cb + 1) * BS] = high
            a_low[cb * BS : (cb + 1) * BS] = low

    one, two = solve(slab[:, 0].reshape(BS, PIV), meta[139 + b], meta[149 + b])
    top = meta[169] == 1
    high, low = halves(
        jnp.where(jnp.logical_and(top, b < 2), 0.0, jnp.concatenate([one, two], axis=1))
    )
    for cb in range(col_blocks):
        rows = slice(cb * BS, (cb + 1) * BS)
        product = nt(high, a_high[rows]) + (nt(high, a_low[rows]) + nt(low, a_high[rows]))
        out_ref[:, rows] = -product

    @pl.loop(meta[128 + b], meta[129 + b])
    def _(g):
        for c in copies(g):
            c.wait()
        cols = pl.ds(pl.multiple_of(meta[64 + g] * BS, BS), BS)
        out_ref[:, cols] += ring[g % RING].reshape(BS, BS)

        @pl.when(g + RING < total)
        def _():
            for c in copies(g + RING):
                c.start()

    @pl.when(meta[170] == 1)
    def _():
        out_ref[:, :BS] = jnp.where(jnp.logical_and(top, b == 0), first_factor[...], one)
        out_ref[:, BS:PIV] = jnp.where(jnp.logical_and(top, b == 1), second_factor[...], two)


def final(meta, slab, across, mats, incoming, row_blocks, col_blocks):
    whole = pl.BlockSpec((BS, BS), lambda b, meta: (0, 0))
    return pl.pallas_call(
        lambda *refs: final_kernel(col_blocks, *refs),
        grid_spec=pltpu.PrefetchScalarGridSpec(
            num_scalar_prefetch=1,
            grid=(row_blocks,),
            in_specs=[
                pl.BlockSpec((NSTRIP, 1, STRIP, PIV), lambda b, meta: (0, b, 0, 0)),
                pl.BlockSpec((NSTRIP, col_blocks, STRIP, PIV), lambda b, meta: (0, 0, 0, 0)),
            ]
            + [whole] * 5
            + [pl.BlockSpec(memory_space=pl.ANY)] * NPART,
            out_specs=pl.BlockSpec((BS, col_blocks * BS), lambda b, meta: (b, 0)),
            scratch_shapes=[
                pltpu.VMEM((col_blocks * BS, PIV), bf16),
                pltpu.VMEM((col_blocks * BS, PIV), bf16),
                pltpu.VMEM((RING, NSTRIP, STRIP, BS), f32),
                pltpu.SemaphoreType.DMA((RING, NPART)),
            ],
        ),
        out_shape=jax.ShapeDtypeStruct((row_blocks * BS, col_blocks * BS), f32),
        compiler_params=pltpu.CompilerParams(vmem_limit_bytes=48 << 20),
        cost_estimate=pl.CostEstimate(
            flops=6 * row_blocks * col_blocks * BS * BS * PIV,
            bytes_accessed=4 * 2 * row_blocks * col_blocks * BS * BS,
            transcendentals=0,
        ),
        name="place_and_update",
    )(meta, slab, across, *mats, *incoming)


def dot(a, b):
    return jnp.dot(a, b, precision=HIGH)


def inverse(lower):
    size = lower.shape[0]
    eye = jnp.eye(size, dtype=f32)
    scale = jnp.sum(lower * eye, axis=0)
    power = eye - lower / scale[None, :]
    out = eye + power
    for _ in range(6):
        power = dot(power, power)
        out = out + dot(power, out)
    return out / scale[:, None]


def panel(block):
    half = BS // 2
    first = jnp.linalg.cholesky(lower_sym(block[:half, :half]))
    first_inv = inverse(first)
    below = dot(block[half:, :half], first_inv.T)
    second = jnp.linalg.cholesky(lower_sym(block[half:, half:] - dot(below, below.T)))
    second_inv = inverse(second)
    across = -dot(second_inv, dot(below, first_inv))
    zero = jnp.zeros((half, half), f32)
    factor = jnp.block([[first, zero], [below, second]])
    return factor, jnp.block([[first_inv.T, across.T], [zero, second_inv.T]])


def ordered(key, valid, span):
    count = key.shape[0]
    key = jnp.where(valid, key, span)
    index = jnp.arange(count, dtype=i32)
    ahead = (key[None, :] < key[:, None]) | (
        (key[None, :] == key[:, None]) & (index[None, :] < index[:, None])
    )
    rank = jnp.sum(ahead.astype(i32), axis=1)
    chosen = rank[None, :] == index[:, None]
    order = jnp.sum(jnp.where(chosen, index[None, :], 0), axis=1)
    return order, jnp.sum(jnp.where(chosen, key[None, :], 0), axis=1), key


def body(tiles, dest, block_row, block_col, rows_from, cols_from, initial, pattern):
    n_front = lax.axis_size("front")
    n_row = lax.axis_size("row")
    n_col = lax.axis_size("col")
    my_row = lax.axis_index("row")
    my_col = lax.axis_index("col")
    row_blocks = ORDER // n_row // BS
    col_blocks = ORDER // n_col // BS
    lead = PIV // BS
    slots = n_front * n_row * CAP
    target = dest[:, 0]
    owner_row = target % n_row
    local_row = jnp.where(owner_row == 0, lead + block_row % (row_blocks - lead), block_row)
    block_id = local_row * col_blocks + block_col
    same = (target[:, None] == target[None, :]).astype(i32)
    slot = target * CAP + jnp.sum(jnp.tril(same, -1), axis=1)
    choose = jnp.arange(slots, dtype=i32)[:, None] == slot[None, :]
    labels = jnp.where(
        jnp.any(choose, axis=1), jnp.sum(jnp.where(choose, block_id[None, :], 0), axis=1), -1
    )
    names = lax.all_to_all(labels, ("front", "row"), split_axis=0, concat_axis=0, tiled=True)

    row = jnp.zeros((1, initial.shape[2]), f32)
    slot_row = row.at[0, : slot.shape[0]].set(slot.astype(f32))
    near = lax.all_gather(
        jnp.concatenate([initial[0, :PIV], jnp.broadcast_to(slot_row, (8, row.shape[1]))]),
        ("row", "col"),
        axis=0,
    )
    corner = near[:n_col, :PIV].transpose(1, 0, 2).reshape(PIV, PIV)
    first_slot = lax.dynamic_index_in_dim(near[:, PIV], my_row * n_col, 0, keepdims=False)
    slot_meta = jnp.append(first_slot[: slot.shape[0]].astype(i32), my_col)
    names_row = row.at[0, :slots].set(names.astype(f32))
    wide = lax.all_gather(
        jnp.concatenate([initial[0], jnp.broadcast_to(names_row, (8, row.shape[1]))]), "col", axis=0
    )
    first_names = wide[0, row_blocks * BS, :slots].astype(i32)
    columns = wide[:, : row_blocks * BS].reshape(n_col, row_blocks, NSTRIP, STRIP, -1)
    columns = lax.dynamic_index_in_dim(columns, my_col, 2, keepdims=False)
    columns = columns.transpose(1, 2, 0, 3).reshape(row_blocks, STRIP, PIV)

    valid = names >= 0
    order, sorted_id, key = ordered(names, valid, row_blocks * col_blocks)
    bounds = jnp.arange(row_blocks + 1, dtype=i32)[:, None] * col_blocks
    starts = jnp.sum((key[None, :] < bounds).astype(i32), axis=1)
    in_slab = (first_names >= 0) & (first_names % col_blocks < lead)
    slab_key = (first_names // col_blocks) * lead + first_names % col_blocks
    slab_order, slab_id, _ = ordered(slab_key, in_slab, row_blocks * lead)
    slab_meta = jnp.concatenate([slab_order, slab_id, jnp.sum(in_slab.astype(i32))[None]])

    def kept(first_block, count):
        blocks = first_block + jnp.arange(count, dtype=i32)
        flags = lax.dynamic_slice_in_dim(pattern[0], first_block, count, axis=1)
        ahead = blocks[None, :] > jnp.arange(2, dtype=i32)[:, None]
        return jnp.where(ahead, flags, 0).reshape(-1)

    meta = jnp.concatenate(
        [
            order,
            sorted_id % col_blocks,
            starts,
            kept(my_row * row_blocks, row_blocks),
            kept(my_col * col_blocks, col_blocks),
            (my_row == 0).astype(i32)[None],
            (my_col == 0).astype(i32)[None],
        ]
    )

    def send(part):
        return lax.all_to_all(part, ("front", "row"), split_axis=0, concat_axis=0, tiled=True)

    strips, parts = permute(slot, tiles, rows_from, cols_from, slots)
    incoming = [send(parts[0])]
    sources = [strips[0]] + [lax.ppermute(strips[c], "col", [(0, c)]) for c in range(1, n_col)]
    strip = slab_strip(slab_meta, columns, send(slot_strips(slot_meta, sources, slots)))

    first, first_inv = panel(corner[:BS, :BS])
    below = dot(corner[BS:, :BS], first_inv)
    below = jnp.where(pattern[0, 0, 1] == 1, below, jnp.zeros_like(below))
    second, second_inv = panel(corner[BS:, BS:] - dot(below, below.T))
    mats = (first_inv, second_inv, dot(below.T, second_inv), first, second)

    part, strip = lax.optimization_barrier((parts[1], strip))
    incoming.append(send(part))
    slab = lax.all_gather(strip, "col", axis=0)
    own = lax.dynamic_slice_in_dim(slab, (my_col % 2) * col_blocks, col_blocks, 1)
    own = jnp.where(my_row == my_col // 2, own, jnp.zeros_like(own))
    part, own, mats = lax.optimization_barrier((parts[2], own, mats))
    incoming.append(send(part))
    across = lax.psum(own, "row")
    return final(meta, slab, across, mats, incoming, row_blocks, col_blocks)[None]


def solution(mesh):
    placed = (
        P(("front", "row", "col"), None, None),
        P(("front", "row", "col"), None),
        P(("front", "row", "col")),
        P(("front", "row", "col")),
        P(("front", "row", "col"), None),
        P(("front", "row", "col"), None),
        P("front", "row", "col"),
        P("front", None, None),
    )
    return jax.shard_map(
        body, mesh=mesh, in_specs=placed, out_specs=P("front", "row", "col"), check_vma=False
    )
```

```python
import jax
import jax.numpy as jnp
from jax import lax
from jax.experimental import pallas as pl
from jax.experimental.pallas import tpu as pltpu
from jax.sharding import PartitionSpec as P

ORDER = 10240
BS = 256
CAP = 4
PIV = 512
STRIP = 32
NSTRIP = BS // STRIP
NCHIP = NSTRIP // 2
PARTS = (2, 3, 3)
OFFSETS = tuple(sum(PARTS[:q]) for q in range(len(PARTS)))
NPART = len(PARTS)
GROUP = 8
RING = 8

HIGH = lax.Precision.HIGHEST
f32, bf16, i32 = jnp.float32, jnp.bfloat16, jnp.int32


def lower_sym(block):
    return jnp.tril(block) + jnp.tril(block, -1).T


def permute_kernel(slot_ref, tile_ref, rows_ref, cols_ref, *refs):
    chip_refs, part_refs = refs[:NCHIP], refs[NCHIP : NCHIP + NPART]
    hold, strip_sems, part_sems = refs[NCHIP + NPART :]
    step = pl.program_id(0)
    half = BS // 2
    lane = lax.broadcasted_iota(i32, (BS, half), 1)
    place = lax.broadcasted_iota(i32, (BS, BS), 0)

    def move(g, carry):
        t = step * GROUP + g
        tile = tile_ref[g]
        high = tile.astype(bf16)
        rest = tile - high.astype(f32)
        mid = rest.astype(bf16)
        low = (rest - mid.astype(f32)).astype(bf16)
        parts = jnp.concatenate([high, mid, low], axis=1)
        wanted = jnp.transpose(jnp.broadcast_to(rows_ref[g], (half, BS)))
        pick_rows = jnp.concatenate(
            [jnp.where(wanted == lane + k * half, 1.0, 0.0) for k in range(2)], axis=1
        ).astype(bf16)
        pick_cols = jnp.where(place == cols_ref[g], 1.0, 0.0).astype(bf16)
        moved = jnp.dot(pick_rows, parts, preferred_element_type=f32).astype(bf16)
        out = jnp.dot(moved[:, :BS], pick_cols, preferred_element_type=f32)
        out = out + jnp.dot(moved[:, BS : 2 * BS], pick_cols, preferred_element_type=f32)
        out = out + jnp.dot(moved[:, 2 * BS :], pick_cols, preferred_element_type=f32)
        hold[t] = out.reshape(NSTRIP, STRIP, BS)
        for k in range(NSTRIP):
            pltpu.make_async_copy(
                hold.at[t, k], chip_refs[k // 2].at[k % 2, t], strip_sems.at[t]
            ).start()
        for q in range(NPART):
            pltpu.make_async_copy(
                hold.at[t, pl.ds(OFFSETS[q], PARTS[q])],
                part_refs[q].at[slot_ref[t]],
                part_sems.at[t],
            ).start()
        return carry

    lax.fori_loop(0, GROUP, move, 0, unroll=2)

    @pl.when(step == pl.num_programs(0) - 1)
    def _():
        def finish(t, carry):
            pltpu.make_async_copy(hold.at[t], hold.at[t], strip_sems.at[t]).wait()
            pltpu.make_async_copy(hold.at[t], hold.at[t], part_sems.at[t]).wait()
            return carry

        lax.fori_loop(0, hold.shape[0], finish, 0)


def permute(slot, tiles, rows_from, cols_from, slots):
    count = tiles.shape[0]
    out = pl.pallas_call(
        permute_kernel,
        grid_spec=pltpu.PrefetchScalarGridSpec(
            num_scalar_prefetch=1,
            grid=(count // GROUP,),
            in_specs=[
                pl.BlockSpec((GROUP, BS, BS), lambda t, slot: (t, 0, 0)),
                pl.BlockSpec((GROUP, 1, BS), lambda t, slot: (t, 0, 0)),
                pl.BlockSpec((GROUP, 1, BS), lambda t, slot: (t, 0, 0)),
            ],
            out_specs=[pl.BlockSpec(memory_space=pl.ANY)] * (NCHIP + NPART),
            scratch_shapes=[
                pltpu.VMEM((count, NSTRIP, STRIP, BS), f32),
                pltpu.SemaphoreType.DMA((count,)),
                pltpu.SemaphoreType.DMA((count,)),
            ],
        ),
        out_shape=[jax.ShapeDtypeStruct((2, count, STRIP, BS), f32)] * NCHIP
        + [jax.ShapeDtypeStruct((slots, n, STRIP, BS), f32) for n in PARTS],
        compiler_params=pltpu.CompilerParams(vmem_limit_bytes=58 << 20),
        cost_estimate=pl.CostEstimate(
            flops=12 * count * BS**3, bytes_accessed=12 * count * BS * BS, transcendentals=0
        ),
        name="permute_tiles",
    )(slot, tiles, rows_from[:, None, :], cols_from[:, None, :])
    return list(out[:NCHIP]), list(out[NCHIP:])


def slot_kernel(count, meta, own_ref, other_ref, out_ref, hold, in_sem, sems):
    @pl.when(meta[count] % 2 == 0)
    def _():
        copy = pltpu.make_async_copy(own_ref.at[0], hold, in_sem)
        copy.start()
        copy.wait()

    @pl.when(meta[count] % 2 == 1)
    def _():
        copy = pltpu.make_async_copy(other_ref, hold, in_sem)
        copy.start()
        copy.wait()

    def begin(t, carry):
        pltpu.make_async_copy(hold.at[t], out_ref.at[meta[t]], sems.at[t]).start()
        return carry

    lax.fori_loop(0, count, begin, 0)

    def finish(t, carry):
        pltpu.make_async_copy(hold.at[t], out_ref.at[meta[t]], sems.at[t]).wait()
        return carry

    lax.fori_loop(0, count, finish, 0)


def slot_strips(meta, own, other, slots):
    count = other.shape[0]
    return pl.pallas_call(
        lambda *refs: slot_kernel(count, *refs),
        grid_spec=pltpu.PrefetchScalarGridSpec(
            num_scalar_prefetch=1,
            grid=(1,),
            in_specs=[pl.BlockSpec(memory_space=pl.ANY)] * 2,
            out_specs=pl.BlockSpec(memory_space=pl.ANY),
            scratch_shapes=[
                pltpu.VMEM(other.shape, f32),
                pltpu.SemaphoreType.DMA(()),
                pltpu.SemaphoreType.DMA((count,)),
            ],
        ),
        out_shape=jax.ShapeDtypeStruct((slots, STRIP, BS), f32),
        compiler_params=pltpu.CompilerParams(vmem_limit_bytes=58 << 20),
        cost_estimate=pl.CostEstimate(
            flops=0, bytes_accessed=8 * count * STRIP * BS, transcendentals=0
        ),
        name="slot_strips",
    )(meta, own, other)


def slab_kernel(meta, initial_ref, in_ref, out_ref, ring, sems):
    total = meta[128]

    def copy(g):
        return pltpu.make_async_copy(in_ref.at[meta[g]], ring.at[g % RING], sems.at[g % RING])

    for g in range(RING):

        @pl.when(g < total)
        def _():
            copy(g).start()

    out_ref[...] = initial_ref[...]

    @pl.loop(0, total)
    def _(g):
        copy(g).wait()
        spot = meta[64 + g]
        cols = pl.ds(pl.multiple_of((spot % 2) * BS, BS), BS)
        out_ref[spot // 2, :, cols] += ring[g % RING]

        @pl.when(g + RING < total)
        def _():
            copy(g + RING).start()


def slab_strip(meta, initial, incoming):
    spec = pl.BlockSpec(initial.shape, lambda i, meta: (0, 0, 0))
    return pl.pallas_call(
        slab_kernel,
        grid_spec=pltpu.PrefetchScalarGridSpec(
            num_scalar_prefetch=1,
            grid=(1,),
            in_specs=[spec, pl.BlockSpec(memory_space=pl.ANY)],
            out_specs=spec,
            scratch_shapes=[
                pltpu.VMEM((RING, STRIP, BS), f32),
                pltpu.SemaphoreType.DMA((RING,)),
            ],
        ),
        out_shape=jax.ShapeDtypeStruct(initial.shape, f32),
        compiler_params=pltpu.CompilerParams(vmem_limit_bytes=32 << 20),
        cost_estimate=pl.CostEstimate(
            flops=0, bytes_accessed=12 * initial.size, transcendentals=0
        ),
        name="slab_strip",
    )(meta, initial, incoming)


def halves(x):
    high = x.astype(bf16)
    return high, (x - high.astype(f32)).astype(bf16)


def final_kernel(col_blocks, *refs):
    meta = refs[0]
    slab, first_inv, second_inv, cross, first_factor, second_factor = refs[1:7]
    across, incoming = refs[7 : 7 + NSTRIP], refs[7 + NSTRIP : 7 + NSTRIP + NPART]
    out_ref, stage, a_high, a_low, ring, sems = refs[7 + NSTRIP + NPART :]
    b = pl.program_id(0)
    total = meta[138]

    def copies(g):
        return [
            pltpu.make_async_copy(
                incoming[q].at[meta[g]],
                ring.at[g % RING, pl.ds(OFFSETS[q], PARTS[q])],
                sems.at[g % RING, q],
            )
            for q in range(NPART)
        ]

    def solve(block, keep_first, keep_second):
        one = jnp.dot(block[:, :BS], first_inv[...], precision=HIGH, preferred_element_type=f32)
        one = jnp.where(keep_first == 1, one, 0.0)
        two = jnp.dot(block[:, BS:], second_inv[...], precision=HIGH, preferred_element_type=f32)
        two = two - jnp.dot(one, cross[...], precision=HIGH, preferred_element_type=f32)
        return one, jnp.where(keep_second == 1, two, 0.0)

    @pl.when(b == 0)
    def _():
        for g in range(RING):

            @pl.when(g < total)
            def _():
                for c in copies(g):
                    c.start()

        for step in range(NSTRIP):
            stage[(meta[171] + NSTRIP - step) % NSTRIP] = across[step][...]
        for cb in range(col_blocks):
            one, two = solve(stage[:, cb].reshape(BS, PIV), meta[159 + cb], meta[164 + cb])
            high, low = halves(jnp.concatenate([one, two], axis=1).T)
            a_high[:, cb * BS : (cb + 1) * BS] = high
            a_low[:, cb * BS : (cb + 1) * BS] = low

    one, two = solve(slab[:, 0].reshape(BS, PIV), meta[139 + b], meta[149 + b])
    top = meta[169] == 1
    high, low = halves(
        jnp.where(jnp.logical_and(top, b < 2), 0.0, jnp.concatenate([one, two], axis=1))
    )
    for cb in range(col_blocks):
        cols = slice(cb * BS, (cb + 1) * BS)
        product = jnp.dot(high, a_low[:, cols], preferred_element_type=f32)
        product = product + jnp.dot(low, a_high[:, cols], preferred_element_type=f32)
        product = product + jnp.dot(high, a_high[:, cols], preferred_element_type=f32)
        out_ref[:, cols] = -product

    @pl.loop(meta[128 + b], meta[129 + b])
    def _(g):
        for c in copies(g):
            c.wait()
        cols = pl.ds(pl.multiple_of(meta[64 + g] * BS, BS), BS)
        out_ref[:, cols] += ring[g % RING].reshape(BS, BS)

        @pl.when(g + RING < total)
        def _():
            for c in copies(g + RING):
                c.start()

    @pl.when(meta[170] == 1)
    def _():
        out_ref[:, :BS] = jnp.where(jnp.logical_and(top, b == 0), first_factor[...], one)
        out_ref[:, BS:PIV] = jnp.where(jnp.logical_and(top, b == 1), second_factor[...], two)


def final(meta, slab, across, mats, incoming, row_blocks, col_blocks):
    whole = pl.BlockSpec((BS, BS), lambda b, meta: (0, 0))
    return pl.pallas_call(
        lambda *refs: final_kernel(col_blocks, *refs),
        grid_spec=pltpu.PrefetchScalarGridSpec(
            num_scalar_prefetch=1,
            grid=(row_blocks,),
            in_specs=[
                pl.BlockSpec((NSTRIP, 1, STRIP, PIV), lambda b, meta: (0, b, 0, 0)),
            ]
            + [whole] * 5
            + [pl.BlockSpec((col_blocks, STRIP, PIV), lambda b, meta: (0, 0, 0))] * NSTRIP
            + [pl.BlockSpec(memory_space=pl.ANY)] * NPART,
            out_specs=pl.BlockSpec((BS, col_blocks * BS), lambda b, meta: (b, 0)),
            scratch_shapes=[
                pltpu.VMEM((NSTRIP, col_blocks, STRIP, PIV), f32),
                pltpu.VMEM((PIV, col_blocks * BS), bf16),
                pltpu.VMEM((PIV, col_blocks * BS), bf16),
                pltpu.VMEM((RING, NSTRIP, STRIP, BS), f32),
                pltpu.SemaphoreType.DMA((RING, NPART)),
            ],
        ),
        out_shape=jax.ShapeDtypeStruct((row_blocks * BS, col_blocks * BS), f32),
        compiler_params=pltpu.CompilerParams(vmem_limit_bytes=48 << 20),
        cost_estimate=pl.CostEstimate(
            flops=6 * row_blocks * col_blocks * BS * BS * PIV,
            bytes_accessed=4 * 2 * row_blocks * col_blocks * BS * BS,
            transcendentals=0,
        ),
        name="place_and_update",
    )(meta, slab, *mats, *across, *incoming)


def dot(a, b):
    return jnp.dot(a, b, precision=HIGH)


def inverse(lower):
    size = lower.shape[0]
    eye = jnp.eye(size, dtype=f32)
    scale = jnp.sum(lower * eye, axis=0)
    power = eye - lower / scale[None, :]
    out = eye + power
    for _ in range(6):
        power = dot(power, power)
        out = out + dot(power, out)
    return out / scale[:, None]


def panel(block):
    half = BS // 2
    first = jnp.linalg.cholesky(lower_sym(block[:half, :half]))
    first_inv = inverse(first)
    below = dot(block[half:, :half], first_inv.T)
    second = jnp.linalg.cholesky(lower_sym(block[half:, half:] - dot(below, below.T)))
    second_inv = inverse(second)
    across = -dot(second_inv, dot(below, first_inv))
    zero = jnp.zeros((half, half), f32)
    factor = jnp.block([[first, zero], [below, second]])
    return factor, jnp.block([[first_inv.T, across.T], [zero, second_inv.T]])


def ordered(key, valid, span):
    count = key.shape[0]
    key = jnp.where(valid, key, span)
    index = jnp.arange(count, dtype=i32)
    ahead = (key[None, :] < key[:, None]) | (
        (key[None, :] == key[:, None]) & (index[None, :] < index[:, None])
    )
    rank = jnp.sum(ahead.astype(i32), axis=1)
    chosen = rank[None, :] == index[:, None]
    order = jnp.sum(jnp.where(chosen, index[None, :], 0), axis=1)
    return order, jnp.sum(jnp.where(chosen, key[None, :], 0), axis=1), key


def body(tiles, dest, block_row, block_col, rows_from, cols_from, initial, pattern):
    n_front = lax.axis_size("front")
    n_row = lax.axis_size("row")
    n_col = lax.axis_size("col")
    my_row = lax.axis_index("row")
    my_col = lax.axis_index("col")
    row_blocks = ORDER // n_row // BS
    col_blocks = ORDER // n_col // BS
    lead = PIV // BS
    slots = n_front * n_row * CAP
    target = dest[:, 0]
    owner_row = target % n_row
    local_row = jnp.where(owner_row == 0, lead + block_row % (row_blocks - lead), block_row)
    block_id = local_row * col_blocks + block_col
    same = (target[:, None] == target[None, :]).astype(i32)
    slot = target * CAP + jnp.sum(jnp.tril(same, -1), axis=1)
    choose = jnp.arange(slots, dtype=i32)[:, None] == slot[None, :]
    labels = jnp.where(
        jnp.any(choose, axis=1), jnp.sum(jnp.where(choose, block_id[None, :], 0), axis=1), -1
    )
    names = lax.all_to_all(labels, ("front", "row"), split_axis=0, concat_axis=0, tiled=True)

    row = jnp.zeros((1, initial.shape[2]), f32)
    slot_row = row.at[0, : slot.shape[0]].set(slot.astype(f32))
    near = lax.all_gather(
        jnp.concatenate([initial[0, :PIV], jnp.broadcast_to(slot_row, (8, row.shape[1]))]),
        ("row", "col"),
        axis=0,
    )
    corner = near[:n_col, :PIV].transpose(1, 0, 2).reshape(PIV, PIV)
    first_slot = lax.dynamic_index_in_dim(near[:, PIV], my_row * n_col, 0, keepdims=False)
    slot_meta = jnp.append(first_slot[: slot.shape[0]].astype(i32), my_col)
    strips, parts = permute(slot, tiles, rows_from, cols_from, slots)
    names, parts[0] = lax.optimization_barrier((names, parts[0]))
    names_row = row.at[0, :slots].set(names.astype(f32))
    wide = lax.all_gather(
        jnp.concatenate([initial[0], jnp.broadcast_to(names_row, (8, row.shape[1]))]), "col", axis=0
    )
    first_names = wide[0, row_blocks * BS, :slots].astype(i32)
    columns = wide[:, : row_blocks * BS].reshape(n_col, row_blocks, NSTRIP, STRIP, -1)
    columns = lax.dynamic_index_in_dim(columns, my_col, 2, keepdims=False)
    columns = columns.transpose(1, 2, 0, 3).reshape(row_blocks, STRIP, PIV)

    valid = names >= 0
    order, sorted_id, key = ordered(names, valid, row_blocks * col_blocks)
    bounds = jnp.arange(row_blocks + 1, dtype=i32)[:, None] * col_blocks
    starts = jnp.sum((key[None, :] < bounds).astype(i32), axis=1)
    in_slab = (first_names >= 0) & (first_names % col_blocks < lead)
    slab_key = (first_names // col_blocks) * lead + first_names % col_blocks
    slab_order, slab_id, _ = ordered(slab_key, in_slab, row_blocks * lead)
    slab_meta = jnp.concatenate([slab_order, slab_id, jnp.sum(in_slab.astype(i32))[None]])

    def kept(first_block, count):
        blocks = first_block + jnp.arange(count, dtype=i32)
        flags = lax.dynamic_slice_in_dim(pattern[0], first_block, count, axis=1)
        ahead = blocks[None, :] > jnp.arange(2, dtype=i32)[:, None]
        return jnp.where(ahead, flags, 0).reshape(-1)

    meta = jnp.concatenate(
        [
            order,
            sorted_id % col_blocks,
            starts,
            kept(my_row * row_blocks, row_blocks),
            kept(my_col * col_blocks, col_blocks),
            (my_row == 0).astype(i32)[None],
            (my_col == 0).astype(i32)[None],
            my_col[None],
        ]
    )

    def send(part):
        return lax.all_to_all(part, ("front", "row"), split_axis=0, concat_axis=0, tiled=True)

    incoming = [send(parts[0])]
    got = [lax.ppermute(strips[k], "col", [(0, 2 * k)]) for k in range(1, NCHIP)]
    own = jnp.where(my_col == 0, strips[0], got[0] + got[1] + got[2])
    other = lax.ppermute(own[1], "col", [(2 * k, 2 * k + 1) for k in range(NCHIP)])
    slotted = slot_strips(slot_meta, own, other, slots)
    slotted, incoming[0] = lax.optimization_barrier((slotted, incoming[0]))
    strip = slab_strip(slab_meta, columns, send(slotted))

    first, first_inv = panel(corner[:BS, :BS])
    below = dot(corner[BS:, :BS], first_inv)
    below = jnp.where(pattern[0, 0, 1] == 1, below, jnp.zeros_like(below))
    second, second_inv = panel(corner[BS:, BS:] - dot(below, below.T))
    mats = (first_inv, second_inv, dot(below.T, second_inv), first, second)

    part, strip = lax.optimization_barrier((parts[1], strip))
    incoming.append(send(part))
    rows = lax.all_gather(strip, "row", axis=0)
    part, rows, strip, mats = lax.optimization_barrier((parts[2], rows, strip, mats))
    incoming.append(send(part))
    slab = lax.all_gather(strip, "col", axis=0)
    rows = rows.reshape(n_col, col_blocks, STRIP, PIV)
    across = []
    for step in range(n_col):
        piece = lax.dynamic_index_in_dim(rows, (my_col + step) % n_col, 0, keepdims=False)
        if step:
            piece = lax.ppermute(piece, "col", [(c, (c + step) % n_col) for c in range(n_col)])
        across.append(piece)
    return final(meta, slab, across, mats, incoming, row_blocks, col_blocks)[None]


def solution(mesh):
    placed = (
        P(("front", "row", "col"), None, None),
        P(("front", "row", "col"), None),
        P(("front", "row", "col")),
        P(("front", "row", "col")),
        P(("front", "row", "col"), None),
        P(("front", "row", "col"), None),
        P("front", "row", "col"),
        P("front", None, None),
    )
    return jax.shard_map(
        body, mesh=mesh, in_specs=placed, out_specs=P("front", "row", "col"), check_vma=False
    )
```

```python
import jax
import jax.numpy as jnp
from jax import lax
from jax.experimental import pallas as pl
from jax.experimental.pallas import tpu as pltpu
from jax.sharding import PartitionSpec as P

ORDER = 10240
BS = 256
CAP = 4
PIV = 512
STRIP = 32
NSTRIP = BS // STRIP
NCHIP = NSTRIP // 2
PARTS = (2, 3, 3)
OFFSETS = tuple(sum(PARTS[:q]) for q in range(len(PARTS)))
NPART = len(PARTS)
GROUP = 8
RING = 8

HIGH = lax.Precision.HIGHEST
f32, bf16, i32 = jnp.float32, jnp.bfloat16, jnp.int32


def lower_sym(block):
    return jnp.tril(block) + jnp.tril(block, -1).T


def permute_kernel(slot_ref, tile_ref, rows_ref, cols_ref, *refs):
    chip_refs, part_refs = refs[:NCHIP], refs[NCHIP : NCHIP + NPART]
    hold, strip_sems, part_sems = refs[NCHIP + NPART :]
    step = pl.program_id(0)
    half = BS // 2
    lane = lax.broadcasted_iota(i32, (BS, half), 1)
    place = lax.broadcasted_iota(i32, (BS, BS), 0)

    def move(g, carry):
        t = step * GROUP + g
        tile = tile_ref[g]
        high = tile.astype(bf16)
        rest = tile - high.astype(f32)
        mid = rest.astype(bf16)
        low = (rest - mid.astype(f32)).astype(bf16)
        parts = jnp.concatenate([high, mid, low], axis=1)
        wanted = jnp.transpose(jnp.broadcast_to(rows_ref[g], (half, BS)))
        pick_rows = jnp.concatenate(
            [jnp.where(wanted == lane + k * half, 1.0, 0.0) for k in range(2)], axis=1
        ).astype(bf16)
        pick_cols = jnp.where(place == cols_ref[g], 1.0, 0.0).astype(bf16)
        moved = jnp.dot(pick_rows, parts, preferred_element_type=f32).astype(bf16)
        out = jnp.dot(moved[:, :BS], pick_cols, preferred_element_type=f32)
        out = out + jnp.dot(moved[:, BS : 2 * BS], pick_cols, preferred_element_type=f32)
        out = out + jnp.dot(moved[:, 2 * BS :], pick_cols, preferred_element_type=f32)
        hold[t] = out.reshape(NSTRIP, STRIP, BS)
        for k in range(NSTRIP):
            pltpu.make_async_copy(
                hold.at[t, k], chip_refs[k // 2].at[k % 2, t], strip_sems.at[t]
            ).start()
        for q in range(NPART):
            pltpu.make_async_copy(
                hold.at[t, pl.ds(OFFSETS[q], PARTS[q])],
                part_refs[q].at[slot_ref[t]],
                part_sems.at[t],
            ).start()
        return carry

    lax.fori_loop(0, GROUP, move, 0, unroll=2)

    @pl.when(step == pl.num_programs(0) - 1)
    def _():
        def finish(t, carry):
            pltpu.make_async_copy(hold.at[t], hold.at[t], strip_sems.at[t]).wait()
            pltpu.make_async_copy(hold.at[t], hold.at[t], part_sems.at[t]).wait()
            return carry

        lax.fori_loop(0, hold.shape[0], finish, 0)


def permute(slot, tiles, rows_from, cols_from, slots):
    count = tiles.shape[0]
    out = pl.pallas_call(
        permute_kernel,
        grid_spec=pltpu.PrefetchScalarGridSpec(
            num_scalar_prefetch=1,
            grid=(count // GROUP,),
            in_specs=[
                pl.BlockSpec((GROUP, BS, BS), lambda t, slot: (t, 0, 0)),
                pl.BlockSpec((GROUP, 1, BS), lambda t, slot: (t, 0, 0)),
                pl.BlockSpec((GROUP, 1, BS), lambda t, slot: (t, 0, 0)),
            ],
            out_specs=[pl.BlockSpec(memory_space=pl.ANY)] * (NCHIP + NPART),
            scratch_shapes=[
                pltpu.VMEM((count, NSTRIP, STRIP, BS), f32),
                pltpu.SemaphoreType.DMA((count,)),
                pltpu.SemaphoreType.DMA((count,)),
            ],
        ),
        out_shape=[jax.ShapeDtypeStruct((2, count, STRIP, BS), f32)] * NCHIP
        + [jax.ShapeDtypeStruct((slots, n, STRIP, BS), f32) for n in PARTS],
        compiler_params=pltpu.CompilerParams(vmem_limit_bytes=58 << 20),
        cost_estimate=pl.CostEstimate(
            flops=12 * count * BS**3, bytes_accessed=12 * count * BS * BS, transcendentals=0
        ),
        name="permute_tiles",
    )(slot, tiles, rows_from[:, None, :], cols_from[:, None, :])
    return list(out[:NCHIP]), list(out[NCHIP:])


def slot_kernel(count, meta, own_ref, other_ref, out_ref, hold, in_sem, sems):
    @pl.when(meta[count] % 2 == 0)
    def _():
        copy = pltpu.make_async_copy(own_ref.at[0], hold, in_sem)
        copy.start()
        copy.wait()

    @pl.when(meta[count] % 2 == 1)
    def _():
        copy = pltpu.make_async_copy(other_ref, hold, in_sem)
        copy.start()
        copy.wait()

    def begin(t, carry):
        pltpu.make_async_copy(hold.at[t], out_ref.at[meta[t]], sems.at[t]).start()
        return carry

    lax.fori_loop(0, count, begin, 0)

    def finish(t, carry):
        pltpu.make_async_copy(hold.at[t], out_ref.at[meta[t]], sems.at[t]).wait()
        return carry

    lax.fori_loop(0, count, finish, 0)


def slot_strips(meta, own, other, slots):
    count = other.shape[0]
    return pl.pallas_call(
        lambda *refs: slot_kernel(count, *refs),
        grid_spec=pltpu.PrefetchScalarGridSpec(
            num_scalar_prefetch=1,
            grid=(1,),
            in_specs=[pl.BlockSpec(memory_space=pl.ANY)] * 2,
            out_specs=pl.BlockSpec(memory_space=pl.ANY),
            scratch_shapes=[
                pltpu.VMEM(other.shape, f32),
                pltpu.SemaphoreType.DMA(()),
                pltpu.SemaphoreType.DMA((count,)),
            ],
        ),
        out_shape=jax.ShapeDtypeStruct((slots, STRIP, BS), f32),
        compiler_params=pltpu.CompilerParams(vmem_limit_bytes=58 << 20),
        cost_estimate=pl.CostEstimate(
            flops=0, bytes_accessed=8 * count * STRIP * BS, transcendentals=0
        ),
        name="slot_strips",
    )(meta, own, other)


def slab_kernel(meta, wide_ref, in_ref, out_ref, hold, ring, hold_sems, sems):
    total = meta[128]
    pieces, blocks, width = hold.shape[0], hold.shape[1], hold.shape[3]

    def copy(g):
        return pltpu.make_async_copy(in_ref.at[meta[g]], ring.at[g % RING], sems.at[g % RING])

    def initial(b):
        rows = pl.ds(pl.multiple_of(b * BS + meta[129] * STRIP, STRIP), STRIP)
        return pltpu.make_async_copy(wide_ref.at[:, rows], hold.at[:, b], hold_sems.at[b])

    for b in range(blocks):
        initial(b).start()
    for g in range(RING):

        @pl.when(g < total)
        def _():
            copy(g).start()

    for b in range(blocks):
        initial(b).wait()
    for k in range(pieces):
        out_ref[:, :, k * width : (k + 1) * width] = hold[k]

    @pl.loop(0, total)
    def _(g):
        copy(g).wait()
        spot = meta[64 + g]
        cols = pl.ds(pl.multiple_of((spot % 2) * BS, BS), BS)
        out_ref[spot // 2, :, cols] += ring[g % RING]

        @pl.when(g + RING < total)
        def _():
            copy(g + RING).start()


def slab_strip(meta, wide, incoming):
    pieces, rows, width = wide.shape
    blocks = rows // BS
    shape = (blocks, STRIP, pieces * width)
    return pl.pallas_call(
        slab_kernel,
        grid_spec=pltpu.PrefetchScalarGridSpec(
            num_scalar_prefetch=1,
            grid=(1,),
            in_specs=[pl.BlockSpec(memory_space=pl.ANY)] * 2,
            out_specs=pl.BlockSpec(shape, lambda i, meta: (0, 0, 0)),
            scratch_shapes=[
                pltpu.VMEM((pieces, blocks, STRIP, width), f32),
                pltpu.VMEM((RING, STRIP, BS), f32),
                pltpu.SemaphoreType.DMA((blocks,)),
                pltpu.SemaphoreType.DMA((RING,)),
            ],
        ),
        out_shape=jax.ShapeDtypeStruct(shape, f32),
        compiler_params=pltpu.CompilerParams(vmem_limit_bytes=32 << 20),
        cost_estimate=pl.CostEstimate(
            flops=0, bytes_accessed=12 * blocks * STRIP * PIV, transcendentals=0
        ),
        name="slab_strip",
    )(meta, wide, incoming)


def halves(x):
    high = x.astype(bf16)
    return high, (x - high.astype(f32)).astype(bf16)


def final_kernel(col_blocks, *refs):
    meta = refs[0]
    slab, first_factor, second_factor = refs[1:4]
    across, incoming = refs[4 : 4 + NSTRIP], refs[4 + NSTRIP : 4 + NSTRIP + NPART]
    out_ref, stage, a_high, a_low, ring, sems = refs[4 + NSTRIP + NPART :]
    b = pl.program_id(0)
    total = meta[138]

    def copies(g):
        return [
            pltpu.make_async_copy(
                incoming[q].at[meta[g]],
                ring.at[g % RING, pl.ds(OFFSETS[q], PARTS[q])],
                sems.at[g % RING, q],
            )
            for q in range(NPART)
        ]

    @pl.when(b == 0)
    def _():
        for g in range(RING):

            @pl.when(g < total)
            def _():
                for c in copies(g):
                    c.start()

        for step in range(NSTRIP):
            stage[(meta[140] + NSTRIP - step) % NSTRIP] = across[step][...]
        for cb in range(col_blocks):
            high, low = halves(stage[:, cb].reshape(BS, PIV).T)
            a_high[:, cb * BS : (cb + 1) * BS] = high
            a_low[:, cb * BS : (cb + 1) * BS] = low

    rows = slab[:, 0].reshape(BS, PIV)
    top = meta[139] == 1
    high, low = halves(jnp.where(jnp.logical_and(top, b < 2), 0.0, rows))
    for cb in range(col_blocks):
        cols = slice(cb * BS, (cb + 1) * BS)
        product = jnp.dot(high, a_low[:, cols], preferred_element_type=f32)
        product = product + jnp.dot(low, a_high[:, cols], preferred_element_type=f32)
        product = product + jnp.dot(high, a_high[:, cols], preferred_element_type=f32)
        out_ref[:, cols] = -product

    @pl.loop(meta[128 + b], meta[129 + b])
    def _(g):
        for c in copies(g):
            c.wait()
        cols = pl.ds(pl.multiple_of(meta[64 + g] * BS, BS), BS)
        out_ref[:, cols] += ring[g % RING].reshape(BS, BS)

        @pl.when(g + RING < total)
        def _():
            for c in copies(g + RING):
                c.start()

    @pl.when(meta[140] == 0)
    def _():
        out_ref[:, :BS] = jnp.where(jnp.logical_and(top, b == 0), first_factor[...], rows[:, :BS])
        out_ref[:, BS:PIV] = jnp.where(jnp.logical_and(top, b == 1), second_factor[...], rows[:, BS:])


def final(meta, slab, across, mats, incoming, row_blocks, col_blocks):
    whole = pl.BlockSpec((BS, BS), lambda b, meta: (0, 0))
    return pl.pallas_call(
        lambda *refs: final_kernel(col_blocks, *refs),
        grid_spec=pltpu.PrefetchScalarGridSpec(
            num_scalar_prefetch=1,
            grid=(row_blocks,),
            in_specs=[
                pl.BlockSpec((NSTRIP, 1, STRIP, PIV), lambda b, meta: (0, b, 0, 0)),
            ]
            + [whole] * 2
            + [pl.BlockSpec((col_blocks, STRIP, PIV), lambda b, meta: (0, 0, 0))] * NSTRIP
            + [pl.BlockSpec(memory_space=pl.ANY)] * NPART,
            out_specs=pl.BlockSpec((BS, col_blocks * BS), lambda b, meta: (b, 0)),
            scratch_shapes=[
                pltpu.VMEM((NSTRIP, col_blocks, STRIP, PIV), f32),
                pltpu.VMEM((PIV, col_blocks * BS), bf16),
                pltpu.VMEM((PIV, col_blocks * BS), bf16),
                pltpu.VMEM((RING, NSTRIP, STRIP, BS), f32),
                pltpu.SemaphoreType.DMA((RING, NPART)),
            ],
        ),
        out_shape=jax.ShapeDtypeStruct((row_blocks * BS, col_blocks * BS), f32),
        compiler_params=pltpu.CompilerParams(vmem_limit_bytes=48 << 20),
        cost_estimate=pl.CostEstimate(
            flops=6 * row_blocks * col_blocks * BS * BS * PIV,
            bytes_accessed=4 * 2 * row_blocks * col_blocks * BS * BS,
            transcendentals=0,
        ),
        name="place_and_update",
    )(meta, slab, *mats, *across, *incoming)


def dot(a, b):
    return jnp.dot(a, b, precision=HIGH)


def inverse(lower):
    size = lower.shape[0]
    eye = jnp.eye(size, dtype=f32)
    scale = jnp.sum(lower * eye, axis=0)
    power = eye - lower / scale[None, :]
    out = eye + power
    for _ in range(6):
        power = dot(power, power)
        out = out + dot(power, out)
    return out / scale[:, None]


def panel(block):
    half = BS // 2
    first = jnp.linalg.cholesky(lower_sym(block[:half, :half]))
    first_inv = inverse(first)
    below = dot(block[half:, :half], first_inv.T)
    second = jnp.linalg.cholesky(lower_sym(block[half:, half:] - dot(below, below.T)))
    second_inv = inverse(second)
    across = -dot(second_inv, dot(below, first_inv))
    zero = jnp.zeros((half, half), f32)
    factor = jnp.block([[first, zero], [below, second]])
    return factor, jnp.block([[first_inv.T, across.T], [zero, second_inv.T]])


def ordered(key, valid, span):
    count = key.shape[0]
    key = jnp.where(valid, key, span)
    index = jnp.arange(count, dtype=i32)
    ahead = (key[None, :] < key[:, None]) | (
        (key[None, :] == key[:, None]) & (index[None, :] < index[:, None])
    )
    rank = jnp.sum(ahead.astype(i32), axis=1)
    chosen = rank[None, :] == index[:, None]
    order = jnp.sum(jnp.where(chosen, index[None, :], 0), axis=1)
    return order, jnp.sum(jnp.where(chosen, key[None, :], 0), axis=1), key


def body(tiles, dest, block_row, block_col, rows_from, cols_from, initial, pattern):
    n_front = lax.axis_size("front")
    n_row = lax.axis_size("row")
    n_col = lax.axis_size("col")
    my_row = lax.axis_index("row")
    my_col = lax.axis_index("col")
    row_blocks = ORDER // n_row // BS
    col_blocks = ORDER // n_col // BS
    lead = PIV // BS
    slots = n_front * n_row * CAP
    target = dest[:, 0]
    owner_row = target % n_row
    local_row = jnp.where(owner_row == 0, lead + block_row % (row_blocks - lead), block_row)
    block_id = local_row * col_blocks + block_col
    same = (target[:, None] == target[None, :]).astype(i32)
    slot = target * CAP + jnp.sum(jnp.tril(same, -1), axis=1)
    choose = jnp.arange(slots, dtype=i32)[:, None] == slot[None, :]
    labels = jnp.where(
        jnp.any(choose, axis=1), jnp.sum(jnp.where(choose, block_id[None, :], 0), axis=1), -1
    )
    row = jnp.zeros((1, initial.shape[2]), f32).at[0, : slot.shape[0]].set(slot.astype(f32))
    near = lax.all_gather(
        jnp.concatenate([initial[0, :PIV], jnp.broadcast_to(row, (8, row.shape[1]))]),
        ("row", "col"),
        axis=0,
    )
    corner = near[:n_col, :PIV].transpose(1, 0, 2).reshape(PIV, PIV)
    first_slot = lax.dynamic_index_in_dim(near[:, PIV], my_row * n_col, 0, keepdims=False)
    slot_meta = jnp.append(first_slot[: slot.shape[0]].astype(i32), my_col)
    every = lax.all_gather(labels, ("front", "row"), axis=0)
    mine = (lax.axis_index("front") * n_row + my_row) * CAP
    names = lax.dynamic_slice_in_dim(every, mine, CAP, 1).reshape(slots)
    first_names = lax.all_gather(names, "col", axis=0)[0]

    valid = names >= 0
    order, sorted_id, key = ordered(names, valid, row_blocks * col_blocks)
    bounds = jnp.arange(row_blocks + 1, dtype=i32)[:, None] * col_blocks
    starts = jnp.sum((key[None, :] < bounds).astype(i32), axis=1)
    in_slab = (first_names >= 0) & (first_names % col_blocks < lead)
    slab_key = (first_names // col_blocks) * lead + first_names % col_blocks
    slab_order, slab_id, _ = ordered(slab_key, in_slab, row_blocks * lead)
    slab_meta = jnp.concatenate(
        [slab_order, slab_id, jnp.sum(in_slab.astype(i32))[None], my_col[None]]
    )

    meta = jnp.concatenate(
        [order, sorted_id % col_blocks, starts, (my_row == 0).astype(i32)[None], my_col[None]]
    )

    def send(part):
        return lax.all_to_all(part, ("front", "row"), split_axis=0, concat_axis=0, tiled=True)

    strips, parts = permute(slot, tiles, rows_from, cols_from, slots)
    incoming = [send(parts[0])]
    got = [lax.ppermute(strips[k], "col", [(0, 2 * k)]) for k in range(1, NCHIP)]
    own = jnp.where(my_col == 0, strips[0], got[0] + got[1] + got[2])
    own, pivot_columns = lax.optimization_barrier((own, initial[0]))
    other = lax.ppermute(own[1], "col", [(2 * k, 2 * k + 1) for k in range(NCHIP)])
    wide = lax.all_gather(pivot_columns, "col", axis=0)

    first, first_inv = panel(corner[:BS, :BS])
    below = dot(corner[BS:, :BS], first_inv)
    below = jnp.where(pattern[0, 0, 1] == 1, below, jnp.zeros_like(below))
    rest = corner[BS:, BS:] - dot(below, below.T)
    other, rest = lax.optimization_barrier((other, rest))
    slotted = slot_strips(slot_meta, own, other, slots)
    slotted, rest, incoming[0] = lax.optimization_barrier((slotted, rest, incoming[0]))
    strip = slab_strip(slab_meta, wide, send(slotted))
    second, second_inv = panel(rest)
    cross = dot(below.T, second_inv)

    blocks = my_row * row_blocks + jnp.arange(row_blocks, dtype=i32)
    flags = lax.dynamic_slice_in_dim(pattern[0], my_row * row_blocks, row_blocks, 1)
    keep = (flags == 1) & (blocks[None, :] > jnp.arange(2, dtype=i32)[:, None])
    keep = jnp.repeat(keep, STRIP, axis=1)[:, :, None]
    strip = strip.reshape(row_blocks * STRIP, PIV)
    one = dot(strip[:, :BS], first_inv)
    one = jnp.where(keep[0], one, jnp.zeros_like(one))
    two = dot(strip[:, BS:], second_inv) - dot(one, cross)
    two = jnp.where(keep[1], two, jnp.zeros_like(two))
    solved = jnp.concatenate([one, two], axis=1).reshape(row_blocks, STRIP, PIV)

    part, solved = lax.optimization_barrier((parts[1], solved))
    incoming.append(send(part))
    rows = lax.all_gather(solved, "row", axis=0)
    part, rows, solved = lax.optimization_barrier((parts[2], rows, solved))
    incoming.append(send(part))
    slab = lax.all_gather(solved, "col", axis=0)
    rows = rows.reshape(n_col, col_blocks, STRIP, PIV)
    across = []
    for step in range(n_col):
        piece = lax.dynamic_index_in_dim(rows, (my_col + step) % n_col, 0, keepdims=False)
        if step:
            piece = lax.ppermute(piece, "col", [(c, (c + step) % n_col) for c in range(n_col)])
        across.append(piece)
    return final(meta, slab, across, (first, second), incoming, row_blocks, col_blocks)[None]


def solution(mesh):
    placed = (
        P(("front", "row", "col"), None, None),
        P(("front", "row", "col"), None),
        P(("front", "row", "col")),
        P(("front", "row", "col")),
        P(("front", "row", "col"), None),
        P(("front", "row", "col"), None),
        P("front", "row", "col"),
        P("front", None, None),
    )
    return jax.shard_map(
        body, mesh=mesh, in_specs=placed, out_specs=P("front", "row", "col"), check_vma=False
    )
```

```python
import jax
import jax.numpy as jnp
from jax import lax
from jax.experimental import pallas as pl
from jax.experimental.pallas import tpu as pltpu
from jax.sharding import PartitionSpec as P

ORDER = 10240
BS = 256
CAP = 4
PIV = 512
STRIP = 32
NSTRIP = BS // STRIP
NCHIP = NSTRIP // 2
MARK = 8
PARTS = (64, 96, 96)
OFFSETS = tuple(sum(PARTS[:q]) for q in range(len(PARTS)))
NPART = len(PARTS)
GROUP = 8
RING = 8

HIGH = lax.Precision.HIGHEST
f32, bf16, i32 = jnp.float32, jnp.bfloat16, jnp.int32


def lower_sym(block):
    return jnp.tril(block) + jnp.tril(block, -1).T


def permute_kernel(slot_ref, label_ref, tile_ref, rows_ref, cols_ref, *refs):
    chip_refs, part_refs = refs[:NCHIP], refs[NCHIP : NCHIP + NPART]
    hold, mark, mark_sem, strip_sems, part_sems = refs[NCHIP + NPART :]
    step = pl.program_id(0)

    def marks():
        rows = part_refs[0].at[:, pl.ds(PARTS[0], MARK)]
        return pltpu.make_async_copy(mark, rows, mark_sem)

    @pl.when(step == 0)
    def _():
        def fill(s, carry):
            mark[s] = jnp.full(mark.shape[1:], label_ref[s].astype(f32))
            return carry

        lax.fori_loop(0, mark.shape[0], fill, 0)
        marks().start()

    half = BS // 2
    lane = lax.broadcasted_iota(i32, (BS, half), 1)
    place = lax.broadcasted_iota(i32, (BS, BS), 0)

    def move(g, carry):
        t = step * GROUP + g
        tile = tile_ref[g]
        high = tile.astype(bf16)
        rest = tile - high.astype(f32)
        mid = rest.astype(bf16)
        low = (rest - mid.astype(f32)).astype(bf16)
        parts = jnp.concatenate([high, mid, low], axis=1)
        wanted = jnp.transpose(jnp.broadcast_to(rows_ref[g], (half, BS)))
        pick_rows = jnp.concatenate(
            [jnp.where(wanted == lane + k * half, 1.0, 0.0) for k in range(2)], axis=1
        ).astype(bf16)
        pick_cols = jnp.where(place == cols_ref[g], 1.0, 0.0).astype(bf16)
        moved = jnp.dot(pick_rows, parts, preferred_element_type=f32).astype(bf16)
        out = jnp.dot(moved[:, :BS], pick_cols, preferred_element_type=f32)
        out = out + jnp.dot(moved[:, BS : 2 * BS], pick_cols, preferred_element_type=f32)
        out = out + jnp.dot(moved[:, 2 * BS :], pick_cols, preferred_element_type=f32)
        hold[t] = out
        for k in range(NSTRIP):
            pltpu.make_async_copy(
                hold.at[t, pl.ds(k * STRIP, STRIP)], chip_refs[k // 2].at[k % 2, t], strip_sems.at[t]
            ).start()
        for q in range(NPART):
            pltpu.make_async_copy(
                hold.at[t, pl.ds(OFFSETS[q], PARTS[q])],
                part_refs[q].at[slot_ref[t], pl.ds(0, PARTS[q])],
                part_sems.at[t],
            ).start()
        return carry

    lax.fori_loop(0, GROUP, move, 0, unroll=2)

    @pl.when(step == pl.num_programs(0) - 1)
    def _():
        def finish(t, carry):
            pltpu.make_async_copy(hold.at[t], hold.at[t], strip_sems.at[t]).wait()
            pltpu.make_async_copy(hold.at[t], hold.at[t], part_sems.at[t]).wait()
            return carry

        lax.fori_loop(0, hold.shape[0], finish, 0)
        marks().wait()


def permute(slot, labels, tiles, rows_from, cols_from, slots):
    count = tiles.shape[0]
    out = pl.pallas_call(
        permute_kernel,
        grid_spec=pltpu.PrefetchScalarGridSpec(
            num_scalar_prefetch=2,
            grid=(count // GROUP,),
            in_specs=[
                pl.BlockSpec((GROUP, BS, BS), lambda t, slot, labels: (t, 0, 0)),
                pl.BlockSpec((GROUP, 1, BS), lambda t, slot, labels: (t, 0, 0)),
                pl.BlockSpec((GROUP, 1, BS), lambda t, slot, labels: (t, 0, 0)),
            ],
            out_specs=[pl.BlockSpec(memory_space=pl.ANY)] * (NCHIP + NPART),
            scratch_shapes=[
                pltpu.VMEM((count, BS, BS), f32),
                pltpu.VMEM((slots, MARK, BS), f32),
                pltpu.SemaphoreType.DMA(()),
                pltpu.SemaphoreType.DMA((count,)),
                pltpu.SemaphoreType.DMA((count,)),
            ],
        ),
        out_shape=[jax.ShapeDtypeStruct((2, count, STRIP, BS), f32)] * NCHIP
        + [
            jax.ShapeDtypeStruct((slots, n + (MARK if q == 0 else 0), BS), f32)
            for q, n in enumerate(PARTS)
        ],
        compiler_params=pltpu.CompilerParams(vmem_limit_bytes=58 << 20),
        cost_estimate=pl.CostEstimate(
            flops=12 * count * BS**3, bytes_accessed=12 * count * BS * BS, transcendentals=0
        ),
        name="permute_tiles",
    )(slot, labels, tiles, rows_from[:, None, :], cols_from[:, None, :])
    return list(out[:NCHIP]), list(out[NCHIP:])


def slot_kernel(count, meta, own_ref, other_ref, out_ref, hold, in_sem, sems):
    @pl.when(meta[count] % 2 == 0)
    def _():
        copy = pltpu.make_async_copy(own_ref.at[0], hold, in_sem)
        copy.start()
        copy.wait()

    @pl.when(meta[count] % 2 == 1)
    def _():
        copy = pltpu.make_async_copy(other_ref, hold, in_sem)
        copy.start()
        copy.wait()

    def begin(t, carry):
        pltpu.make_async_copy(hold.at[t], out_ref.at[meta[t]], sems.at[t]).start()
        return carry

    lax.fori_loop(0, count, begin, 0)

    def finish(t, carry):
        pltpu.make_async_copy(hold.at[t], out_ref.at[meta[t]], sems.at[t]).wait()
        return carry

    lax.fori_loop(0, count, finish, 0)


def slot_strips(meta, own, other, slots):
    count = other.shape[0]
    return pl.pallas_call(
        lambda *refs: slot_kernel(count, *refs),
        grid_spec=pltpu.PrefetchScalarGridSpec(
            num_scalar_prefetch=1,
            grid=(1,),
            in_specs=[pl.BlockSpec(memory_space=pl.ANY)] * 2,
            out_specs=pl.BlockSpec(memory_space=pl.ANY),
            scratch_shapes=[
                pltpu.VMEM(other.shape, f32),
                pltpu.SemaphoreType.DMA(()),
                pltpu.SemaphoreType.DMA((count,)),
            ],
        ),
        out_shape=jax.ShapeDtypeStruct((slots, STRIP, BS), f32),
        compiler_params=pltpu.CompilerParams(vmem_limit_bytes=58 << 20),
        cost_estimate=pl.CostEstimate(
            flops=0, bytes_accessed=8 * count * STRIP * BS, transcendentals=0
        ),
        name="slot_strips",
    )(meta, own, other)


def slab_kernel(meta, initial_ref, in_ref, out_ref, ring, sems):
    total = meta[128]
    pieces, width = initial_ref.shape[0], initial_ref.shape[3]

    def copy(g):
        return pltpu.make_async_copy(in_ref.at[meta[g]], ring.at[g % RING], sems.at[g % RING])

    for g in range(RING):

        @pl.when(g < total)
        def _():
            copy(g).start()

    for k in range(pieces):
        out_ref[:, :, k * width : (k + 1) * width] = initial_ref[k]

    @pl.loop(0, total)
    def _(g):
        copy(g).wait()
        spot = meta[64 + g]
        cols = pl.ds(pl.multiple_of((spot % 2) * BS, BS), BS)
        out_ref[spot // 2, :, cols] += ring[g % RING]

        @pl.when(g + RING < total)
        def _():
            copy(g + RING).start()


def slab_strip(meta, initial, incoming):
    pieces, blocks, height, width = initial.shape
    shape = (blocks, height, pieces * width)
    return pl.pallas_call(
        slab_kernel,
        grid_spec=pltpu.PrefetchScalarGridSpec(
            num_scalar_prefetch=1,
            grid=(1,),
            in_specs=[
                pl.BlockSpec(initial.shape, lambda i, meta: (0, 0, 0, 0)),
                pl.BlockSpec(memory_space=pl.ANY),
            ],
            out_specs=pl.BlockSpec(shape, lambda i, meta: (0, 0, 0)),
            scratch_shapes=[
                pltpu.VMEM((RING, height, BS), f32),
                pltpu.SemaphoreType.DMA((RING,)),
            ],
        ),
        out_shape=jax.ShapeDtypeStruct(shape, f32),
        compiler_params=pltpu.CompilerParams(vmem_limit_bytes=32 << 20),
        cost_estimate=pl.CostEstimate(
            flops=0, bytes_accessed=12 * blocks * STRIP * PIV, transcendentals=0
        ),
        name="slab_strip",
    )(meta, initial, incoming)


def halves(x):
    high = x.astype(bf16)
    return high, (x - high.astype(f32)).astype(bf16)


def final_kernel(col_blocks, *refs):
    meta = refs[0]
    slab, first_factor, second_factor = refs[1:4]
    across, incoming = refs[4], refs[5 : 5 + NPART]
    out_ref, a_high, a_low, ring, sems = refs[5 + NPART :]
    b = pl.program_id(0)
    total = meta[138]

    def copies(g):
        return [
            pltpu.make_async_copy(
                incoming[q].at[meta[g], pl.ds(0, PARTS[q])],
                ring.at[g % RING, pl.ds(OFFSETS[q], PARTS[q])],
                sems.at[g % RING, q],
            )
            for q in range(NPART)
        ]

    @pl.when(b == 0)
    def _():
        for g in range(RING):

            @pl.when(g < total)
            def _():
                for c in copies(g):
                    c.start()

        for cb in range(col_blocks):
            high, low = halves(across[:, cb].reshape(BS, PIV).T)
            a_high[:, cb * BS : (cb + 1) * BS] = high
            a_low[:, cb * BS : (cb + 1) * BS] = low

    rows = slab[:, 0].reshape(BS, PIV)
    top = meta[139] == 1
    high, low = halves(jnp.where(jnp.logical_and(top, b < 2), 0.0, rows))
    for cb in range(col_blocks):
        cols = slice(cb * BS, (cb + 1) * BS)
        product = jnp.dot(high, a_low[:, cols], preferred_element_type=f32)
        product = product + jnp.dot(low, a_high[:, cols], preferred_element_type=f32)
        product = product + jnp.dot(high, a_high[:, cols], preferred_element_type=f32)
        out_ref[:, cols] = -product

    @pl.loop(meta[128 + b], meta[129 + b])
    def _(g):
        for c in copies(g):
            c.wait()
        cols = pl.ds(pl.multiple_of(meta[64 + g] * BS, BS), BS)
        out_ref[:, cols] += ring[g % RING]

        @pl.when(g + RING < total)
        def _():
            for c in copies(g + RING):
                c.start()

    @pl.when(meta[140] == 0)
    def _():
        out_ref[:, :BS] = jnp.where(jnp.logical_and(top, b == 0), first_factor[...], rows[:, :BS])
        out_ref[:, BS:PIV] = jnp.where(jnp.logical_and(top, b == 1), second_factor[...], rows[:, BS:])


def final(meta, slab, across, mats, incoming, row_blocks, col_blocks):
    whole = pl.BlockSpec((BS, BS), lambda b, meta: (0, 0))
    return pl.pallas_call(
        lambda *refs: final_kernel(col_blocks, *refs),
        grid_spec=pltpu.PrefetchScalarGridSpec(
            num_scalar_prefetch=1,
            grid=(row_blocks,),
            in_specs=[
                pl.BlockSpec((NSTRIP, 1, STRIP, PIV), lambda b, meta: (0, b, 0, 0)),
            ]
            + [whole] * 2
            + [pl.BlockSpec((NSTRIP, col_blocks, STRIP, PIV), lambda b, meta: (0, 0, 0, 0))]
            + [pl.BlockSpec(memory_space=pl.ANY)] * NPART,
            out_specs=pl.BlockSpec((BS, col_blocks * BS), lambda b, meta: (b, 0)),
            scratch_shapes=[
                pltpu.VMEM((PIV, col_blocks * BS), bf16),
                pltpu.VMEM((PIV, col_blocks * BS), bf16),
                pltpu.VMEM((RING, BS, BS), f32),
                pltpu.SemaphoreType.DMA((RING, NPART)),
            ],
        ),
        out_shape=jax.ShapeDtypeStruct((row_blocks * BS, col_blocks * BS), f32),
        compiler_params=pltpu.CompilerParams(vmem_limit_bytes=48 << 20),
        cost_estimate=pl.CostEstimate(
            flops=6 * row_blocks * col_blocks * BS * BS * PIV,
            bytes_accessed=4 * 2 * row_blocks * col_blocks * BS * BS,
            transcendentals=0,
        ),
        name="place_and_update",
    )(meta, slab, *mats, across, *incoming)


def dot(a, b):
    return jnp.dot(a, b, precision=HIGH)


def inverse(lower):
    size = lower.shape[0]
    eye = jnp.eye(size, dtype=f32)
    scale = jnp.sum(lower * eye, axis=0)
    power = eye - lower / scale[None, :]
    out = eye + power
    for _ in range(6):
        power = dot(power, power)
        out = out + dot(power, out)
    return out / scale[:, None]


def panel(block):
    half = BS // 2
    first = jnp.linalg.cholesky(lower_sym(block[:half, :half]))
    first_inv = inverse(first)
    below = dot(block[half:, :half], first_inv.T)
    second = jnp.linalg.cholesky(lower_sym(block[half:, half:] - dot(below, below.T)))
    second_inv = inverse(second)
    across = -dot(second_inv, dot(below, first_inv))
    zero = jnp.zeros((half, half), f32)
    factor = jnp.block([[first, zero], [below, second]])
    return factor, jnp.block([[first_inv.T, across.T], [zero, second_inv.T]])


def exchange(x, my_col, n_col):
    chip, core = my_col // 2, my_col % 2
    chips = n_col // 2
    pairs = x.reshape((chips, 2) + x.shape[1:])
    got = []
    for step in range(chips):
        pair = lax.dynamic_index_in_dim(pairs, (chip + step) % chips, 0, keepdims=False)
        if step:
            pair = lax.ppermute(pair, "col", [(c, (c + 2 * step) % n_col) for c in range(n_col)])
        got.append(pair)

    def from_chips(wanted):
        ordered_by = [lax.dynamic_index_in_dim(p, wanted, 0, keepdims=False) for p in got]
        return jnp.stack(ordered_by)

    mine = from_chips(core)
    other = lax.ppermute(from_chips(1 - core), "col", [(c, c ^ 1) for c in range(n_col)])
    both = jnp.stack([jnp.where(core == 0, mine, other), jnp.where(core == 0, other, mine)], 1)
    placed = [
        lax.dynamic_index_in_dim(both, (chip + chips - k) % chips, 0, keepdims=False)
        for k in range(chips)
    ]
    return jnp.stack(placed).reshape(x.shape)


def ordered(key, valid, span):
    count = key.shape[0]
    key = jnp.where(valid, key, span)
    index = jnp.arange(count, dtype=i32)
    ahead = (key[None, :] < key[:, None]) | (
        (key[None, :] == key[:, None]) & (index[None, :] < index[:, None])
    )
    rank = jnp.sum(ahead.astype(i32), axis=1)
    chosen = rank[None, :] == index[:, None]
    order = jnp.sum(jnp.where(chosen, index[None, :], 0), axis=1)
    return order, jnp.sum(jnp.where(chosen, key[None, :], 0), axis=1), key


def body(tiles, dest, block_row, block_col, rows_from, cols_from, initial, pattern):
    n_front = lax.axis_size("front")
    n_row = lax.axis_size("row")
    n_col = lax.axis_size("col")
    my_row = lax.axis_index("row")
    my_col = lax.axis_index("col")
    row_blocks = ORDER // n_row // BS
    col_blocks = ORDER // n_col // BS
    lead = PIV // BS
    slots = n_front * n_row * CAP
    target = dest[:, 0]
    owner_row = target % n_row
    local_row = jnp.where(owner_row == 0, lead + block_row % (row_blocks - lead), block_row)
    block_id = local_row * col_blocks + block_col
    same = (target[:, None] == target[None, :]).astype(i32)
    slot = target * CAP + jnp.sum(jnp.tril(same, -1), axis=1)
    choose = jnp.arange(slots, dtype=i32)[:, None] == slot[None, :]
    labels = jnp.where(
        jnp.any(choose, axis=1), jnp.sum(jnp.where(choose, block_id[None, :], 0), axis=1), -1
    )
    pivot = initial[0, :PIV]
    sent = [lax.ppermute(pivot, "row", [(0, to)]) for to in range(1, n_row)]
    pivot = jnp.where(my_row == 0, pivot, sent[0] + sent[1] + sent[2])
    row = jnp.zeros((1, pivot.shape[1]), f32).at[0, : slot.shape[0]].set(slot.astype(f32))
    near = lax.all_gather(
        jnp.concatenate([pivot, jnp.broadcast_to(row, (8, row.shape[1]))]), "col", axis=0
    )
    corner = near[:, :PIV].transpose(1, 0, 2).reshape(PIV, PIV)
    slot_meta = jnp.append(near[0, PIV, : slot.shape[0]].astype(i32), my_col)

    def send(part):
        return lax.all_to_all(part, ("front", "row"), split_axis=0, concat_axis=0, tiled=True)

    strips, parts = permute(slot, labels, tiles, rows_from, cols_from, slots)
    incoming = [send(parts[0])]
    got = [lax.ppermute(strips[k], "col", [(0, 2 * k)]) for k in range(1, NCHIP)]
    own = jnp.where(my_col == 0, strips[0], got[0] + got[1] + got[2])
    other = lax.ppermute(own[1], "col", [(2 * k, 2 * k + 1) for k in range(NCHIP)])
    pivot_columns, strips[1] = lax.optimization_barrier((initial[0], strips[1]))
    pivot_columns = pivot_columns.reshape(row_blocks, NSTRIP, STRIP, -1).transpose(1, 0, 2, 3)
    pivot_columns = exchange(pivot_columns, my_col, n_col)

    first, first_inv = panel(corner[:BS, :BS])
    below = dot(corner[BS:, :BS], first_inv)
    below = jnp.where(pattern[0, 0, 1] == 1, below, jnp.zeros_like(below))
    rest = corner[BS:, BS:] - dot(below, below.T)
    other, rest = lax.optimization_barrier((other, rest))
    slotted = slot_strips(slot_meta, own, other, slots)
    slotted, rest, incoming[0] = lax.optimization_barrier((slotted, rest, incoming[0]))
    names = incoming[0][:, PARTS[0], 0]
    lent = jnp.broadcast_to(names, (8, slots))
    got = [lax.ppermute(lent, "col", [(0, 2 * k)]) for k in range(1, NCHIP)]
    first_names = jnp.where(my_col == 0, lent, got[0] + got[1] + got[2])
    got = lax.ppermute(first_names, "col", [(2 * k, 2 * k + 1) for k in range(NCHIP)])
    first_names = jnp.where(my_col % 2 == 0, first_names, got)[0].astype(i32)
    names = names.astype(i32)

    valid = names >= 0
    order, sorted_id, key = ordered(names, valid, row_blocks * col_blocks)
    bounds = jnp.arange(row_blocks + 1, dtype=i32)[:, None] * col_blocks
    starts = jnp.sum((key[None, :] < bounds).astype(i32), axis=1)
    in_slab = (first_names >= 0) & (first_names % col_blocks < lead)
    slab_key = (first_names // col_blocks) * lead + first_names % col_blocks
    slab_order, slab_id, _ = ordered(slab_key, in_slab, row_blocks * lead)
    slab_meta = jnp.concatenate(
        [slab_order, slab_id, jnp.sum(in_slab.astype(i32))[None], my_col[None]]
    )

    meta = jnp.concatenate(
        [order, sorted_id % col_blocks, starts, (my_row == 0).astype(i32)[None], my_col[None]]
    )

    strip = slab_strip(slab_meta, pivot_columns, send(slotted))
    second, second_inv = panel(rest)
    cross = dot(below.T, second_inv)

    blocks = my_row * row_blocks + jnp.arange(row_blocks, dtype=i32)
    flags = lax.dynamic_slice_in_dim(pattern[0], my_row * row_blocks, row_blocks, 1)
    keep = (flags == 1) & (blocks[None, :] > jnp.arange(2, dtype=i32)[:, None])
    keep = jnp.repeat(keep, STRIP, axis=1)[:, :, None]
    strip = strip.reshape(row_blocks * STRIP, PIV)
    one = dot(strip[:, :BS], first_inv)
    one = jnp.where(keep[0], one, jnp.zeros_like(one))
    two = dot(strip[:, BS:], second_inv) - dot(one, cross)
    two = jnp.where(keep[1], two, jnp.zeros_like(two))
    solved = jnp.concatenate([one, two], axis=1).reshape(row_blocks, STRIP, PIV)

    part, solved = lax.optimization_barrier((parts[1], solved))
    incoming.append(send(part))
    rows = lax.all_gather(solved, "row", axis=0)
    part, rows, solved = lax.optimization_barrier((parts[2], rows, solved))
    incoming.append(send(part))
    slab = lax.all_gather(solved, "col", axis=0)
    across = exchange(rows.reshape(n_col, col_blocks, STRIP, PIV), my_col, n_col)
    return final(meta, slab, across, (first, second), incoming, row_blocks, col_blocks)[None]


def solution(mesh):
    placed = (
        P(("front", "row", "col"), None, None),
        P(("front", "row", "col"), None),
        P(("front", "row", "col")),
        P(("front", "row", "col")),
        P(("front", "row", "col"), None),
        P(("front", "row", "col"), None),
        P("front", "row", "col"),
        P("front", None, None),
    )
    return jax.shard_map(
        body, mesh=mesh, in_specs=placed, out_specs=P("front", "row", "col"), check_vma=False
    )
```

```python
import jax
import jax.numpy as jnp
from jax import lax
from jax.experimental import pallas as pl
from jax.experimental.pallas import tpu as pltpu
from jax.sharding import PartitionSpec as P

ORDER = 10240
BS = 256
CAP = 4
PIV = 512
STRIP = 32
NSTRIP = BS // STRIP
NCHIP = NSTRIP // 2
MARK = 8
GROUP = 8
RING = 8

HIGH = lax.Precision.HIGHEST
f32, bf16, i32 = jnp.float32, jnp.bfloat16, jnp.int32


def lower_sym(block):
    return jnp.tril(block) + jnp.tril(block, -1).T


def permute_kernel(slot_ref, label_ref, tile_ref, rows_ref, cols_ref, out_ref, *refs):
    hold, mark, mark_sem, sems = refs
    step = pl.program_id(0)

    def marks():
        rows = out_ref.at[:, pl.ds(BS, MARK)]
        return pltpu.make_async_copy(mark, rows, mark_sem)

    def copy(t):
        rows = out_ref.at[slot_ref[t], pl.ds(0, BS)]
        return pltpu.make_async_copy(hold.at[t], rows, sems.at[t])

    @pl.when(step == 0)
    def _():
        def fill(s, carry):
            mark[s] = jnp.full(mark.shape[1:], label_ref[s].astype(f32))
            return carry

        lax.fori_loop(0, mark.shape[0], fill, 0)
        marks().start()

    half = BS // 2
    lane = lax.broadcasted_iota(i32, (BS, half), 1)
    place = lax.broadcasted_iota(i32, (BS, BS), 0)

    def move(g, carry):
        t = step * GROUP + g
        tile = tile_ref[g]
        high = tile.astype(bf16)
        rest = tile - high.astype(f32)
        mid = rest.astype(bf16)
        low = (rest - mid.astype(f32)).astype(bf16)
        parts = jnp.concatenate([high, mid, low], axis=1)
        wanted = jnp.transpose(jnp.broadcast_to(rows_ref[g], (half, BS)))
        pick_rows = jnp.concatenate(
            [jnp.where(wanted == lane + k * half, 1.0, 0.0) for k in range(2)], axis=1
        ).astype(bf16)
        pick_cols = jnp.where(place == cols_ref[g], 1.0, 0.0).astype(bf16)
        moved = jnp.dot(pick_rows, parts, preferred_element_type=f32).astype(bf16)
        out = jnp.dot(moved[:, :BS], pick_cols, preferred_element_type=f32)
        out = out + jnp.dot(moved[:, BS : 2 * BS], pick_cols, preferred_element_type=f32)
        out = out + jnp.dot(moved[:, 2 * BS :], pick_cols, preferred_element_type=f32)
        hold[t] = out
        copy(t).start()
        return carry

    lax.fori_loop(0, GROUP, move, 0, unroll=2)

    @pl.when(step == pl.num_programs(0) - 1)
    def _():
        def finish(t, carry):
            copy(t).wait()
            return carry

        lax.fori_loop(0, hold.shape[0], finish, 0)
        marks().wait()


def permute(slot, labels, tiles, rows_from, cols_from, slots):
    count = tiles.shape[0]
    return pl.pallas_call(
        permute_kernel,
        grid_spec=pltpu.PrefetchScalarGridSpec(
            num_scalar_prefetch=2,
            grid=(count // GROUP,),
            in_specs=[
                pl.BlockSpec((GROUP, BS, BS), lambda t, slot, labels: (t, 0, 0)),
                pl.BlockSpec((GROUP, 1, BS), lambda t, slot, labels: (t, 0, 0)),
                pl.BlockSpec((GROUP, 1, BS), lambda t, slot, labels: (t, 0, 0)),
            ],
            out_specs=pl.BlockSpec(memory_space=pl.ANY),
            scratch_shapes=[
                pltpu.VMEM((count, BS, BS), f32),
                pltpu.VMEM((slots, MARK, BS), f32),
                pltpu.SemaphoreType.DMA(()),
                pltpu.SemaphoreType.DMA((count,)),
            ],
        ),
        out_shape=jax.ShapeDtypeStruct((slots, BS + MARK, BS), f32),
        compiler_params=pltpu.CompilerParams(vmem_limit_bytes=58 << 20),
        cost_estimate=pl.CostEstimate(
            flops=12 * count * BS**3, bytes_accessed=12 * count * BS * BS, transcendentals=0
        ),
        name="permute_tiles",
    )(slot, labels, tiles, rows_from[:, None, :], cols_from[:, None, :])


def slab_kernel(meta, wide_ref, in_ref, *refs):
    chip_refs, (hold, ring, hold_sems, sems) = refs[:NCHIP], refs[NCHIP:]
    total = meta[128]
    pieces, rows, width = hold.shape
    blocks = rows // BS

    def copy(g):
        source = in_ref.at[meta[g], pl.ds(0, BS)]
        return pltpu.make_async_copy(source, ring.at[g % RING], sems.at[g % RING])

    def initial(k):
        return pltpu.make_async_copy(wide_ref.at[k], hold.at[k], hold_sems.at[k])

    @pl.when(meta[129] == 0)
    def _():
        for k in range(pieces):
            initial(k).start()
        for g in range(RING):

            @pl.when(g < total)
            def _():
                copy(g).start()

        for k in range(pieces):
            initial(k).wait()
            for b in range(blocks):
                for strip in range(NSTRIP):
                    at = b * BS + strip * STRIP
                    chip_refs[strip // 2][strip % 2, b, :, k * width : (k + 1) * width] = hold[
                        k, at : at + STRIP
                    ]

        @pl.loop(0, total)
        def _(g):
            copy(g).wait()
            spot = meta[64 + g]
            cols = pl.ds(pl.multiple_of((spot % 2) * BS, BS), BS)
            for strip in range(NSTRIP):
                part = ring[g % RING, strip * STRIP : (strip + 1) * STRIP]
                chip_refs[strip // 2][strip % 2, spot // 2, :, cols] += part

            @pl.when(g + RING < total)
            def _():
                copy(g + RING).start()


def slab_strips(meta, wide, incoming):
    pieces, rows, width = wide.shape
    shape = (2, rows // BS, STRIP, pieces * width)
    return pl.pallas_call(
        slab_kernel,
        grid_spec=pltpu.PrefetchScalarGridSpec(
            num_scalar_prefetch=1,
            grid=(1,),
            in_specs=[pl.BlockSpec(memory_space=pl.ANY)] * 2,
            out_specs=[pl.BlockSpec(shape, lambda i, meta: (0, 0, 0, 0))] * NCHIP,
            scratch_shapes=[
                pltpu.VMEM((pieces, rows, width), f32),
                pltpu.VMEM((RING, BS, BS), f32),
                pltpu.SemaphoreType.DMA((pieces,)),
                pltpu.SemaphoreType.DMA((RING,)),
            ],
        ),
        out_shape=[jax.ShapeDtypeStruct(shape, f32)] * NCHIP,
        compiler_params=pltpu.CompilerParams(vmem_limit_bytes=48 << 20),
        cost_estimate=pl.CostEstimate(
            flops=0, bytes_accessed=12 * rows * PIV, transcendentals=0
        ),
        name="slab_strips",
    )(meta, wide, incoming)


def halves(x):
    high = x.astype(bf16)
    return high, (x - high.astype(f32)).astype(bf16)


def final_kernel(col_blocks, *refs):
    meta = refs[0]
    slab, first_inv, second_inv, cross, first_factor, second_factor = refs[1:7]
    across, incoming, out_ref, a_high, a_low, ring, sems = refs[7:]
    b = pl.program_id(0)
    total = meta[138]

    def copy(g):
        source = incoming.at[meta[g], pl.ds(0, BS)]
        return pltpu.make_async_copy(source, ring.at[g % RING], sems.at[g % RING])

    def solve(block, keep_first, keep_second):
        one = jnp.dot(block[:, :BS], first_inv[...], precision=HIGH, preferred_element_type=f32)
        one = jnp.where(keep_first == 1, one, 0.0)
        two = jnp.dot(block[:, BS:], second_inv[...], precision=HIGH, preferred_element_type=f32)
        two = two - jnp.dot(one, cross[...], precision=HIGH, preferred_element_type=f32)
        return one, jnp.where(keep_second == 1, two, 0.0)

    @pl.when(b == 0)
    def _():
        for g in range(RING):

            @pl.when(g < total)
            def _():
                copy(g).start()

        for cb in range(col_blocks):
            one, two = solve(across[:, cb].reshape(BS, PIV), meta[159 + cb], meta[164 + cb])
            high, low = halves(jnp.concatenate([one, two], axis=1).T)
            a_high[:, cb * BS : (cb + 1) * BS] = high
            a_low[:, cb * BS : (cb + 1) * BS] = low

    one, two = solve(slab[:, 0].reshape(BS, PIV), meta[139 + b], meta[149 + b])
    top = meta[169] == 1
    high, low = halves(
        jnp.where(jnp.logical_and(top, b < 2), 0.0, jnp.concatenate([one, two], axis=1))
    )
    for cb in range(col_blocks):
        cols = slice(cb * BS, (cb + 1) * BS)
        product = jnp.dot(high, a_low[:, cols], preferred_element_type=f32)
        product = product + jnp.dot(low, a_high[:, cols], preferred_element_type=f32)
        product = product + jnp.dot(high, a_high[:, cols], preferred_element_type=f32)
        out_ref[:, cols] = -product

    @pl.loop(meta[128 + b], meta[129 + b])
    def _(g):
        copy(g).wait()
        cols = pl.ds(pl.multiple_of(meta[64 + g] * BS, BS), BS)
        out_ref[:, cols] += ring[g % RING]

        @pl.when(g + RING < total)
        def _():
            copy(g + RING).start()

    @pl.when(meta[170] == 1)
    def _():
        out_ref[:, :BS] = jnp.where(jnp.logical_and(top, b == 0), first_factor[...], one)
        out_ref[:, BS:PIV] = jnp.where(jnp.logical_and(top, b == 1), second_factor[...], two)


def final(meta, slab, across, mats, incoming, row_blocks, col_blocks):
    whole = pl.BlockSpec((BS, BS), lambda b, meta: (0, 0))
    return pl.pallas_call(
        lambda *refs: final_kernel(col_blocks, *refs),
        grid_spec=pltpu.PrefetchScalarGridSpec(
            num_scalar_prefetch=1,
            grid=(row_blocks,),
            in_specs=[
                pl.BlockSpec((NSTRIP, 1, STRIP, PIV), lambda b, meta: (0, b, 0, 0)),
            ]
            + [whole] * 5
            + [
                pl.BlockSpec((NSTRIP, col_blocks, STRIP, PIV), lambda b, meta: (0, 0, 0, 0)),
                pl.BlockSpec(memory_space=pl.ANY),
            ],
            out_specs=pl.BlockSpec((BS, col_blocks * BS), lambda b, meta: (b, 0)),
            scratch_shapes=[
                pltpu.VMEM((PIV, col_blocks * BS), bf16),
                pltpu.VMEM((PIV, col_blocks * BS), bf16),
                pltpu.VMEM((RING, BS, BS), f32),
                pltpu.SemaphoreType.DMA((RING,)),
            ],
        ),
        out_shape=jax.ShapeDtypeStruct((row_blocks * BS, col_blocks * BS), f32),
        compiler_params=pltpu.CompilerParams(vmem_limit_bytes=48 << 20),
        cost_estimate=pl.CostEstimate(
            flops=6 * row_blocks * col_blocks * BS * BS * PIV,
            bytes_accessed=4 * 2 * row_blocks * col_blocks * BS * BS,
            transcendentals=0,
        ),
        name="place_and_update",
    )(meta, slab, *mats, across, incoming)


def dot(a, b):
    return jnp.dot(a, b, precision=HIGH)


def inverse(lower):
    size = lower.shape[0]
    eye = jnp.eye(size, dtype=f32)
    scale = jnp.sum(lower * eye, axis=0)
    power = eye - lower / scale[None, :]
    out = eye + power
    for _ in range(6):
        power = dot(power, power)
        out = out + dot(power, out)
    return out / scale[:, None]


def panel(block):
    half = BS // 2
    first = jnp.linalg.cholesky(lower_sym(block[:half, :half]))
    first_inv = inverse(first)
    below = dot(block[half:, :half], first_inv.T)
    second = jnp.linalg.cholesky(lower_sym(block[half:, half:] - dot(below, below.T)))
    second_inv = inverse(second)
    across = -dot(second_inv, dot(below, first_inv))
    zero = jnp.zeros((half, half), f32)
    factor = jnp.block([[first, zero], [below, second]])
    return factor, jnp.block([[first_inv.T, across.T], [zero, second_inv.T]])


def exchange(pairs, base, my_col, n_col):
    chip, core = my_col // 2, my_col % 2
    chips = n_col // 2
    got = []
    for step in range(chips):
        pair = lax.dynamic_index_in_dim(pairs, (chip + step - base) % chips, 0, keepdims=False)
        if step:
            pair = lax.ppermute(pair, "col", [(c, (c + 2 * step) % n_col) for c in range(n_col)])
        got.append(pair)

    def from_chips(wanted):
        ordered_by = [lax.dynamic_index_in_dim(p, wanted, 0, keepdims=False) for p in got]
        return jnp.stack(ordered_by)

    mine = from_chips(core)
    other = lax.ppermute(from_chips(1 - core), "col", [(c, c ^ 1) for c in range(n_col)])
    both = jnp.stack([jnp.where(core == 0, mine, other), jnp.where(core == 0, other, mine)], 1)
    placed = [
        lax.dynamic_index_in_dim(both, (chip + chips - k) % chips, 0, keepdims=False)
        for k in range(chips)
    ]
    return jnp.stack(placed).reshape((n_col,) + pairs.shape[2:])


def ordered(key, valid, span):
    count = key.shape[0]
    key = jnp.where(valid, key, span)
    index = jnp.arange(count, dtype=i32)
    ahead = (key[None, :] < key[:, None]) | (
        (key[None, :] == key[:, None]) & (index[None, :] < index[:, None])
    )
    rank = jnp.sum(ahead.astype(i32), axis=1)
    chosen = rank[None, :] == index[:, None]
    order = jnp.sum(jnp.where(chosen, index[None, :], 0), axis=1)
    return order, jnp.sum(jnp.where(chosen, key[None, :], 0), axis=1), key


def body(tiles, dest, block_row, block_col, rows_from, cols_from, initial, pattern):
    n_front = lax.axis_size("front")
    n_row = lax.axis_size("row")
    n_col = lax.axis_size("col")
    my_row = lax.axis_index("row")
    my_col = lax.axis_index("col")
    row_blocks = ORDER // n_row // BS
    col_blocks = ORDER // n_col // BS
    lead = PIV // BS
    slots = n_front * n_row * CAP
    target = dest[:, 0]
    owner_row = target % n_row
    local_row = jnp.where(owner_row == 0, lead + block_row % (row_blocks - lead), block_row)
    block_id = local_row * col_blocks + block_col
    same = (target[:, None] == target[None, :]).astype(i32)
    slot = target * CAP + jnp.sum(jnp.tril(same, -1), axis=1)
    choose = jnp.arange(slots, dtype=i32)[:, None] == slot[None, :]
    labels = jnp.where(
        jnp.any(choose, axis=1), jnp.sum(jnp.where(choose, block_id[None, :], 0), axis=1), -1
    )
    pivot = lax.all_gather(initial[0, :PIV], "row", axis=0)[0]
    outgoing = permute(slot, labels, tiles, rows_from, cols_from, slots)
    outgoing, pivot = lax.optimization_barrier((outgoing, pivot))
    near = lax.all_gather(pivot, "col", axis=0)
    wide = lax.all_gather(initial[0], "col", axis=0)
    incoming = lax.all_to_all(outgoing, ("front", "row"), split_axis=0, concat_axis=0, tiled=True)
    incoming, near, wide, pattern = lax.optimization_barrier((incoming, near, wide, pattern))

    names = incoming[:, BS, 0].astype(i32)
    valid = names >= 0
    in_slab = valid & (names % col_blocks < lead)
    slab_key = (names // col_blocks) * lead + names % col_blocks
    slab_order, slab_id, _ = ordered(slab_key, in_slab, row_blocks * lead)
    slab_meta = jnp.concatenate(
        [slab_order, slab_id, jnp.sum(in_slab.astype(i32))[None], my_col[None]]
    )
    strips = list(slab_strips(slab_meta, wide, incoming))
    strips[0], near = lax.optimization_barrier((strips[0], near))
    got = [lax.ppermute(strips[k], "col", [(0, 2 * k)]) for k in range(1, NCHIP)]
    own = jnp.where(my_col == 0, strips[0], got[0] + got[1] + got[2])
    other = lax.ppermute(own[1], "col", [(2 * k, 2 * k + 1) for k in range(NCHIP)])
    strip = jnp.where(my_col % 2 == 0, own[0], other)
    corner = near.transpose(1, 0, 2).reshape(PIV, PIV)
    first, first_inv = panel(corner[:BS, :BS])
    below = dot(corner[BS:, :BS], first_inv)
    below = jnp.where(pattern[0, 0, 1] == 1, below, jnp.zeros_like(below))
    rest = corner[BS:, BS:] - dot(below, below.T)
    strip, rest = lax.optimization_barrier((strip, rest))
    second, second_inv = panel(rest)
    mats = (first_inv, second_inv, dot(below.T, second_inv), first, second)
    slab = lax.all_gather(strip, "col", axis=0)

    def shift(x, by):
        return lax.ppermute(x, "row", [(r, (r + by) % n_row) for r in range(n_row)])

    before, after = shift(strip, 1), shift(strip, -1)
    far = jnp.concatenate([shift(before[:col_blocks], 1), shift(after[col_blocks:], -1)])
    rows = jnp.stack([strip, after, far, before])
    rows = rows.reshape(n_row, 2, col_blocks, STRIP, PIV)
    across = exchange(rows, my_row, my_col, n_col)

    order, sorted_id, key = ordered(names, valid, row_blocks * col_blocks)
    bounds = jnp.arange(row_blocks + 1, dtype=i32)[:, None] * col_blocks
    starts = jnp.sum((key[None, :] < bounds).astype(i32), axis=1)

    def kept(first_block, count):
        blocks = first_block + jnp.arange(count, dtype=i32)
        flags = lax.dynamic_slice_in_dim(pattern[0], first_block, count, axis=1)
        ahead = blocks[None, :] > jnp.arange(2, dtype=i32)[:, None]
        return jnp.where(ahead, flags, 0).reshape(-1)

    meta = jnp.concatenate(
        [
            order,
            sorted_id % col_blocks,
            starts,
            kept(my_row * row_blocks, row_blocks),
            kept(my_col * col_blocks, col_blocks),
            (my_row == 0).astype(i32)[None],
            (my_col == 0).astype(i32)[None],
        ]
    )
    return final(meta, slab, across, mats, incoming, row_blocks, col_blocks)[None]


def solution(mesh):
    placed = (
        P(("front", "row", "col"), None, None),
        P(("front", "row", "col"), None),
        P(("front", "row", "col")),
        P(("front", "row", "col")),
        P(("front", "row", "col"), None),
        P(("front", "row", "col"), None),
        P("front", "row", "col"),
        P("front", None, None),
    )
    return jax.shard_map(
        body, mesh=mesh, in_specs=placed, out_specs=P("front", "row", "col"), check_vma=False
    )
```

```python
import jax
import jax.numpy as jnp
from jax import lax
from jax.experimental import pallas as pl
from jax.experimental.pallas import tpu as pltpu
from jax.sharding import PartitionSpec as P

ORDER = 10240
BS = 256
CAP = 4
PIV = 512
STRIP = 32
NSTRIP = BS // STRIP
NCHIP = NSTRIP // 2
MARK = 8
PARTS = (64, 96, 96)
OFFSETS = tuple(sum(PARTS[:q]) for q in range(len(PARTS)))
NPART = len(PARTS)
GROUP = 8
RING = 8

HIGH = lax.Precision.HIGHEST
f32, bf16, i32 = jnp.float32, jnp.bfloat16, jnp.int32


def lower_sym(block):
    return jnp.tril(block) + jnp.tril(block, -1).T


def permute_kernel(slot_ref, label_ref, tile_ref, rows_ref, cols_ref, *refs):
    chip_refs, part_refs = refs[:NCHIP], refs[NCHIP : NCHIP + NPART]
    hold, mark, mark_sem, strip_sems, part_sems = refs[NCHIP + NPART :]
    step = pl.program_id(0)

    def marks():
        rows = part_refs[0].at[:, pl.ds(PARTS[0], MARK)]
        return pltpu.make_async_copy(mark, rows, mark_sem)

    @pl.when(step == 0)
    def _():
        def fill(s, carry):
            mark[s] = jnp.full(mark.shape[1:], label_ref[s].astype(f32))
            return carry

        lax.fori_loop(0, mark.shape[0], fill, 0)
        marks().start()

    half = BS // 2
    lane = lax.broadcasted_iota(i32, (BS, half), 1)
    place = lax.broadcasted_iota(i32, (BS, BS), 0)

    def move(g, carry):
        t = step * GROUP + g
        tile = tile_ref[g]
        high = tile.astype(bf16)
        rest = tile - high.astype(f32)
        mid = rest.astype(bf16)
        low = (rest - mid.astype(f32)).astype(bf16)
        parts = jnp.concatenate([high, mid, low], axis=1)
        wanted = jnp.transpose(jnp.broadcast_to(rows_ref[g], (half, BS)))
        pick_rows = jnp.concatenate(
            [jnp.where(wanted == lane + k * half, 1.0, 0.0) for k in range(2)], axis=1
        ).astype(bf16)
        pick_cols = jnp.where(place == cols_ref[g], 1.0, 0.0).astype(bf16)
        moved = jnp.dot(pick_rows, parts, preferred_element_type=f32).astype(bf16)
        out = jnp.dot(moved[:, :BS], pick_cols, preferred_element_type=f32)
        out = out + jnp.dot(moved[:, BS : 2 * BS], pick_cols, preferred_element_type=f32)
        out = out + jnp.dot(moved[:, 2 * BS :], pick_cols, preferred_element_type=f32)
        hold[t] = out
        for k in range(NSTRIP):
            pltpu.make_async_copy(
                hold.at[t, pl.ds(k * STRIP, STRIP)], chip_refs[k // 2].at[k % 2, t], strip_sems.at[t]
            ).start()
        for q in range(NPART):
            pltpu.make_async_copy(
                hold.at[t, pl.ds(OFFSETS[q], PARTS[q])],
                part_refs[q].at[slot_ref[t], pl.ds(0, PARTS[q])],
                part_sems.at[t],
            ).start()
        return carry

    lax.fori_loop(0, GROUP, move, 0, unroll=2)

    @pl.when(step == pl.num_programs(0) - 1)
    def _():
        def finish(t, carry):
            pltpu.make_async_copy(hold.at[t], hold.at[t], strip_sems.at[t]).wait()
            pltpu.make_async_copy(hold.at[t], hold.at[t], part_sems.at[t]).wait()
            return carry

        lax.fori_loop(0, hold.shape[0], finish, 0)
        marks().wait()


def permute(slot, labels, tiles, rows_from, cols_from, slots):
    count = tiles.shape[0]
    out = pl.pallas_call(
        permute_kernel,
        grid_spec=pltpu.PrefetchScalarGridSpec(
            num_scalar_prefetch=2,
            grid=(count // GROUP,),
            in_specs=[
                pl.BlockSpec((GROUP, BS, BS), lambda t, slot, labels: (t, 0, 0)),
                pl.BlockSpec((GROUP, 1, BS), lambda t, slot, labels: (t, 0, 0)),
                pl.BlockSpec((GROUP, 1, BS), lambda t, slot, labels: (t, 0, 0)),
            ],
            out_specs=[pl.BlockSpec(memory_space=pl.ANY)] * (NCHIP + NPART),
            scratch_shapes=[
                pltpu.VMEM((count, BS, BS), f32),
                pltpu.VMEM((slots, MARK, BS), f32),
                pltpu.SemaphoreType.DMA(()),
                pltpu.SemaphoreType.DMA((count,)),
                pltpu.SemaphoreType.DMA((count,)),
            ],
        ),
        out_shape=[jax.ShapeDtypeStruct((2, count, STRIP, BS), f32)] * NCHIP
        + [
            jax.ShapeDtypeStruct((slots, n + (MARK if q == 0 else 0), BS), f32)
            for q, n in enumerate(PARTS)
        ],
        compiler_params=pltpu.CompilerParams(vmem_limit_bytes=58 << 20),
        cost_estimate=pl.CostEstimate(
            flops=12 * count * BS**3, bytes_accessed=12 * count * BS * BS, transcendentals=0
        ),
        name="permute_tiles",
    )(slot, labels, tiles, rows_from[:, None, :], cols_from[:, None, :])
    return list(out[:NCHIP]), list(out[NCHIP:])


def slot_kernel(count, meta, own_ref, other_ref, out_ref, hold, in_sem, sems):
    @pl.when(meta[count] % 2 == 0)
    def _():
        copy = pltpu.make_async_copy(own_ref.at[0], hold, in_sem)
        copy.start()
        copy.wait()

    @pl.when(meta[count] % 2 == 1)
    def _():
        copy = pltpu.make_async_copy(other_ref, hold, in_sem)
        copy.start()
        copy.wait()

    def begin(t, carry):
        pltpu.make_async_copy(hold.at[t], out_ref.at[meta[t]], sems.at[t]).start()
        return carry

    lax.fori_loop(0, count, begin, 0)

    def finish(t, carry):
        pltpu.make_async_copy(hold.at[t], out_ref.at[meta[t]], sems.at[t]).wait()
        return carry

    lax.fori_loop(0, count, finish, 0)


def slot_strips(meta, own, other, slots):
    count = other.shape[0]
    return pl.pallas_call(
        lambda *refs: slot_kernel(count, *refs),
        grid_spec=pltpu.PrefetchScalarGridSpec(
            num_scalar_prefetch=1,
            grid=(1,),
            in_specs=[pl.BlockSpec(memory_space=pl.ANY)] * 2,
            out_specs=pl.BlockSpec(memory_space=pl.ANY),
            scratch_shapes=[
                pltpu.VMEM(other.shape, f32),
                pltpu.SemaphoreType.DMA(()),
                pltpu.SemaphoreType.DMA((count,)),
            ],
        ),
        out_shape=jax.ShapeDtypeStruct((slots, STRIP, BS), f32),
        compiler_params=pltpu.CompilerParams(vmem_limit_bytes=58 << 20),
        cost_estimate=pl.CostEstimate(
            flops=0, bytes_accessed=8 * count * STRIP * BS, transcendentals=0
        ),
        name="slot_strips",
    )(meta, own, other)


def slab_kernel(meta, initial_ref, in_ref, out_ref, ring, sems):
    total = meta[128]
    pieces, width = initial_ref.shape[0], initial_ref.shape[3]

    def copy(g):
        return pltpu.make_async_copy(in_ref.at[meta[g]], ring.at[g % RING], sems.at[g % RING])

    for g in range(RING):

        @pl.when(g < total)
        def _():
            copy(g).start()

    for k in range(pieces):
        out_ref[:, :, k * width : (k + 1) * width] = initial_ref[k]

    @pl.loop(0, total)
    def _(g):
        copy(g).wait()
        spot = meta[64 + g]
        cols = pl.ds(pl.multiple_of((spot % 2) * BS, BS), BS)
        out_ref[spot // 2, :, cols] += ring[g % RING]

        @pl.when(g + RING < total)
        def _():
            copy(g + RING).start()


def slab_strip(meta, initial, incoming):
    pieces, blocks, height, width = initial.shape
    shape = (blocks, height, pieces * width)
    return pl.pallas_call(
        slab_kernel,
        grid_spec=pltpu.PrefetchScalarGridSpec(
            num_scalar_prefetch=1,
            grid=(1,),
            in_specs=[
                pl.BlockSpec(initial.shape, lambda i, meta: (0, 0, 0, 0)),
                pl.BlockSpec(memory_space=pl.ANY),
            ],
            out_specs=pl.BlockSpec(shape, lambda i, meta: (0, 0, 0)),
            scratch_shapes=[
                pltpu.VMEM((RING, height, BS), f32),
                pltpu.SemaphoreType.DMA((RING,)),
            ],
        ),
        out_shape=jax.ShapeDtypeStruct(shape, f32),
        compiler_params=pltpu.CompilerParams(vmem_limit_bytes=32 << 20),
        cost_estimate=pl.CostEstimate(
            flops=0, bytes_accessed=12 * blocks * STRIP * PIV, transcendentals=0
        ),
        name="slab_strip",
    )(meta, initial, incoming)


def halves(x):
    high = x.astype(bf16)
    return high, (x - high.astype(f32)).astype(bf16)


def final_kernel(col_blocks, *refs):
    meta = refs[0]
    slab, first_factor, second_factor = refs[1:4]
    across, incoming = refs[4], refs[5 : 5 + NPART]
    out_ref, a_high, a_low, ring, sems = refs[5 + NPART :]
    b = pl.program_id(0)
    total = meta[138]

    def copies(g):
        return [
            pltpu.make_async_copy(
                incoming[q].at[meta[g], pl.ds(0, PARTS[q])],
                ring.at[g % RING, pl.ds(OFFSETS[q], PARTS[q])],
                sems.at[g % RING, q],
            )
            for q in range(NPART)
        ]

    @pl.when(b == 0)
    def _():
        for g in range(RING):

            @pl.when(g < total)
            def _():
                for c in copies(g):
                    c.start()

        for cb in range(col_blocks):
            high, low = halves(across[:, cb].reshape(BS, PIV).T)
            a_high[:, cb * BS : (cb + 1) * BS] = high
            a_low[:, cb * BS : (cb + 1) * BS] = low

    rows = slab[:, 0].reshape(BS, PIV)
    top = meta[139] == 1
    high, low = halves(jnp.where(jnp.logical_and(top, b < 2), 0.0, rows))
    for cb in range(col_blocks):
        cols = slice(cb * BS, (cb + 1) * BS)
        product = jnp.dot(high, a_low[:, cols], preferred_element_type=f32)
        product = product + jnp.dot(low, a_high[:, cols], preferred_element_type=f32)
        product = product + jnp.dot(high, a_high[:, cols], preferred_element_type=f32)
        out_ref[:, cols] = -product

    @pl.loop(meta[128 + b], meta[129 + b])
    def _(g):
        for c in copies(g):
            c.wait()
        cols = pl.ds(pl.multiple_of(meta[64 + g] * BS, BS), BS)
        out_ref[:, cols] += ring[g % RING]

        @pl.when(g + RING < total)
        def _():
            for c in copies(g + RING):
                c.start()

    @pl.when(meta[140] == 0)
    def _():
        out_ref[:, :BS] = jnp.where(jnp.logical_and(top, b == 0), first_factor[...], rows[:, :BS])
        out_ref[:, BS:PIV] = jnp.where(jnp.logical_and(top, b == 1), second_factor[...], rows[:, BS:])


def final(meta, slab, across, mats, incoming, row_blocks, col_blocks):
    whole = pl.BlockSpec((BS, BS), lambda b, meta: (0, 0))
    return pl.pallas_call(
        lambda *refs: final_kernel(col_blocks, *refs),
        grid_spec=pltpu.PrefetchScalarGridSpec(
            num_scalar_prefetch=1,
            grid=(row_blocks,),
            in_specs=[
                pl.BlockSpec((NSTRIP, 1, STRIP, PIV), lambda b, meta: (0, b, 0, 0)),
            ]
            + [whole] * 2
            + [pl.BlockSpec((NSTRIP, col_blocks, STRIP, PIV), lambda b, meta: (0, 0, 0, 0))]
            + [pl.BlockSpec(memory_space=pl.ANY)] * NPART,
            out_specs=pl.BlockSpec((BS, col_blocks * BS), lambda b, meta: (b, 0)),
            scratch_shapes=[
                pltpu.VMEM((PIV, col_blocks * BS), bf16),
                pltpu.VMEM((PIV, col_blocks * BS), bf16),
                pltpu.VMEM((RING, BS, BS), f32),
                pltpu.SemaphoreType.DMA((RING, NPART)),
            ],
        ),
        out_shape=jax.ShapeDtypeStruct((row_blocks * BS, col_blocks * BS), f32),
        compiler_params=pltpu.CompilerParams(vmem_limit_bytes=48 << 20),
        cost_estimate=pl.CostEstimate(
            flops=6 * row_blocks * col_blocks * BS * BS * PIV,
            bytes_accessed=4 * 2 * row_blocks * col_blocks * BS * BS,
            transcendentals=0,
        ),
        name="place_and_update",
    )(meta, slab, *mats, across, *incoming)


def dot(a, b):
    return jnp.dot(a, b, precision=HIGH)


def inverse(lower):
    size = lower.shape[0]
    eye = jnp.eye(size, dtype=f32)
    scale = jnp.sum(lower * eye, axis=0)
    power = eye - lower / scale[None, :]
    out = eye + power
    for _ in range(6):
        power = dot(power, power)
        out = out + dot(power, out)
    return out / scale[:, None]


def panel(block):
    half = BS // 2
    first = jnp.linalg.cholesky(lower_sym(block[:half, :half]))
    first_inv = inverse(first)
    below = dot(block[half:, :half], first_inv.T)
    second = jnp.linalg.cholesky(lower_sym(block[half:, half:] - dot(below, below.T)))
    second_inv = inverse(second)
    across = -dot(second_inv, dot(below, first_inv))
    zero = jnp.zeros((half, half), f32)
    factor = jnp.block([[first, zero], [below, second]])
    return factor, jnp.block([[first_inv.T, across.T], [zero, second_inv.T]])


def exchange(x, my_col, n_col):
    chip, core = my_col // 2, my_col % 2
    chips = n_col // 2
    pairs = x
    got = []
    for step in range(chips):
        pair = lax.dynamic_index_in_dim(pairs, (chip + step) % chips, 0, keepdims=False)
        if step:
            pair = lax.ppermute(pair, "col", [(c, (c + 2 * step) % n_col) for c in range(n_col)])
        got.append(pair)

    def from_chips(wanted):
        ordered_by = [lax.dynamic_index_in_dim(p, wanted, 0, keepdims=False) for p in got]
        return jnp.stack(ordered_by)

    mine = from_chips(core)
    other = lax.ppermute(from_chips(1 - core), "col", [(c, c ^ 1) for c in range(n_col)])
    both = jnp.stack([jnp.where(core == 0, mine, other), jnp.where(core == 0, other, mine)], 1)
    placed = [
        lax.dynamic_index_in_dim(both, (chip + chips - k) % chips, 0, keepdims=False)
        for k in range(chips)
    ]
    return jnp.stack(placed).reshape((n_col,) + x.shape[2:])


def ordered(key, valid, span):
    count = key.shape[0]
    key = jnp.where(valid, key, span)
    index = jnp.arange(count, dtype=i32)
    ahead = (key[None, :] < key[:, None]) | (
        (key[None, :] == key[:, None]) & (index[None, :] < index[:, None])
    )
    rank = jnp.sum(ahead.astype(i32), axis=1)
    chosen = rank[None, :] == index[:, None]
    order = jnp.sum(jnp.where(chosen, index[None, :], 0), axis=1)
    return order, jnp.sum(jnp.where(chosen, key[None, :], 0), axis=1), key


def body(tiles, dest, block_row, block_col, rows_from, cols_from, initial, pattern):
    n_front = lax.axis_size("front")
    n_row = lax.axis_size("row")
    n_col = lax.axis_size("col")
    my_row = lax.axis_index("row")
    my_col = lax.axis_index("col")
    row_blocks = ORDER // n_row // BS
    col_blocks = ORDER // n_col // BS
    lead = PIV // BS
    slots = n_front * n_row * CAP
    target = dest[:, 0]
    owner_row = target % n_row
    local_row = jnp.where(owner_row == 0, lead + block_row % (row_blocks - lead), block_row)
    block_id = local_row * col_blocks + block_col
    same = (target[:, None] == target[None, :]).astype(i32)
    slot = target * CAP + jnp.sum(jnp.tril(same, -1), axis=1)
    choose = jnp.arange(slots, dtype=i32)[:, None] == slot[None, :]
    labels = jnp.where(
        jnp.any(choose, axis=1), jnp.sum(jnp.where(choose, block_id[None, :], 0), axis=1), -1
    )
    pivot = initial[0, :PIV]
    sent = [lax.ppermute(pivot, "row", [(0, to)]) for to in range(1, n_row)]
    pivot = jnp.where(my_row == 0, pivot, sent[0] + sent[1] + sent[2])
    row = jnp.zeros((1, pivot.shape[1]), f32).at[0, : slot.shape[0]].set(slot.astype(f32))
    near = jnp.concatenate([pivot, jnp.broadcast_to(row, (8, row.shape[1]))])
    near, slot = lax.optimization_barrier((near, slot))
    near = lax.all_gather(near, "col", axis=0)
    corner = near[:, :PIV].transpose(1, 0, 2).reshape(PIV, PIV)
    slot_meta = jnp.append(near[0, PIV, : slot.shape[0]].astype(i32), my_col)

    def send(part):
        return lax.all_to_all(part, ("front", "row"), split_axis=0, concat_axis=0, tiled=True)

    strips, parts = permute(slot, labels, tiles, rows_from, cols_from, slots)
    incoming = [send(parts[0])]
    got = [lax.ppermute(strips[k], "col", [(0, 2 * k)]) for k in range(1, NCHIP)]
    own = jnp.where(my_col == 0, strips[0], got[0] + got[1] + got[2])
    other = lax.ppermute(own[1], "col", [(2 * k, 2 * k + 1) for k in range(NCHIP)])
    first, first_inv = panel(corner[:BS, :BS])
    below = dot(corner[BS:, :BS], first_inv)
    below = jnp.where(pattern[0, 0, 1] == 1, below, jnp.zeros_like(below))
    rest = corner[BS:, BS:] - dot(below, below.T)
    second, second_inv = panel(rest)
    cross = dot(below.T, second_inv)
    other, first, second, first_inv, second_inv, cross = lax.optimization_barrier(
        (other, first, second, first_inv, second_inv, cross)
    )
    slotted = slot_strips(slot_meta, own, other, slots)
    slotted, incoming[0] = lax.optimization_barrier((slotted, incoming[0]))
    names = incoming[0][:, PARTS[0], 0]
    pivot_columns = initial[0].reshape(row_blocks, NSTRIP, STRIP, -1).transpose(1, 0, 2, 3)
    pivot_columns = pivot_columns.reshape(NCHIP, 2, row_blocks * STRIP, -1)
    extra = jnp.broadcast_to(names, (NCHIP, 2, 8, slots))
    got = exchange(jnp.concatenate([pivot_columns, extra], axis=2), my_col, n_col)
    pivot_columns = got[:, : row_blocks * STRIP].reshape(n_col, row_blocks, STRIP, -1)
    first_names = got[0, row_blocks * STRIP].astype(i32)
    names = names.astype(i32)

    valid = names >= 0
    order, sorted_id, key = ordered(names, valid, row_blocks * col_blocks)
    bounds = jnp.arange(row_blocks + 1, dtype=i32)[:, None] * col_blocks
    starts = jnp.sum((key[None, :] < bounds).astype(i32), axis=1)
    in_slab = (first_names >= 0) & (first_names % col_blocks < lead)
    slab_key = (first_names // col_blocks) * lead + first_names % col_blocks
    slab_order, slab_id, _ = ordered(slab_key, in_slab, row_blocks * lead)
    slab_meta = jnp.concatenate(
        [slab_order, slab_id, jnp.sum(in_slab.astype(i32))[None], my_col[None]]
    )

    meta = jnp.concatenate(
        [order, sorted_id % col_blocks, starts, (my_row == 0).astype(i32)[None], my_col[None]]
    )

    strip = slab_strip(slab_meta, pivot_columns, send(slotted))

    blocks = my_row * row_blocks + jnp.arange(row_blocks, dtype=i32)
    flags = lax.dynamic_slice_in_dim(pattern[0], my_row * row_blocks, row_blocks, 1)
    keep = (flags == 1) & (blocks[None, :] > jnp.arange(2, dtype=i32)[:, None])
    keep = jnp.repeat(keep, STRIP, axis=1)[:, :, None]
    strip = strip.reshape(row_blocks * STRIP, PIV)
    one = dot(strip[:, :BS], first_inv)
    one = jnp.where(keep[0], one, jnp.zeros_like(one))
    two = dot(strip[:, BS:], second_inv) - dot(one, cross)
    two = jnp.where(keep[1], two, jnp.zeros_like(two))
    solved = jnp.concatenate([one, two], axis=1).reshape(row_blocks, STRIP, PIV)

    part, solved = lax.optimization_barrier((parts[1], solved))
    rows = lax.all_gather(solved, "row", axis=0)
    incoming.append(send(part))
    part, rows, solved, incoming[1] = lax.optimization_barrier((parts[2], rows, solved, incoming[1]))
    incoming.append(send(part))
    slab = lax.all_gather(solved, "col", axis=0)
    across = exchange(rows.reshape(NCHIP, 2, col_blocks, STRIP, PIV), my_col, n_col)
    return final(meta, slab, across, (first, second), incoming, row_blocks, col_blocks)[None]


def solution(mesh):
    placed = (
        P(("front", "row", "col"), None, None),
        P(("front", "row", "col"), None),
        P(("front", "row", "col")),
        P(("front", "row", "col")),
        P(("front", "row", "col"), None),
        P(("front", "row", "col"), None),
        P("front", "row", "col"),
        P("front", None, None),
    )
    return jax.shard_map(
        body, mesh=mesh, in_specs=placed, out_specs=P("front", "row", "col"), check_vma=False
    )
```

```python
import jax
import jax.numpy as jnp
from jax import lax
from jax.experimental import pallas as pl
from jax.experimental.pallas import tpu as pltpu
from jax.sharding import PartitionSpec as P

ORDER = 10240
BS = 256
CAP = 4
PIV = 512
STRIP = 32
NSTRIP = BS // STRIP
NCHIP = NSTRIP // 2
MARK = 8
PARTS = (96, 80, 80)
OFFSETS = tuple(sum(PARTS[:q]) for q in range(len(PARTS)))
NPART = len(PARTS)
GROUP = 8
RING = 8

HIGH = lax.Precision.HIGHEST
f32, bf16, i32 = jnp.float32, jnp.bfloat16, jnp.int32


def lower_sym(block):
    return jnp.tril(block) + jnp.tril(block, -1).T


def permute_kernel(slot_ref, label_ref, tile_ref, rows_ref, cols_ref, *refs):
    chip_refs, part_refs = refs[:NCHIP], refs[NCHIP : NCHIP + NPART]
    hold, mark, mark_sem, strip_sems, part_sems = refs[NCHIP + NPART :]
    step = pl.program_id(0)

    def marks():
        rows = part_refs[0].at[:, pl.ds(PARTS[0], MARK)]
        return pltpu.make_async_copy(mark, rows, mark_sem)

    @pl.when(step == 0)
    def _():
        def fill(s, carry):
            mark[s] = jnp.full(mark.shape[1:], label_ref[s].astype(f32))
            return carry

        lax.fori_loop(0, mark.shape[0], fill, 0)
        marks().start()

    half = BS // 2
    lane = lax.broadcasted_iota(i32, (BS, half), 1)
    place = lax.broadcasted_iota(i32, (BS, BS), 0)

    def move(g, carry):
        t = step * GROUP + g
        tile = tile_ref[g]
        high = tile.astype(bf16)
        rest = tile - high.astype(f32)
        mid = rest.astype(bf16)
        low = (rest - mid.astype(f32)).astype(bf16)
        parts = jnp.concatenate([high, mid, low], axis=1)
        wanted = jnp.transpose(jnp.broadcast_to(rows_ref[g], (half, BS)))
        pick_rows = jnp.concatenate(
            [jnp.where(wanted == lane + k * half, 1.0, 0.0) for k in range(2)], axis=1
        ).astype(bf16)
        pick_cols = jnp.where(place == cols_ref[g], 1.0, 0.0).astype(bf16)
        moved = jnp.dot(pick_rows, parts, preferred_element_type=f32).astype(bf16)
        out = jnp.dot(moved[:, :BS], pick_cols, preferred_element_type=f32)
        out = out + jnp.dot(moved[:, BS : 2 * BS], pick_cols, preferred_element_type=f32)
        out = out + jnp.dot(moved[:, 2 * BS :], pick_cols, preferred_element_type=f32)
        hold[t] = out
        for k in range(NSTRIP):
            pltpu.make_async_copy(
                hold.at[t, pl.ds(k * STRIP, STRIP)], chip_refs[k // 2].at[k % 2, t], strip_sems.at[t]
            ).start()
        for q in range(NPART):
            pltpu.make_async_copy(
                hold.at[t, pl.ds(OFFSETS[q], PARTS[q])],
                part_refs[q].at[slot_ref[t], pl.ds(0, PARTS[q])],
                part_sems.at[t],
            ).start()
        return carry

    lax.fori_loop(0, GROUP, move, 0, unroll=2)

    @pl.when(step == pl.num_programs(0) - 1)
    def _():
        def finish(t, carry):
            pltpu.make_async_copy(hold.at[t], hold.at[t], strip_sems.at[t]).wait()
            pltpu.make_async_copy(hold.at[t], hold.at[t], part_sems.at[t]).wait()
            return carry

        lax.fori_loop(0, hold.shape[0], finish, 0)
        marks().wait()


def permute(slot, labels, tiles, rows_from, cols_from, slots):
    count = tiles.shape[0]
    out = pl.pallas_call(
        permute_kernel,
        grid_spec=pltpu.PrefetchScalarGridSpec(
            num_scalar_prefetch=2,
            grid=(count // GROUP,),
            in_specs=[
                pl.BlockSpec((GROUP, BS, BS), lambda t, slot, labels: (t, 0, 0)),
                pl.BlockSpec((GROUP, 1, BS), lambda t, slot, labels: (t, 0, 0)),
                pl.BlockSpec((GROUP, 1, BS), lambda t, slot, labels: (t, 0, 0)),
            ],
            out_specs=[pl.BlockSpec(memory_space=pl.ANY)] * (NCHIP + NPART),
            scratch_shapes=[
                pltpu.VMEM((count, BS, BS), f32),
                pltpu.VMEM((slots, MARK, BS), f32),
                pltpu.SemaphoreType.DMA(()),
                pltpu.SemaphoreType.DMA((count,)),
                pltpu.SemaphoreType.DMA((count,)),
            ],
        ),
        out_shape=[jax.ShapeDtypeStruct((2, count, STRIP, BS), f32)] * NCHIP
        + [
            jax.ShapeDtypeStruct((slots, n + (MARK if q == 0 else 0), BS), f32)
            for q, n in enumerate(PARTS)
        ],
        compiler_params=pltpu.CompilerParams(vmem_limit_bytes=58 << 20),
        cost_estimate=pl.CostEstimate(
            flops=12 * count * BS**3, bytes_accessed=12 * count * BS * BS, transcendentals=0
        ),
        name="permute_tiles",
    )(slot, labels, tiles, rows_from[:, None, :], cols_from[:, None, :])
    return list(out[:NCHIP]), list(out[NCHIP:])


def slot_kernel(count, meta, own_ref, other_ref, out_ref, hold, in_sem, sems):
    @pl.when(meta[count] % 2 == 0)
    def _():
        copy = pltpu.make_async_copy(own_ref.at[0], hold, in_sem)
        copy.start()
        copy.wait()

    @pl.when(meta[count] % 2 == 1)
    def _():
        copy = pltpu.make_async_copy(other_ref, hold, in_sem)
        copy.start()
        copy.wait()

    def begin(t, carry):
        pltpu.make_async_copy(hold.at[t], out_ref.at[meta[t]], sems.at[t]).start()
        return carry

    lax.fori_loop(0, count, begin, 0)

    def finish(t, carry):
        pltpu.make_async_copy(hold.at[t], out_ref.at[meta[t]], sems.at[t]).wait()
        return carry

    lax.fori_loop(0, count, finish, 0)


def slot_strips(meta, own, other, slots):
    count = other.shape[0]
    return pl.pallas_call(
        lambda *refs: slot_kernel(count, *refs),
        grid_spec=pltpu.PrefetchScalarGridSpec(
            num_scalar_prefetch=1,
            grid=(1,),
            in_specs=[pl.BlockSpec(memory_space=pl.ANY)] * 2,
            out_specs=pl.BlockSpec(memory_space=pl.ANY),
            scratch_shapes=[
                pltpu.VMEM(other.shape, f32),
                pltpu.SemaphoreType.DMA(()),
                pltpu.SemaphoreType.DMA((count,)),
            ],
        ),
        out_shape=jax.ShapeDtypeStruct((slots, STRIP, BS), f32),
        compiler_params=pltpu.CompilerParams(vmem_limit_bytes=58 << 20),
        cost_estimate=pl.CostEstimate(
            flops=0, bytes_accessed=8 * count * STRIP * BS, transcendentals=0
        ),
        name="slot_strips",
    )(meta, own, other)


def slab_kernel(meta, initial_ref, in_ref, out_ref, ring, sems):
    total = meta[128]
    pieces, width = initial_ref.shape[0], initial_ref.shape[3]

    def copy(g):
        return pltpu.make_async_copy(in_ref.at[meta[g]], ring.at[g % RING], sems.at[g % RING])

    for g in range(RING):

        @pl.when(g < total)
        def _():
            copy(g).start()

    for k in range(pieces):
        out_ref[:, :, k * width : (k + 1) * width] = initial_ref[k]

    @pl.loop(0, total)
    def _(g):
        copy(g).wait()
        spot = meta[64 + g]
        cols = pl.ds(pl.multiple_of((spot % 2) * BS, BS), BS)
        out_ref[spot // 2, :, cols] += ring[g % RING]

        @pl.when(g + RING < total)
        def _():
            copy(g + RING).start()


def slab_strip(meta, initial, incoming):
    pieces, blocks, height, width = initial.shape
    shape = (blocks, height, pieces * width)
    return pl.pallas_call(
        slab_kernel,
        grid_spec=pltpu.PrefetchScalarGridSpec(
            num_scalar_prefetch=1,
            grid=(1,),
            in_specs=[
                pl.BlockSpec(initial.shape, lambda i, meta: (0, 0, 0, 0)),
                pl.BlockSpec(memory_space=pl.ANY),
            ],
            out_specs=pl.BlockSpec(shape, lambda i, meta: (0, 0, 0)),
            scratch_shapes=[
                pltpu.VMEM((RING, height, BS), f32),
                pltpu.SemaphoreType.DMA((RING,)),
            ],
        ),
        out_shape=jax.ShapeDtypeStruct(shape, f32),
        compiler_params=pltpu.CompilerParams(vmem_limit_bytes=32 << 20),
        cost_estimate=pl.CostEstimate(
            flops=0, bytes_accessed=12 * blocks * STRIP * PIV, transcendentals=0
        ),
        name="slab_strip",
    )(meta, initial, incoming)


def halves(x):
    high = x.astype(bf16)
    return high, (x - high.astype(f32)).astype(bf16)


def final_kernel(col_blocks, *refs):
    meta = refs[0]
    slab, first_factor, second_factor = refs[1:4]
    across, incoming = refs[4], refs[5 : 5 + NPART]
    out_ref, a_high, a_low, ring, sems = refs[5 + NPART :]
    b = pl.program_id(0)
    total = meta[138]

    def copies(g):
        return [
            pltpu.make_async_copy(
                incoming[q].at[meta[g], pl.ds(0, PARTS[q])],
                ring.at[g % RING, pl.ds(OFFSETS[q], PARTS[q])],
                sems.at[g % RING, q],
            )
            for q in range(NPART)
        ]

    @pl.when(b == 0)
    def _():
        for g in range(RING):

            @pl.when(g < total)
            def _():
                for c in copies(g):
                    c.start()

        for cb in range(col_blocks):
            high, low = halves(across[:, cb].reshape(BS, PIV).T)
            a_high[:, cb * BS : (cb + 1) * BS] = high
            a_low[:, cb * BS : (cb + 1) * BS] = low

    rows = slab[:, 0].reshape(BS, PIV)
    top = meta[139] == 1
    high, low = halves(jnp.where(jnp.logical_and(top, b < 2), 0.0, rows))
    for cb in range(col_blocks):
        cols = slice(cb * BS, (cb + 1) * BS)
        product = jnp.dot(high, a_low[:, cols], preferred_element_type=f32)
        product = product + jnp.dot(low, a_high[:, cols], preferred_element_type=f32)
        product = product + jnp.dot(high, a_high[:, cols], preferred_element_type=f32)
        out_ref[:, cols] = -product

    @pl.loop(meta[128 + b], meta[129 + b])
    def _(g):
        for c in copies(g):
            c.wait()
        cols = pl.ds(pl.multiple_of(meta[64 + g] * BS, BS), BS)
        out_ref[:, cols] += ring[g % RING]

        @pl.when(g + RING < total)
        def _():
            for c in copies(g + RING):
                c.start()

    @pl.when(meta[140] == 0)
    def _():
        out_ref[:, :BS] = jnp.where(jnp.logical_and(top, b == 0), first_factor[...], rows[:, :BS])
        out_ref[:, BS:PIV] = jnp.where(jnp.logical_and(top, b == 1), second_factor[...], rows[:, BS:])


def final(meta, slab, across, mats, incoming, row_blocks, col_blocks):
    whole = pl.BlockSpec((BS, BS), lambda b, meta: (0, 0))
    return pl.pallas_call(
        lambda *refs: final_kernel(col_blocks, *refs),
        grid_spec=pltpu.PrefetchScalarGridSpec(
            num_scalar_prefetch=1,
            grid=(row_blocks,),
            in_specs=[
                pl.BlockSpec((NSTRIP, 1, STRIP, PIV), lambda b, meta: (0, b, 0, 0)),
            ]
            + [whole] * 2
            + [pl.BlockSpec((NSTRIP, col_blocks, STRIP, PIV), lambda b, meta: (0, 0, 0, 0))]
            + [pl.BlockSpec(memory_space=pl.ANY)] * NPART,
            out_specs=pl.BlockSpec((BS, col_blocks * BS), lambda b, meta: (b, 0)),
            scratch_shapes=[
                pltpu.VMEM((PIV, col_blocks * BS), bf16),
                pltpu.VMEM((PIV, col_blocks * BS), bf16),
                pltpu.VMEM((RING, BS, BS), f32),
                pltpu.SemaphoreType.DMA((RING, NPART)),
            ],
        ),
        out_shape=jax.ShapeDtypeStruct((row_blocks * BS, col_blocks * BS), f32),
        compiler_params=pltpu.CompilerParams(vmem_limit_bytes=48 << 20),
        cost_estimate=pl.CostEstimate(
            flops=6 * row_blocks * col_blocks * BS * BS * PIV,
            bytes_accessed=4 * 2 * row_blocks * col_blocks * BS * BS,
            transcendentals=0,
        ),
        name="place_and_update",
    )(meta, slab, *mats, across, *incoming)


def dot(a, b):
    return jnp.dot(a, b, precision=HIGH)


def inverse(lower):
    size = lower.shape[0]
    eye = jnp.eye(size, dtype=f32)
    scale = jnp.sum(lower * eye, axis=0)
    power = eye - lower / scale[None, :]
    out = eye + power
    for _ in range(6):
        power = dot(power, power)
        out = out + dot(power, out)
    return out / scale[:, None]


def panel(block):
    half = BS // 2
    first = jnp.linalg.cholesky(lower_sym(block[:half, :half]))
    first_inv = inverse(first)
    below = dot(block[half:, :half], first_inv.T)
    second = jnp.linalg.cholesky(lower_sym(block[half:, half:] - dot(below, below.T)))
    second_inv = inverse(second)
    across = -dot(second_inv, dot(below, first_inv))
    zero = jnp.zeros((half, half), f32)
    factor = jnp.block([[first, zero], [below, second]])
    return factor, jnp.block([[first_inv.T, across.T], [zero, second_inv.T]])


def exchange(x, my_col, n_col):
    chip, core = my_col // 2, my_col % 2
    chips = n_col // 2
    pairs = x
    got = []
    for step in range(chips):
        pair = lax.dynamic_index_in_dim(pairs, (chip + step) % chips, 0, keepdims=False)
        if step:
            pair = lax.ppermute(pair, "col", [(c, (c + 2 * step) % n_col) for c in range(n_col)])
        got.append(pair)

    def from_chips(wanted):
        ordered_by = [lax.dynamic_index_in_dim(p, wanted, 0, keepdims=False) for p in got]
        return jnp.stack(ordered_by)

    mine = from_chips(core)
    other = lax.ppermute(from_chips(1 - core), "col", [(c, c ^ 1) for c in range(n_col)])
    both = jnp.stack([jnp.where(core == 0, mine, other), jnp.where(core == 0, other, mine)], 1)
    placed = [
        lax.dynamic_index_in_dim(both, (chip + chips - k) % chips, 0, keepdims=False)
        for k in range(chips)
    ]
    return jnp.stack(placed).reshape((n_col,) + x.shape[2:])


def ordered(key, valid, span):
    count = key.shape[0]
    key = jnp.where(valid, key, span)
    index = jnp.arange(count, dtype=i32)
    ahead = (key[None, :] < key[:, None]) | (
        (key[None, :] == key[:, None]) & (index[None, :] < index[:, None])
    )
    rank = jnp.sum(ahead.astype(i32), axis=1)
    chosen = rank[None, :] == index[:, None]
    order = jnp.sum(jnp.where(chosen, index[None, :], 0), axis=1)
    return order, jnp.sum(jnp.where(chosen, key[None, :], 0), axis=1), key


def body(tiles, dest, block_row, block_col, rows_from, cols_from, initial, pattern):
    n_front = lax.axis_size("front")
    n_row = lax.axis_size("row")
    n_col = lax.axis_size("col")
    my_row = lax.axis_index("row")
    my_col = lax.axis_index("col")
    row_blocks = ORDER // n_row // BS
    col_blocks = ORDER // n_col // BS
    lead = PIV // BS
    slots = n_front * n_row * CAP
    target = dest[:, 0]
    owner_row = target % n_row
    local_row = jnp.where(owner_row == 0, lead + block_row % (row_blocks - lead), block_row)
    block_id = local_row * col_blocks + block_col
    same = (target[:, None] == target[None, :]).astype(i32)
    slot = target * CAP + jnp.sum(jnp.tril(same, -1), axis=1)
    choose = jnp.arange(slots, dtype=i32)[:, None] == slot[None, :]
    labels = jnp.where(
        jnp.any(choose, axis=1), jnp.sum(jnp.where(choose, block_id[None, :], 0), axis=1), -1
    )
    def send(part):
        return lax.all_to_all(part, ("front", "row"), split_axis=0, concat_axis=0, tiled=True)

    strips, parts = permute(slot, labels, tiles, rows_from, cols_from, slots)
    incoming = [send(parts[0])]
    strips[0], pivot, slot = lax.optimization_barrier((strips[0], initial[0, :PIV], slot))
    sent = [lax.ppermute(pivot, "row", [(0, to)]) for to in range(1, n_row)]
    pivot = jnp.where(my_row == 0, pivot, sent[0] + sent[1] + sent[2])
    row = jnp.zeros((1, pivot.shape[1]), f32).at[0, : slot.shape[0]].set(slot.astype(f32))
    near = jnp.concatenate([pivot, jnp.broadcast_to(row, (8, row.shape[1]))])
    near, *strips = lax.optimization_barrier((near, *strips))
    near = lax.all_gather(near, "col", axis=0)
    corner = near[:, :PIV].transpose(1, 0, 2).reshape(PIV, PIV)
    slot_meta = jnp.append(near[0, PIV, : slot.shape[0]].astype(i32), my_col)
    got = [lax.ppermute(strips[k], "col", [(0, 2 * k)]) for k in range(1, NCHIP)]
    own = jnp.where(my_col == 0, strips[0], got[0] + got[1] + got[2])
    other = lax.ppermute(own[1], "col", [(2 * k, 2 * k + 1) for k in range(NCHIP)])
    first, first_inv = panel(corner[:BS, :BS])
    below = dot(corner[BS:, :BS], first_inv)
    below = jnp.where(pattern[0, 0, 1] == 1, below, jnp.zeros_like(below))
    rest = corner[BS:, BS:] - dot(below, below.T)
    other, first, first_inv, rest = lax.optimization_barrier((other, first, first_inv, rest))
    slotted = slot_strips(slot_meta, own, other, slots)
    slotted, incoming[0] = lax.optimization_barrier((slotted, incoming[0]))
    names = incoming[0][:, PARTS[0], 0]
    pivot_columns = initial[0].reshape(row_blocks, NSTRIP, STRIP, -1).transpose(1, 0, 2, 3)
    pivot_columns = pivot_columns.reshape(NCHIP, 2, row_blocks * STRIP, -1)
    extra = jnp.broadcast_to(names, (NCHIP, 2, 8, slots))
    got = exchange(jnp.concatenate([pivot_columns, extra], axis=2), my_col, n_col)
    pivot_columns = got[:, : row_blocks * STRIP].reshape(n_col, row_blocks, STRIP, -1)
    first_names = got[0, row_blocks * STRIP].astype(i32)
    names = names.astype(i32)

    valid = names >= 0
    order, sorted_id, key = ordered(names, valid, row_blocks * col_blocks)
    bounds = jnp.arange(row_blocks + 1, dtype=i32)[:, None] * col_blocks
    starts = jnp.sum((key[None, :] < bounds).astype(i32), axis=1)
    in_slab = (first_names >= 0) & (first_names % col_blocks < lead)
    slab_key = (first_names // col_blocks) * lead + first_names % col_blocks
    slab_order, slab_id, _ = ordered(slab_key, in_slab, row_blocks * lead)
    slab_meta = jnp.concatenate(
        [slab_order, slab_id, jnp.sum(in_slab.astype(i32))[None], my_col[None]]
    )

    meta = jnp.concatenate(
        [order, sorted_id % col_blocks, starts, (my_row == 0).astype(i32)[None], my_col[None]]
    )

    strip = slab_strip(slab_meta, pivot_columns, send(slotted))

    part, strip, rest = lax.optimization_barrier((parts[1], strip, rest))
    incoming.append(send(part))
    rows = lax.all_gather(strip, "row", axis=0)
    second, second_inv = panel(rest)
    cross = dot(below.T, second_inv)
    part, rows, incoming[1], second, second_inv, cross = lax.optimization_barrier(
        (parts[2], rows, incoming[1], second, second_inv, cross)
    )
    incoming.append(send(part))

    blocks = jnp.arange(n_row * row_blocks, dtype=i32)
    keep = (pattern[0] == 1) & (blocks[None, :] > jnp.arange(2, dtype=i32)[:, None])
    keep = jnp.repeat(keep, STRIP, axis=1)[:, :, None]
    rows = rows.reshape(n_row * row_blocks * STRIP, PIV)
    one = dot(rows[:, :BS], first_inv)
    one = jnp.where(keep[0], one, jnp.zeros_like(one))
    two = dot(rows[:, BS:], second_inv) - dot(one, cross)
    two = jnp.where(keep[1], two, jnp.zeros_like(two))
    solved = jnp.concatenate([one, two], axis=1).reshape(n_row, row_blocks, STRIP, PIV)
    slab = lax.all_gather(
        lax.dynamic_index_in_dim(solved, my_row, 0, keepdims=False), "col", axis=0
    )
    across = exchange(solved.reshape(NCHIP, 2, col_blocks, STRIP, PIV), my_col, n_col)
    return final(meta, slab, across, (first, second), incoming, row_blocks, col_blocks)[None]


def solution(mesh):
    placed = (
        P(("front", "row", "col"), None, None),
        P(("front", "row", "col"), None),
        P(("front", "row", "col")),
        P(("front", "row", "col")),
        P(("front", "row", "col"), None),
        P(("front", "row", "col"), None),
        P("front", "row", "col"),
        P("front", None, None),
    )
    return jax.shard_map(
        body, mesh=mesh, in_specs=placed, out_specs=P("front", "row", "col"), check_vma=False
    )
```

```python
import jax
import jax.numpy as jnp
from jax import lax
from jax.experimental import pallas as pl
from jax.experimental.pallas import tpu as pltpu
from jax.sharding import PartitionSpec as P

ORDER = 10240
BS = 256
CAP = 4
PIV = 512
STRIP = 32
NSTRIP = BS // STRIP
NCHIP = NSTRIP // 2
MARK = 8
PARTS = (80, 96, 80)
OFFSETS = tuple(sum(PARTS[:q]) for q in range(len(PARTS)))
NPART = len(PARTS)
GROUP = 8
RING = 8

HIGH = lax.Precision.HIGHEST
f32, bf16, i32 = jnp.float32, jnp.bfloat16, jnp.int32


def lower_sym(block):
    return jnp.tril(block) + jnp.tril(block, -1).T


def permute_kernel(slot_ref, label_ref, tile_ref, rows_ref, cols_ref, *refs):
    chip_refs, part_refs = refs[:NCHIP], refs[NCHIP : NCHIP + NPART]
    hold, mark, mark_sem, strip_sems, part_sems = refs[NCHIP + NPART :]
    step = pl.program_id(0)

    def marks():
        rows = part_refs[0].at[:, pl.ds(PARTS[0], MARK)]
        return pltpu.make_async_copy(mark, rows, mark_sem)

    @pl.when(step == 0)
    def _():
        def fill(s, carry):
            mark[s] = jnp.full(mark.shape[1:], label_ref[s].astype(f32))
            return carry

        lax.fori_loop(0, mark.shape[0], fill, 0)
        marks().start()

    half = BS // 2
    lane = lax.broadcasted_iota(i32, (BS, half), 1)
    place = lax.broadcasted_iota(i32, (BS, BS), 0)

    def move(g, carry):
        t = step * GROUP + g
        tile = tile_ref[g]
        high = tile.astype(bf16)
        rest = tile - high.astype(f32)
        mid = rest.astype(bf16)
        low = (rest - mid.astype(f32)).astype(bf16)
        parts = jnp.concatenate([high, mid, low], axis=1)
        wanted = jnp.transpose(jnp.broadcast_to(rows_ref[g], (half, BS)))
        pick_rows = jnp.concatenate(
            [jnp.where(wanted == lane + k * half, 1.0, 0.0) for k in range(2)], axis=1
        ).astype(bf16)
        pick_cols = jnp.where(place == cols_ref[g], 1.0, 0.0).astype(bf16)
        moved = jnp.dot(pick_rows, parts, preferred_element_type=f32).astype(bf16)
        out = jnp.dot(moved[:, :BS], pick_cols, preferred_element_type=f32)
        out = out + jnp.dot(moved[:, BS : 2 * BS], pick_cols, preferred_element_type=f32)
        out = out + jnp.dot(moved[:, 2 * BS :], pick_cols, preferred_element_type=f32)
        hold[t] = out
        for k in range(NSTRIP):
            pltpu.make_async_copy(
                hold.at[t, pl.ds(k * STRIP, STRIP)], chip_refs[k // 2].at[k % 2, t], strip_sems.at[t]
            ).start()
        for q in range(NPART):
            pltpu.make_async_copy(
                hold.at[t, pl.ds(OFFSETS[q], PARTS[q])],
                part_refs[q].at[slot_ref[t], pl.ds(0, PARTS[q])],
                part_sems.at[t],
            ).start()
        return carry

    lax.fori_loop(0, GROUP, move, 0, unroll=2)

    @pl.when(step == pl.num_programs(0) - 1)
    def _():
        def finish(t, carry):
            pltpu.make_async_copy(hold.at[t], hold.at[t], strip_sems.at[t]).wait()
            pltpu.make_async_copy(hold.at[t], hold.at[t], part_sems.at[t]).wait()
            return carry

        lax.fori_loop(0, hold.shape[0], finish, 0)
        marks().wait()


def permute(slot, labels, tiles, rows_from, cols_from, slots):
    count = tiles.shape[0]
    out = pl.pallas_call(
        permute_kernel,
        grid_spec=pltpu.PrefetchScalarGridSpec(
            num_scalar_prefetch=2,
            grid=(count // GROUP,),
            in_specs=[
                pl.BlockSpec((GROUP, BS, BS), lambda t, slot, labels: (t, 0, 0)),
                pl.BlockSpec((GROUP, 1, BS), lambda t, slot, labels: (t, 0, 0)),
                pl.BlockSpec((GROUP, 1, BS), lambda t, slot, labels: (t, 0, 0)),
            ],
            out_specs=[pl.BlockSpec(memory_space=pl.ANY)] * (NCHIP + NPART),
            scratch_shapes=[
                pltpu.VMEM((count, BS, BS), f32),
                pltpu.VMEM((slots, MARK, BS), f32),
                pltpu.SemaphoreType.DMA(()),
                pltpu.SemaphoreType.DMA((count,)),
                pltpu.SemaphoreType.DMA((count,)),
            ],
        ),
        out_shape=[jax.ShapeDtypeStruct((2, count, STRIP, BS), f32)] * NCHIP
        + [
            jax.ShapeDtypeStruct((slots, n + (MARK if q == 0 else 0), BS), f32)
            for q, n in enumerate(PARTS)
        ],
        compiler_params=pltpu.CompilerParams(vmem_limit_bytes=58 << 20),
        cost_estimate=pl.CostEstimate(
            flops=12 * count * BS**3, bytes_accessed=12 * count * BS * BS, transcendentals=0
        ),
        name="permute_tiles",
    )(slot, labels, tiles, rows_from[:, None, :], cols_from[:, None, :])
    return list(out[:NCHIP]), list(out[NCHIP:])


def slot_kernel(count, meta, own_ref, other_ref, out_ref, hold, in_sem, sems):
    @pl.when(meta[count] % 2 == 0)
    def _():
        copy = pltpu.make_async_copy(own_ref.at[0], hold, in_sem)
        copy.start()
        copy.wait()

    @pl.when(meta[count] % 2 == 1)
    def _():
        copy = pltpu.make_async_copy(other_ref, hold, in_sem)
        copy.start()
        copy.wait()

    def begin(t, carry):
        pltpu.make_async_copy(hold.at[t], out_ref.at[meta[t]], sems.at[t]).start()
        return carry

    lax.fori_loop(0, count, begin, 0)

    def finish(t, carry):
        pltpu.make_async_copy(hold.at[t], out_ref.at[meta[t]], sems.at[t]).wait()
        return carry

    lax.fori_loop(0, count, finish, 0)


def slot_strips(meta, own, other, slots):
    count = other.shape[0]
    return pl.pallas_call(
        lambda *refs: slot_kernel(count, *refs),
        grid_spec=pltpu.PrefetchScalarGridSpec(
            num_scalar_prefetch=1,
            grid=(1,),
            in_specs=[pl.BlockSpec(memory_space=pl.ANY)] * 2,
            out_specs=pl.BlockSpec(memory_space=pl.ANY),
            scratch_shapes=[
                pltpu.VMEM(other.shape, f32),
                pltpu.SemaphoreType.DMA(()),
                pltpu.SemaphoreType.DMA((count,)),
            ],
        ),
        out_shape=jax.ShapeDtypeStruct((slots, STRIP, BS), f32),
        compiler_params=pltpu.CompilerParams(vmem_limit_bytes=58 << 20),
        cost_estimate=pl.CostEstimate(
            flops=0, bytes_accessed=8 * count * STRIP * BS, transcendentals=0
        ),
        name="slot_strips",
    )(meta, own, other)


def slab_kernel(meta, initial_ref, in_ref, out_ref, ring, sems):
    total = meta[128]
    pieces, width = initial_ref.shape[0], initial_ref.shape[3]

    def copy(g):
        return pltpu.make_async_copy(in_ref.at[meta[g]], ring.at[g % RING], sems.at[g % RING])

    for g in range(RING):

        @pl.when(g < total)
        def _():
            copy(g).start()

    for k in range(pieces):
        out_ref[:, :, k * width : (k + 1) * width] = initial_ref[k]

    @pl.loop(0, total)
    def _(g):
        copy(g).wait()
        spot = meta[64 + g]
        cols = pl.ds(pl.multiple_of((spot % 2) * BS, BS), BS)
        out_ref[spot // 2, :, cols] += ring[g % RING]

        @pl.when(g + RING < total)
        def _():
            copy(g + RING).start()


def slab_strip(meta, initial, incoming):
    pieces, blocks, height, width = initial.shape
    shape = (blocks, height, pieces * width)
    return pl.pallas_call(
        slab_kernel,
        grid_spec=pltpu.PrefetchScalarGridSpec(
            num_scalar_prefetch=1,
            grid=(1,),
            in_specs=[
                pl.BlockSpec(initial.shape, lambda i, meta: (0, 0, 0, 0)),
                pl.BlockSpec(memory_space=pl.ANY),
            ],
            out_specs=pl.BlockSpec(shape, lambda i, meta: (0, 0, 0)),
            scratch_shapes=[
                pltpu.VMEM((RING, height, BS), f32),
                pltpu.SemaphoreType.DMA((RING,)),
            ],
        ),
        out_shape=jax.ShapeDtypeStruct(shape, f32),
        compiler_params=pltpu.CompilerParams(vmem_limit_bytes=32 << 20),
        cost_estimate=pl.CostEstimate(
            flops=0, bytes_accessed=12 * blocks * STRIP * PIV, transcendentals=0
        ),
        name="slab_strip",
    )(meta, initial, incoming)


def halves(x):
    high = x.astype(bf16)
    return high, (x - high.astype(f32)).astype(bf16)


def final_kernel(col_blocks, *refs):
    meta = refs[0]
    slab, first_factor, second_factor = refs[1:4]
    across, incoming = refs[4], refs[5 : 5 + NPART]
    out_ref, a_high, a_low, ring, sems = refs[5 + NPART :]
    b = pl.program_id(0)
    total = meta[138]

    def copies(g):
        return [
            pltpu.make_async_copy(
                incoming[q].at[meta[g], pl.ds(0, PARTS[q])],
                ring.at[g % RING, pl.ds(OFFSETS[q], PARTS[q])],
                sems.at[g % RING, q],
            )
            for q in range(NPART)
        ]

    @pl.when(b == 0)
    def _():
        for g in range(RING):

            @pl.when(g < total)
            def _():
                for c in copies(g):
                    c.start()

        for cb in range(col_blocks):
            high, low = halves(across[:, cb].reshape(BS, PIV).T)
            a_high[:, cb * BS : (cb + 1) * BS] = high
            a_low[:, cb * BS : (cb + 1) * BS] = low

    rows = slab[:, 0].reshape(BS, PIV)
    top = meta[139] == 1
    high, low = halves(jnp.where(jnp.logical_and(top, b < 2), 0.0, rows))
    for cb in range(col_blocks):
        cols = slice(cb * BS, (cb + 1) * BS)
        product = jnp.dot(high, a_low[:, cols], preferred_element_type=f32)
        product = product + jnp.dot(low, a_high[:, cols], preferred_element_type=f32)
        product = product + jnp.dot(high, a_high[:, cols], preferred_element_type=f32)
        out_ref[:, cols] = -product

    @pl.loop(meta[128 + b], meta[129 + b])
    def _(g):
        for c in copies(g):
            c.wait()
        cols = pl.ds(pl.multiple_of(meta[64 + g] * BS, BS), BS)
        out_ref[:, cols] += ring[g % RING]

        @pl.when(g + RING < total)
        def _():
            for c in copies(g + RING):
                c.start()

    @pl.when(meta[140] == 0)
    def _():
        out_ref[:, :BS] = jnp.where(jnp.logical_and(top, b == 0), first_factor[...], rows[:, :BS])
        out_ref[:, BS:PIV] = jnp.where(jnp.logical_and(top, b == 1), second_factor[...], rows[:, BS:])


def final(meta, slab, across, mats, incoming, row_blocks, col_blocks):
    whole = pl.BlockSpec((BS, BS), lambda b, meta: (0, 0))
    return pl.pallas_call(
        lambda *refs: final_kernel(col_blocks, *refs),
        grid_spec=pltpu.PrefetchScalarGridSpec(
            num_scalar_prefetch=1,
            grid=(row_blocks,),
            in_specs=[
                pl.BlockSpec((NSTRIP, 1, STRIP, PIV), lambda b, meta: (0, b, 0, 0)),
            ]
            + [whole] * 2
            + [pl.BlockSpec((NSTRIP, col_blocks, STRIP, PIV), lambda b, meta: (0, 0, 0, 0))]
            + [pl.BlockSpec(memory_space=pl.ANY)] * NPART,
            out_specs=pl.BlockSpec((BS, col_blocks * BS), lambda b, meta: (b, 0)),
            scratch_shapes=[
                pltpu.VMEM((PIV, col_blocks * BS), bf16),
                pltpu.VMEM((PIV, col_blocks * BS), bf16),
                pltpu.VMEM((RING, BS, BS), f32),
                pltpu.SemaphoreType.DMA((RING, NPART)),
            ],
        ),
        out_shape=jax.ShapeDtypeStruct((row_blocks * BS, col_blocks * BS), f32),
        compiler_params=pltpu.CompilerParams(vmem_limit_bytes=48 << 20),
        cost_estimate=pl.CostEstimate(
            flops=6 * row_blocks * col_blocks * BS * BS * PIV,
            bytes_accessed=4 * 2 * row_blocks * col_blocks * BS * BS,
            transcendentals=0,
        ),
        name="place_and_update",
    )(meta, slab, *mats, across, *incoming)


def dot(a, b):
    return jnp.dot(a, b, precision=HIGH)


def inverse(lower):
    size = lower.shape[0]
    eye = jnp.eye(size, dtype=f32)
    scale = jnp.sum(lower * eye, axis=0)
    power = eye - lower / scale[None, :]
    out = eye + power
    for _ in range(6):
        power = dot(power, power)
        out = out + dot(power, out)
    return out / scale[:, None]


def panel(block):
    half = BS // 2
    first = jnp.linalg.cholesky(lower_sym(block[:half, :half]))
    first_inv = inverse(first)
    below = dot(block[half:, :half], first_inv.T)
    second = jnp.linalg.cholesky(lower_sym(block[half:, half:] - dot(below, below.T)))
    second_inv = inverse(second)
    across = -dot(second_inv, dot(below, first_inv))
    zero = jnp.zeros((half, half), f32)
    factor = jnp.block([[first, zero], [below, second]])
    return factor, jnp.block([[first_inv.T, across.T], [zero, second_inv.T]])


def exchange(x, my_col, n_col):
    chip, core = my_col // 2, my_col % 2
    chips = n_col // 2
    pairs = x
    got = []
    for step in range(chips):
        pair = lax.dynamic_index_in_dim(pairs, (chip + step) % chips, 0, keepdims=False)
        if step:
            pair = lax.ppermute(pair, "col", [(c, (c + 2 * step) % n_col) for c in range(n_col)])
        got.append(pair)

    def from_chips(wanted):
        ordered_by = [lax.dynamic_index_in_dim(p, wanted, 0, keepdims=False) for p in got]
        return jnp.stack(ordered_by)

    mine = from_chips(core)
    other = lax.ppermute(from_chips(1 - core), "col", [(c, c ^ 1) for c in range(n_col)])
    both = jnp.stack([jnp.where(core == 0, mine, other), jnp.where(core == 0, other, mine)], 1)
    placed = [
        lax.dynamic_index_in_dim(both, (chip + chips - k) % chips, 0, keepdims=False)
        for k in range(chips)
    ]
    return jnp.stack(placed).reshape((n_col,) + x.shape[2:])


def ordered(key, valid, span):
    count = key.shape[0]
    key = jnp.where(valid, key, span)
    index = jnp.arange(count, dtype=i32)
    ahead = (key[None, :] < key[:, None]) | (
        (key[None, :] == key[:, None]) & (index[None, :] < index[:, None])
    )
    rank = jnp.sum(ahead.astype(i32), axis=1)
    chosen = rank[None, :] == index[:, None]
    order = jnp.sum(jnp.where(chosen, index[None, :], 0), axis=1)
    return order, jnp.sum(jnp.where(chosen, key[None, :], 0), axis=1), key


def body(tiles, dest, block_row, block_col, rows_from, cols_from, initial, pattern):
    n_front = lax.axis_size("front")
    n_row = lax.axis_size("row")
    n_col = lax.axis_size("col")
    my_row = lax.axis_index("row")
    my_col = lax.axis_index("col")
    row_blocks = ORDER // n_row // BS
    col_blocks = ORDER // n_col // BS
    lead = PIV // BS
    slots = n_front * n_row * CAP
    target = dest[:, 0]
    owner_row = target % n_row
    local_row = jnp.where(owner_row == 0, lead + block_row % (row_blocks - lead), block_row)
    block_id = local_row * col_blocks + block_col
    same = (target[:, None] == target[None, :]).astype(i32)
    slot = target * CAP + jnp.sum(jnp.tril(same, -1), axis=1)
    choose = jnp.arange(slots, dtype=i32)[:, None] == slot[None, :]
    labels = jnp.where(
        jnp.any(choose, axis=1), jnp.sum(jnp.where(choose, block_id[None, :], 0), axis=1), -1
    )
    def send(part):
        return lax.all_to_all(part, ("front", "row"), split_axis=0, concat_axis=0, tiled=True)

    row = jnp.zeros((1, initial.shape[2]), f32).at[0, : slot.shape[0]].set(slot.astype(f32))
    near = jnp.concatenate([initial[0, :PIV], jnp.broadcast_to(row, (8, row.shape[1]))])
    near = lax.all_gather(near, "col", axis=0)
    corner = near[:, :PIV].transpose(1, 0, 2).reshape(PIV, PIV)
    slot_meta = jnp.append(near[0, PIV, : slot.shape[0]].astype(i32), my_col)
    strips, parts = permute(slot, labels, tiles, rows_from, cols_from, slots)
    incoming = [send(parts[0])]
    got = [lax.ppermute(strips[k], "col", [(0, 2 * k)]) for k in range(1, NCHIP)]
    own = jnp.where(my_col == 0, strips[0], got[0] + got[1] + got[2])
    other = lax.ppermute(own[1], "col", [(2 * k, 2 * k + 1) for k in range(NCHIP)])
    first, first_inv = panel(corner[:BS, :BS])
    below = dot(corner[BS:, :BS], first_inv)
    below = jnp.where(pattern[0, 0, 1] == 1, below, jnp.zeros_like(below))
    second, second_inv = panel(corner[BS:, BS:] - dot(below, below.T))
    mats = jnp.concatenate([first_inv, second_inv, dot(below.T, second_inv)])
    mats = jnp.where(my_row == 0, mats, jnp.zeros_like(mats))
    other, mats, first, second = lax.optimization_barrier((other, mats, first, second))
    mats = lax.psum(mats, "row")
    slotted = slot_strips(slot_meta, own, other, slots)
    slotted, incoming[0] = lax.optimization_barrier((slotted, incoming[0]))
    names = incoming[0][:, PARTS[0], 0]
    pivot_columns = initial[0].reshape(row_blocks, NSTRIP, STRIP, -1).transpose(1, 0, 2, 3)
    pivot_columns = pivot_columns.reshape(NCHIP, 2, row_blocks * STRIP, -1)
    extra = jnp.broadcast_to(names, (NCHIP, 2, 8, slots))
    got = exchange(jnp.concatenate([pivot_columns, extra], axis=2), my_col, n_col)
    pivot_columns = got[:, : row_blocks * STRIP].reshape(n_col, row_blocks, STRIP, -1)
    first_names = got[0, row_blocks * STRIP].astype(i32)
    names = names.astype(i32)

    valid = names >= 0
    order, sorted_id, key = ordered(names, valid, row_blocks * col_blocks)
    bounds = jnp.arange(row_blocks + 1, dtype=i32)[:, None] * col_blocks
    starts = jnp.sum((key[None, :] < bounds).astype(i32), axis=1)
    in_slab = (first_names >= 0) & (first_names % col_blocks < lead)
    slab_key = (first_names // col_blocks) * lead + first_names % col_blocks
    slab_order, slab_id, _ = ordered(slab_key, in_slab, row_blocks * lead)
    slab_meta = jnp.concatenate(
        [slab_order, slab_id, jnp.sum(in_slab.astype(i32))[None], my_col[None]]
    )

    meta = jnp.concatenate(
        [order, sorted_id % col_blocks, starts, (my_row == 0).astype(i32)[None], my_col[None]]
    )

    strip = slab_strip(slab_meta, pivot_columns, send(slotted))

    part, strip = lax.optimization_barrier((parts[1], strip))
    incoming.append(send(part))
    rows = lax.all_gather(strip, "row", axis=0)
    part, rows, incoming[1], mats = lax.optimization_barrier((parts[2], rows, incoming[1], mats))
    incoming.append(send(part))
    first_inv, second_inv, cross = mats[:BS], mats[BS : 2 * BS], mats[2 * BS :]

    blocks = jnp.arange(n_row * row_blocks, dtype=i32)
    keep = (pattern[0] == 1) & (blocks[None, :] > jnp.arange(2, dtype=i32)[:, None])
    keep = jnp.repeat(keep, STRIP, axis=1)[:, :, None]
    rows = rows.reshape(n_row * row_blocks * STRIP, PIV)
    one = dot(rows[:, :BS], first_inv)
    one = jnp.where(keep[0], one, jnp.zeros_like(one))
    two = dot(rows[:, BS:], second_inv) - dot(one, cross)
    two = jnp.where(keep[1], two, jnp.zeros_like(two))
    solved = jnp.concatenate([one, two], axis=1).reshape(n_row, row_blocks, STRIP, PIV)
    slab = lax.all_gather(
        lax.dynamic_index_in_dim(solved, my_row, 0, keepdims=False), "col", axis=0
    )
    across = exchange(solved.reshape(NCHIP, 2, col_blocks, STRIP, PIV), my_col, n_col)
    return final(meta, slab, across, (first, second), incoming, row_blocks, col_blocks)[None]


def solution(mesh):
    placed = (
        P(("front", "row", "col"), None, None),
        P(("front", "row", "col"), None),
        P(("front", "row", "col")),
        P(("front", "row", "col")),
        P(("front", "row", "col"), None),
        P(("front", "row", "col"), None),
        P("front", "row", "col"),
        P("front", None, None),
    )
    return jax.shard_map(
        body, mesh=mesh, in_specs=placed, out_specs=P("front", "row", "col"), check_vma=False
    )
```

```python
import jax
import jax.numpy as jnp
from jax import lax
from jax.experimental import pallas as pl
from jax.experimental.pallas import tpu as pltpu
from jax.sharding import PartitionSpec as P

ORDER = 10240
BS = 256
CAP = 4
PIV = 512
STRIP = 32
NSTRIP = BS // STRIP
NCHIP = NSTRIP // 2
MARK = 8
PARTS = (96, 88, 72)
OFFSETS = tuple(sum(PARTS[:q]) for q in range(len(PARTS)))
NPART = len(PARTS)
GROUP = 8
RING = 8

HIGH = lax.Precision.HIGHEST
f32, bf16, i32 = jnp.float32, jnp.bfloat16, jnp.int32


def lower_sym(block):
    return jnp.tril(block) + jnp.tril(block, -1).T


def permute_kernel(slot_ref, label_ref, tile_ref, rows_ref, cols_ref, *refs):
    chip_refs, part_refs = refs[:NCHIP], refs[NCHIP : NCHIP + NPART]
    hold, mark, mark_sem, strip_sems, part_sems = refs[NCHIP + NPART :]
    step = pl.program_id(0)

    def marks():
        rows = part_refs[0].at[:, pl.ds(PARTS[0], MARK)]
        return pltpu.make_async_copy(mark, rows, mark_sem)

    @pl.when(step == 0)
    def _():
        def fill(s, carry):
            mark[s] = jnp.full(mark.shape[1:], label_ref[s].astype(f32))
            return carry

        lax.fori_loop(0, mark.shape[0], fill, 0)
        marks().start()

    half = BS // 2
    lane = lax.broadcasted_iota(i32, (BS, half), 1)
    place = lax.broadcasted_iota(i32, (BS, BS), 0)

    def move(g, carry):
        t = step * GROUP + g
        tile = tile_ref[g]
        high = tile.astype(bf16)
        rest = tile - high.astype(f32)
        mid = rest.astype(bf16)
        low = (rest - mid.astype(f32)).astype(bf16)
        parts = jnp.concatenate([high, mid, low], axis=1)
        wanted = jnp.transpose(jnp.broadcast_to(rows_ref[g], (half, BS)))
        pick_rows = jnp.concatenate(
            [jnp.where(wanted == lane + k * half, 1.0, 0.0) for k in range(2)], axis=1
        ).astype(bf16)
        pick_cols = jnp.where(place == cols_ref[g], 1.0, 0.0).astype(bf16)
        moved = jnp.dot(pick_rows, parts, preferred_element_type=f32).astype(bf16)
        out = jnp.dot(moved[:, :BS], pick_cols, preferred_element_type=f32)
        out = out + jnp.dot(moved[:, BS : 2 * BS], pick_cols, preferred_element_type=f32)
        out = out + jnp.dot(moved[:, 2 * BS :], pick_cols, preferred_element_type=f32)
        hold[t] = out
        for k in range(NSTRIP):
            pltpu.make_async_copy(
                hold.at[t, pl.ds(k * STRIP, STRIP)], chip_refs[k // 2].at[k % 2, t], strip_sems.at[t]
            ).start()
        for q in range(NPART):
            pltpu.make_async_copy(
                hold.at[t, pl.ds(OFFSETS[q], PARTS[q])],
                part_refs[q].at[slot_ref[t], pl.ds(0, PARTS[q])],
                part_sems.at[t],
            ).start()
        return carry

    lax.fori_loop(0, GROUP, move, 0, unroll=2)

    @pl.when(step == pl.num_programs(0) - 1)
    def _():
        def finish(t, carry):
            pltpu.make_async_copy(hold.at[t], hold.at[t], strip_sems.at[t]).wait()
            pltpu.make_async_copy(hold.at[t], hold.at[t], part_sems.at[t]).wait()
            return carry

        lax.fori_loop(0, hold.shape[0], finish, 0)
        marks().wait()


def permute(slot, labels, tiles, rows_from, cols_from, slots):
    count = tiles.shape[0]
    out = pl.pallas_call(
        permute_kernel,
        grid_spec=pltpu.PrefetchScalarGridSpec(
            num_scalar_prefetch=2,
            grid=(count // GROUP,),
            in_specs=[
                pl.BlockSpec((GROUP, BS, BS), lambda t, slot, labels: (t, 0, 0)),
                pl.BlockSpec((GROUP, 1, BS), lambda t, slot, labels: (t, 0, 0)),
                pl.BlockSpec((GROUP, 1, BS), lambda t, slot, labels: (t, 0, 0)),
            ],
            out_specs=[pl.BlockSpec(memory_space=pl.ANY)] * (NCHIP + NPART),
            scratch_shapes=[
                pltpu.VMEM((count, BS, BS), f32),
                pltpu.VMEM((slots, MARK, BS), f32),
                pltpu.SemaphoreType.DMA(()),
                pltpu.SemaphoreType.DMA((count,)),
                pltpu.SemaphoreType.DMA((count,)),
            ],
        ),
        out_shape=[jax.ShapeDtypeStruct((2, count, STRIP, BS), f32)] * NCHIP
        + [
            jax.ShapeDtypeStruct((slots, n + (MARK if q == 0 else 0), BS), f32)
            for q, n in enumerate(PARTS)
        ],
        compiler_params=pltpu.CompilerParams(vmem_limit_bytes=58 << 20),
        cost_estimate=pl.CostEstimate(
            flops=12 * count * BS**3, bytes_accessed=12 * count * BS * BS, transcendentals=0
        ),
        name="permute_tiles",
    )(slot, labels, tiles, rows_from[:, None, :], cols_from[:, None, :])
    return list(out[:NCHIP]), list(out[NCHIP:])


def slot_kernel(count, meta, own_ref, other_ref, out_ref, hold, in_sem, sems):
    @pl.when(meta[count] % 2 == 0)
    def _():
        copy = pltpu.make_async_copy(own_ref.at[0], hold, in_sem)
        copy.start()
        copy.wait()

    @pl.when(meta[count] % 2 == 1)
    def _():
        copy = pltpu.make_async_copy(other_ref, hold, in_sem)
        copy.start()
        copy.wait()

    def begin(t, carry):
        pltpu.make_async_copy(hold.at[t], out_ref.at[meta[t]], sems.at[t]).start()
        return carry

    lax.fori_loop(0, count, begin, 0)

    def finish(t, carry):
        pltpu.make_async_copy(hold.at[t], out_ref.at[meta[t]], sems.at[t]).wait()
        return carry

    lax.fori_loop(0, count, finish, 0)


def slot_strips(meta, own, other, slots):
    count = other.shape[0]
    return pl.pallas_call(
        lambda *refs: slot_kernel(count, *refs),
        grid_spec=pltpu.PrefetchScalarGridSpec(
            num_scalar_prefetch=1,
            grid=(1,),
            in_specs=[pl.BlockSpec(memory_space=pl.ANY)] * 2,
            out_specs=pl.BlockSpec(memory_space=pl.ANY),
            scratch_shapes=[
                pltpu.VMEM(other.shape, f32),
                pltpu.SemaphoreType.DMA(()),
                pltpu.SemaphoreType.DMA((count,)),
            ],
        ),
        out_shape=jax.ShapeDtypeStruct((slots, STRIP, BS), f32),
        compiler_params=pltpu.CompilerParams(vmem_limit_bytes=58 << 20),
        cost_estimate=pl.CostEstimate(
            flops=0, bytes_accessed=8 * count * STRIP * BS, transcendentals=0
        ),
        name="slot_strips",
    )(meta, own, other)


def slab_kernel(meta, initial_ref, in_ref, out_ref, ring, sems):
    total = meta[128]
    pieces, width = initial_ref.shape[0], initial_ref.shape[3]

    def copy(g):
        return pltpu.make_async_copy(in_ref.at[meta[g]], ring.at[g % RING], sems.at[g % RING])

    for g in range(RING):

        @pl.when(g < total)
        def _():
            copy(g).start()

    for k in range(pieces):
        out_ref[:, :, k * width : (k + 1) * width] = initial_ref[k]

    @pl.loop(0, total)
    def _(g):
        copy(g).wait()
        spot = meta[64 + g]
        cols = pl.ds(pl.multiple_of((spot % 2) * BS, BS), BS)
        out_ref[spot // 2, :, cols] += ring[g % RING]

        @pl.when(g + RING < total)
        def _():
            copy(g + RING).start()


def slab_strip(meta, initial, incoming):
    pieces, blocks, height, width = initial.shape
    shape = (blocks, height, pieces * width)
    return pl.pallas_call(
        slab_kernel,
        grid_spec=pltpu.PrefetchScalarGridSpec(
            num_scalar_prefetch=1,
            grid=(1,),
            in_specs=[
                pl.BlockSpec(initial.shape, lambda i, meta: (0, 0, 0, 0)),
                pl.BlockSpec(memory_space=pl.ANY),
            ],
            out_specs=pl.BlockSpec(shape, lambda i, meta: (0, 0, 0)),
            scratch_shapes=[
                pltpu.VMEM((RING, height, BS), f32),
                pltpu.SemaphoreType.DMA((RING,)),
            ],
        ),
        out_shape=jax.ShapeDtypeStruct(shape, f32),
        compiler_params=pltpu.CompilerParams(vmem_limit_bytes=32 << 20),
        cost_estimate=pl.CostEstimate(
            flops=0, bytes_accessed=12 * blocks * STRIP * PIV, transcendentals=0
        ),
        name="slab_strip",
    )(meta, initial, incoming)


def halves(x):
    high = x.astype(bf16)
    return high, (x - high.astype(f32)).astype(bf16)


def final_kernel(col_blocks, *refs):
    meta = refs[0]
    slab, first_factor, second_factor = refs[1:4]
    across, incoming = refs[4], refs[5 : 5 + NPART]
    out_ref, a_high, a_low, ring, sems = refs[5 + NPART :]
    b = pl.program_id(0)
    total = meta[138]

    def copies(g):
        return [
            pltpu.make_async_copy(
                incoming[q].at[meta[g], pl.ds(0, PARTS[q])],
                ring.at[g % RING, pl.ds(OFFSETS[q], PARTS[q])],
                sems.at[g % RING, q],
            )
            for q in range(NPART)
        ]

    @pl.when(b == 0)
    def _():
        for g in range(RING):

            @pl.when(g < total)
            def _():
                for c in copies(g):
                    c.start()

        for cb in range(col_blocks):
            high, low = halves(across[:, cb].reshape(BS, PIV).T)
            a_high[:, cb * BS : (cb + 1) * BS] = high
            a_low[:, cb * BS : (cb + 1) * BS] = low

    rows = slab[:, 0].reshape(BS, PIV)
    top = meta[139] == 1
    high, low = halves(jnp.where(jnp.logical_and(top, b < 2), 0.0, rows))
    for cb in range(col_blocks):
        cols = slice(cb * BS, (cb + 1) * BS)
        product = jnp.dot(high, a_low[:, cols], preferred_element_type=f32)
        product = product + jnp.dot(low, a_high[:, cols], preferred_element_type=f32)
        product = product + jnp.dot(high, a_high[:, cols], preferred_element_type=f32)
        out_ref[:, cols] = -product

    @pl.loop(meta[128 + b], meta[129 + b])
    def _(g):
        for c in copies(g):
            c.wait()
        cols = pl.ds(pl.multiple_of(meta[64 + g] * BS, BS), BS)
        out_ref[:, cols] += ring[g % RING]

        @pl.when(g + RING < total)
        def _():
            for c in copies(g + RING):
                c.start()

    @pl.when(meta[140] == 0)
    def _():
        out_ref[:, :BS] = jnp.where(jnp.logical_and(top, b == 0), first_factor[...], rows[:, :BS])
        out_ref[:, BS:PIV] = jnp.where(jnp.logical_and(top, b == 1), second_factor[...], rows[:, BS:])


def final(meta, slab, across, mats, incoming, row_blocks, col_blocks):
    whole = pl.BlockSpec((BS, BS), lambda b, meta: (0, 0))
    return pl.pallas_call(
        lambda *refs: final_kernel(col_blocks, *refs),
        grid_spec=pltpu.PrefetchScalarGridSpec(
            num_scalar_prefetch=1,
            grid=(row_blocks,),
            in_specs=[
                pl.BlockSpec((NSTRIP, 1, STRIP, PIV), lambda b, meta: (0, b, 0, 0)),
            ]
            + [whole] * 2
            + [pl.BlockSpec((NSTRIP, col_blocks, STRIP, PIV), lambda b, meta: (0, 0, 0, 0))]
            + [pl.BlockSpec(memory_space=pl.ANY)] * NPART,
            out_specs=pl.BlockSpec((BS, col_blocks * BS), lambda b, meta: (b, 0)),
            scratch_shapes=[
                pltpu.VMEM((PIV, col_blocks * BS), bf16),
                pltpu.VMEM((PIV, col_blocks * BS), bf16),
                pltpu.VMEM((RING, BS, BS), f32),
                pltpu.SemaphoreType.DMA((RING, NPART)),
            ],
        ),
        out_shape=jax.ShapeDtypeStruct((row_blocks * BS, col_blocks * BS), f32),
        compiler_params=pltpu.CompilerParams(vmem_limit_bytes=48 << 20),
        cost_estimate=pl.CostEstimate(
            flops=6 * row_blocks * col_blocks * BS * BS * PIV,
            bytes_accessed=4 * 2 * row_blocks * col_blocks * BS * BS,
            transcendentals=0,
        ),
        name="place_and_update",
    )(meta, slab, *mats, across, *incoming)


def dot(a, b):
    return jnp.dot(a, b, precision=HIGH)


def inverse(lower):
    size = lower.shape[0]
    eye = jnp.eye(size, dtype=f32)
    scale = jnp.sum(lower * eye, axis=0)
    power = eye - lower / scale[None, :]
    out = eye + power
    for _ in range(6):
        power = dot(power, power)
        out = out + dot(power, out)
    return out / scale[:, None]


def panel(block):
    half = BS // 2
    first = jnp.linalg.cholesky(lower_sym(block[:half, :half]))
    first_inv = inverse(first)
    below = dot(block[half:, :half], first_inv.T)
    second = jnp.linalg.cholesky(lower_sym(block[half:, half:] - dot(below, below.T)))
    second_inv = inverse(second)
    across = -dot(second_inv, dot(below, first_inv))
    zero = jnp.zeros((half, half), f32)
    factor = jnp.block([[first, zero], [below, second]])
    return factor, jnp.block([[first_inv.T, across.T], [zero, second_inv.T]])


def exchange(x, my_col, n_col):
    chip, core = my_col // 2, my_col % 2
    chips = n_col // 2
    pairs = x
    got = []
    for step in range(chips):
        pair = lax.dynamic_index_in_dim(pairs, (chip + step) % chips, 0, keepdims=False)
        if step:
            pair = lax.ppermute(pair, "col", [(c, (c + 2 * step) % n_col) for c in range(n_col)])
        got.append(pair)

    def from_chips(wanted):
        ordered_by = [lax.dynamic_index_in_dim(p, wanted, 0, keepdims=False) for p in got]
        return jnp.stack(ordered_by)

    mine = from_chips(core)
    other = lax.ppermute(from_chips(1 - core), "col", [(c, c ^ 1) for c in range(n_col)])
    both = jnp.stack([jnp.where(core == 0, mine, other), jnp.where(core == 0, other, mine)], 1)
    placed = [
        lax.dynamic_index_in_dim(both, (chip + chips - k) % chips, 0, keepdims=False)
        for k in range(chips)
    ]
    return jnp.stack(placed).reshape((n_col,) + x.shape[2:])


def ordered(key, valid, span):
    count = key.shape[0]
    key = jnp.where(valid, key, span)
    index = jnp.arange(count, dtype=i32)
    ahead = (key[None, :] < key[:, None]) | (
        (key[None, :] == key[:, None]) & (index[None, :] < index[:, None])
    )
    rank = jnp.sum(ahead.astype(i32), axis=1)
    chosen = rank[None, :] == index[:, None]
    order = jnp.sum(jnp.where(chosen, index[None, :], 0), axis=1)
    return order, jnp.sum(jnp.where(chosen, key[None, :], 0), axis=1), key


def body(tiles, dest, block_row, block_col, rows_from, cols_from, initial, pattern):
    n_front = lax.axis_size("front")
    n_row = lax.axis_size("row")
    n_col = lax.axis_size("col")
    my_row = lax.axis_index("row")
    my_col = lax.axis_index("col")
    row_blocks = ORDER // n_row // BS
    col_blocks = ORDER // n_col // BS
    lead = PIV // BS
    slots = n_front * n_row * CAP
    target = dest[:, 0]
    owner_row = target % n_row
    local_row = jnp.where(owner_row == 0, lead + block_row % (row_blocks - lead), block_row)
    block_id = local_row * col_blocks + block_col
    same = (target[:, None] == target[None, :]).astype(i32)
    slot = target * CAP + jnp.sum(jnp.tril(same, -1), axis=1)
    choose = jnp.arange(slots, dtype=i32)[:, None] == slot[None, :]
    labels = jnp.where(
        jnp.any(choose, axis=1), jnp.sum(jnp.where(choose, block_id[None, :], 0), axis=1), -1
    )
    pivot = initial[0, :PIV]
    sent = [lax.ppermute(pivot, "row", [(0, to)]) for to in range(1, n_row)]
    pivot = jnp.where(my_row == 0, pivot, sent[0] + sent[1] + sent[2])
    row = jnp.zeros((1, pivot.shape[1]), f32).at[0, : slot.shape[0]].set(slot.astype(f32))
    near = jnp.concatenate([pivot, jnp.broadcast_to(row, (8, row.shape[1]))])
    near, slot = lax.optimization_barrier((near, slot))
    near = lax.all_gather(near, "col", axis=0)
    corner = near[:, :PIV].transpose(1, 0, 2).reshape(PIV, PIV)
    slot_meta = jnp.append(near[0, PIV, : slot.shape[0]].astype(i32), my_col)

    def send(part):
        return lax.all_to_all(part, ("front", "row"), split_axis=0, concat_axis=0, tiled=True)

    strips, parts = permute(slot, labels, tiles, rows_from, cols_from, slots)
    incoming = [send(parts[0])]
    got = [lax.ppermute(strips[k], "col", [(0, 2 * k)]) for k in range(1, NCHIP)]
    own = jnp.where(my_col == 0, strips[0], got[0] + got[1] + got[2])
    other = lax.ppermute(own[1], "col", [(2 * k, 2 * k + 1) for k in range(NCHIP)])
    first, first_inv = panel(corner[:BS, :BS])
    below = dot(corner[BS:, :BS], first_inv)
    below = jnp.where(pattern[0, 0, 1] == 1, below, jnp.zeros_like(below))
    rest = corner[BS:, BS:] - dot(below, below.T)
    second, second_inv = panel(rest)
    cross = dot(below.T, second_inv)
    other, first, second, first_inv, second_inv, cross = lax.optimization_barrier(
        (other, first, second, first_inv, second_inv, cross)
    )
    slotted = slot_strips(slot_meta, own, other, slots)
    slotted, incoming[0] = lax.optimization_barrier((slotted, incoming[0]))
    names = incoming[0][:, PARTS[0], 0]
    pivot_columns = initial[0].reshape(row_blocks, NSTRIP, STRIP, -1).transpose(1, 0, 2, 3)
    pivot_columns = pivot_columns.reshape(NCHIP, 2, row_blocks * STRIP, -1)
    extra = jnp.broadcast_to(names, (NCHIP, 2, 8, slots))
    got = exchange(jnp.concatenate([pivot_columns, extra], axis=2), my_col, n_col)
    pivot_columns = got[:, : row_blocks * STRIP].reshape(n_col, row_blocks, STRIP, -1)
    first_names = got[0, row_blocks * STRIP].astype(i32)
    names = names.astype(i32)

    valid = names >= 0
    order, sorted_id, key = ordered(names, valid, row_blocks * col_blocks)
    bounds = jnp.arange(row_blocks + 1, dtype=i32)[:, None] * col_blocks
    starts = jnp.sum((key[None, :] < bounds).astype(i32), axis=1)
    in_slab = (first_names >= 0) & (first_names % col_blocks < lead)
    slab_key = (first_names // col_blocks) * lead + first_names % col_blocks
    slab_order, slab_id, _ = ordered(slab_key, in_slab, row_blocks * lead)
    slab_meta = jnp.concatenate(
        [slab_order, slab_id, jnp.sum(in_slab.astype(i32))[None], my_col[None]]
    )

    meta = jnp.concatenate(
        [order, sorted_id % col_blocks, starts, (my_row == 0).astype(i32)[None], my_col[None]]
    )

    strip = slab_strip(slab_meta, pivot_columns, send(slotted))

    blocks = my_row * row_blocks + jnp.arange(row_blocks, dtype=i32)
    flags = lax.dynamic_slice_in_dim(pattern[0], my_row * row_blocks, row_blocks, 1)
    keep = (flags == 1) & (blocks[None, :] > jnp.arange(2, dtype=i32)[:, None])
    keep = jnp.repeat(keep, STRIP, axis=1)[:, :, None]
    strip = strip.reshape(row_blocks * STRIP, PIV)
    one = dot(strip[:, :BS], first_inv)
    one = jnp.where(keep[0], one, jnp.zeros_like(one))
    two = dot(strip[:, BS:], second_inv) - dot(one, cross)
    two = jnp.where(keep[1], two, jnp.zeros_like(two))
    solved = jnp.concatenate([one, two], axis=1).reshape(row_blocks, STRIP, PIV)

    part, solved = lax.optimization_barrier((parts[1], solved))
    rows = lax.all_gather(solved, "row", axis=0)
    incoming.append(send(part))
    part, rows, solved, incoming[1] = lax.optimization_barrier((parts[2], rows, solved, incoming[1]))
    incoming.append(send(part))
    slab = lax.all_gather(solved, "col", axis=0)
    across = exchange(rows.reshape(NCHIP, 2, col_blocks, STRIP, PIV), my_col, n_col)
    return final(meta, slab, across, (first, second), incoming, row_blocks, col_blocks)[None]


def solution(mesh):
    placed = (
        P(("front", "row", "col"), None, None),
        P(("front", "row", "col"), None),
        P(("front", "row", "col")),
        P(("front", "row", "col")),
        P(("front", "row", "col"), None),
        P(("front", "row", "col"), None),
        P("front", "row", "col"),
        P("front", None, None),
    )
    return jax.shard_map(
        body, mesh=mesh, in_specs=placed, out_specs=P("front", "row", "col"), check_vma=False
    )
```

```python
import jax
import jax.numpy as jnp
from jax import lax
from jax.experimental import pallas as pl
from jax.experimental.pallas import tpu as pltpu
from jax.sharding import PartitionSpec as P

ORDER = 10240
BS = 256
CAP = 4
PIV = 512
STRIP = 32
NSTRIP = BS // STRIP
NCHIP = NSTRIP // 2
MARK = 8
PARTS = (96, 88, 72)
OFFSETS = tuple(sum(PARTS[:q]) for q in range(len(PARTS)))
NPART = len(PARTS)
GROUP = 8
RING = 8

HIGH = lax.Precision.HIGHEST
f32, bf16, i32 = jnp.float32, jnp.bfloat16, jnp.int32


def lower_sym(block):
    return jnp.tril(block) + jnp.tril(block, -1).T


def permute_kernel(slot_ref, label_ref, tile_ref, rows_ref, cols_ref, *refs):
    chip_refs, part_refs = refs[:NCHIP], refs[NCHIP : NCHIP + NPART]
    hold, mark, mark_sem, strip_sems, part_sems = refs[NCHIP + NPART :]
    step = pl.program_id(0)

    def marks():
        rows = part_refs[0].at[:, pl.ds(PARTS[0], MARK)]
        return pltpu.make_async_copy(mark, rows, mark_sem)

    @pl.when(step == 0)
    def _():
        def fill(s, carry):
            mark[s] = jnp.full(mark.shape[1:], label_ref[s].astype(f32))
            return carry

        lax.fori_loop(0, mark.shape[0], fill, 0)
        marks().start()

    half = BS // 2
    lane = lax.broadcasted_iota(i32, (BS, half), 1)
    place = lax.broadcasted_iota(i32, (BS, BS), 0)

    def move(g, carry):
        t = step * GROUP + g
        tile = tile_ref[g]
        high = tile.astype(bf16)
        rest = tile - high.astype(f32)
        mid = rest.astype(bf16)
        low = (rest - mid.astype(f32)).astype(bf16)
        parts = jnp.concatenate([high, mid, low], axis=1)
        wanted = jnp.transpose(jnp.broadcast_to(rows_ref[g], (half, BS)))
        pick_rows = jnp.concatenate(
            [jnp.where(wanted == lane + k * half, 1.0, 0.0) for k in range(2)], axis=1
        ).astype(bf16)
        pick_cols = jnp.where(place == cols_ref[g], 1.0, 0.0).astype(bf16)
        moved = jnp.dot(pick_rows, parts, preferred_element_type=f32).astype(bf16)
        out = jnp.dot(moved[:, :BS], pick_cols, preferred_element_type=f32)
        out = out + jnp.dot(moved[:, BS : 2 * BS], pick_cols, preferred_element_type=f32)
        out = out + jnp.dot(moved[:, 2 * BS :], pick_cols, preferred_element_type=f32)
        hold[t] = out
        for k in range(NSTRIP):
            pltpu.make_async_copy(
                hold.at[t, pl.ds(k * STRIP, STRIP)], chip_refs[k // 2].at[k % 2, t], strip_sems.at[t]
            ).start()
        for q in range(NPART):
            pltpu.make_async_copy(
                hold.at[t, pl.ds(OFFSETS[q], PARTS[q])],
                part_refs[q].at[slot_ref[t], pl.ds(0, PARTS[q])],
                part_sems.at[t],
            ).start()
        return carry

    lax.fori_loop(0, GROUP, move, 0, unroll=4)

    @pl.when(step == pl.num_programs(0) - 1)
    def _():
        def finish(t, carry):
            pltpu.make_async_copy(hold.at[t], hold.at[t], strip_sems.at[t]).wait()
            pltpu.make_async_copy(hold.at[t], hold.at[t], part_sems.at[t]).wait()
            return carry

        lax.fori_loop(0, hold.shape[0], finish, 0)
        marks().wait()


def permute(slot, labels, tiles, rows_from, cols_from, slots):
    count = tiles.shape[0]
    out = pl.pallas_call(
        permute_kernel,
        grid_spec=pltpu.PrefetchScalarGridSpec(
            num_scalar_prefetch=2,
            grid=(count // GROUP,),
            in_specs=[
                pl.BlockSpec((GROUP, BS, BS), lambda t, slot, labels: (t, 0, 0)),
                pl.BlockSpec((GROUP, 1, BS), lambda t, slot, labels: (t, 0, 0)),
                pl.BlockSpec((GROUP, 1, BS), lambda t, slot, labels: (t, 0, 0)),
            ],
            out_specs=[pl.BlockSpec(memory_space=pl.ANY)] * (NCHIP + NPART),
            scratch_shapes=[
                pltpu.VMEM((count, BS, BS), f32),
                pltpu.VMEM((slots, MARK, BS), f32),
                pltpu.SemaphoreType.DMA(()),
                pltpu.SemaphoreType.DMA((count,)),
                pltpu.SemaphoreType.DMA((count,)),
            ],
        ),
        out_shape=[jax.ShapeDtypeStruct((2, count, STRIP, BS), f32)] * NCHIP
        + [
            jax.ShapeDtypeStruct((slots, n + (MARK if q == 0 else 0), BS), f32)
            for q, n in enumerate(PARTS)
        ],
        compiler_params=pltpu.CompilerParams(vmem_limit_bytes=58 << 20),
        cost_estimate=pl.CostEstimate(
            flops=12 * count * BS**3, bytes_accessed=12 * count * BS * BS, transcendentals=0
        ),
        name="permute_tiles",
    )(slot, labels, tiles, rows_from[:, None, :], cols_from[:, None, :])
    return list(out[:NCHIP]), list(out[NCHIP:])


def slot_kernel(count, meta, own_ref, other_ref, out_ref, hold, in_sem, sems):
    @pl.when(meta[count] % 2 == 0)
    def _():
        copy = pltpu.make_async_copy(own_ref.at[0], hold, in_sem)
        copy.start()
        copy.wait()

    @pl.when(meta[count] % 2 == 1)
    def _():
        copy = pltpu.make_async_copy(other_ref, hold, in_sem)
        copy.start()
        copy.wait()

    def begin(t, carry):
        pltpu.make_async_copy(hold.at[t], out_ref.at[meta[t]], sems.at[t]).start()
        return carry

    lax.fori_loop(0, count, begin, 0)

    def finish(t, carry):
        pltpu.make_async_copy(hold.at[t], out_ref.at[meta[t]], sems.at[t]).wait()
        return carry

    lax.fori_loop(0, count, finish, 0)


def slot_strips(meta, own, other, slots):
    count = other.shape[0]
    return pl.pallas_call(
        lambda *refs: slot_kernel(count, *refs),
        grid_spec=pltpu.PrefetchScalarGridSpec(
            num_scalar_prefetch=1,
            grid=(1,),
            in_specs=[pl.BlockSpec(memory_space=pl.ANY)] * 2,
            out_specs=pl.BlockSpec(memory_space=pl.ANY),
            scratch_shapes=[
                pltpu.VMEM(other.shape, f32),
                pltpu.SemaphoreType.DMA(()),
                pltpu.SemaphoreType.DMA((count,)),
            ],
        ),
        out_shape=jax.ShapeDtypeStruct((slots, STRIP, BS), f32),
        compiler_params=pltpu.CompilerParams(vmem_limit_bytes=58 << 20),
        cost_estimate=pl.CostEstimate(
            flops=0, bytes_accessed=8 * count * STRIP * BS, transcendentals=0
        ),
        name="slot_strips",
    )(meta, own, other)


def slab_kernel(meta, initial_ref, in_ref, out_ref, ring, sems):
    total = meta[128]
    pieces, width = initial_ref.shape[0], initial_ref.shape[3]

    def copy(g):
        return pltpu.make_async_copy(in_ref.at[meta[g]], ring.at[g % RING], sems.at[g % RING])

    for g in range(RING):

        @pl.when(g < total)
        def _():
            copy(g).start()

    for k in range(pieces):
        out_ref[:, :, k * width : (k + 1) * width] = initial_ref[k]

    @pl.loop(0, total)
    def _(g):
        copy(g).wait()
        spot = meta[64 + g]
        cols = pl.ds(pl.multiple_of((spot % 2) * BS, BS), BS)
        out_ref[spot // 2, :, cols] += ring[g % RING]

        @pl.when(g + RING < total)
        def _():
            copy(g + RING).start()


def slab_strip(meta, initial, incoming):
    pieces, blocks, height, width = initial.shape
    shape = (blocks, height, pieces * width)
    return pl.pallas_call(
        slab_kernel,
        grid_spec=pltpu.PrefetchScalarGridSpec(
            num_scalar_prefetch=1,
            grid=(1,),
            in_specs=[
                pl.BlockSpec(initial.shape, lambda i, meta: (0, 0, 0, 0)),
                pl.BlockSpec(memory_space=pl.ANY),
            ],
            out_specs=pl.BlockSpec(shape, lambda i, meta: (0, 0, 0)),
            scratch_shapes=[
                pltpu.VMEM((RING, height, BS), f32),
                pltpu.SemaphoreType.DMA((RING,)),
            ],
        ),
        out_shape=jax.ShapeDtypeStruct(shape, f32),
        compiler_params=pltpu.CompilerParams(vmem_limit_bytes=32 << 20),
        cost_estimate=pl.CostEstimate(
            flops=0, bytes_accessed=12 * blocks * STRIP * PIV, transcendentals=0
        ),
        name="slab_strip",
    )(meta, initial, incoming)


def halves(x):
    high = x.astype(bf16)
    return high, (x - high.astype(f32)).astype(bf16)


def final_kernel(col_blocks, *refs):
    meta = refs[0]
    slab, first_factor, second_factor = refs[1:4]
    across, incoming = refs[4], refs[5 : 5 + NPART]
    out_ref, a_high, a_low, ring, sems = refs[5 + NPART :]
    b = pl.program_id(0)
    total = meta[138]

    def copies(g):
        return [
            pltpu.make_async_copy(
                incoming[q].at[meta[g], pl.ds(0, PARTS[q])],
                ring.at[g % RING, pl.ds(OFFSETS[q], PARTS[q])],
                sems.at[g % RING, q],
            )
            for q in range(NPART)
        ]

    @pl.when(b == 0)
    def _():
        for g in range(RING):

            @pl.when(g < total)
            def _():
                for c in copies(g):
                    c.start()

        for cb in range(col_blocks):
            high, low = halves(across[:, cb].reshape(BS, PIV).T)
            a_high[:, cb * BS : (cb + 1) * BS] = high
            a_low[:, cb * BS : (cb + 1) * BS] = low

    rows = slab[:, 0].reshape(BS, PIV)
    top = meta[139] == 1
    high, low = halves(jnp.where(jnp.logical_and(top, b < 2), 0.0, rows))
    for cb in range(col_blocks):
        cols = slice(cb * BS, (cb + 1) * BS)
        product = jnp.dot(high, a_low[:, cols], preferred_element_type=f32)
        product = product + jnp.dot(low, a_high[:, cols], preferred_element_type=f32)
        product = product + jnp.dot(high, a_high[:, cols], preferred_element_type=f32)
        out_ref[:, cols] = -product

    @pl.loop(meta[128 + b], meta[129 + b])
    def _(g):
        for c in copies(g):
            c.wait()
        cols = pl.ds(pl.multiple_of(meta[64 + g] * BS, BS), BS)
        out_ref[:, cols] += ring[g % RING]

        @pl.when(g + RING < total)
        def _():
            for c in copies(g + RING):
                c.start()

    @pl.when(meta[140] == 0)
    def _():
        out_ref[:, :BS] = jnp.where(jnp.logical_and(top, b == 0), first_factor[...], rows[:, :BS])
        out_ref[:, BS:PIV] = jnp.where(jnp.logical_and(top, b == 1), second_factor[...], rows[:, BS:])


def final(meta, slab, across, mats, incoming, row_blocks, col_blocks):
    whole = pl.BlockSpec((BS, BS), lambda b, meta: (0, 0))
    return pl.pallas_call(
        lambda *refs: final_kernel(col_blocks, *refs),
        grid_spec=pltpu.PrefetchScalarGridSpec(
            num_scalar_prefetch=1,
            grid=(row_blocks,),
            in_specs=[
                pl.BlockSpec((NSTRIP, 1, STRIP, PIV), lambda b, meta: (0, b, 0, 0)),
            ]
            + [whole] * 2
            + [pl.BlockSpec((NSTRIP, col_blocks, STRIP, PIV), lambda b, meta: (0, 0, 0, 0))]
            + [pl.BlockSpec(memory_space=pl.ANY)] * NPART,
            out_specs=pl.BlockSpec((BS, col_blocks * BS), lambda b, meta: (b, 0)),
            scratch_shapes=[
                pltpu.VMEM((PIV, col_blocks * BS), bf16),
                pltpu.VMEM((PIV, col_blocks * BS), bf16),
                pltpu.VMEM((RING, BS, BS), f32),
                pltpu.SemaphoreType.DMA((RING, NPART)),
            ],
        ),
        out_shape=jax.ShapeDtypeStruct((row_blocks * BS, col_blocks * BS), f32),
        compiler_params=pltpu.CompilerParams(vmem_limit_bytes=48 << 20),
        cost_estimate=pl.CostEstimate(
            flops=6 * row_blocks * col_blocks * BS * BS * PIV,
            bytes_accessed=4 * 2 * row_blocks * col_blocks * BS * BS,
            transcendentals=0,
        ),
        name="place_and_update",
    )(meta, slab, *mats, across, *incoming)


def dot(a, b):
    return jnp.dot(a, b, precision=HIGH)


def inverse(lower):
    size = lower.shape[0]
    eye = jnp.eye(size, dtype=f32)
    scale = jnp.sum(lower * eye, axis=0)
    power = eye - lower / scale[None, :]
    out = eye + power
    for _ in range(6):
        power = dot(power, power)
        out = out + dot(power, out)
    return out / scale[:, None]


def panel(block):
    half = BS // 2
    first = jnp.linalg.cholesky(lower_sym(block[:half, :half]))
    first_inv = inverse(first)
    below = dot(block[half:, :half], first_inv.T)
    second = jnp.linalg.cholesky(lower_sym(block[half:, half:] - dot(below, below.T)))
    second_inv = inverse(second)
    across = -dot(second_inv, dot(below, first_inv))
    zero = jnp.zeros((half, half), f32)
    factor = jnp.block([[first, zero], [below, second]])
    return factor, jnp.block([[first_inv.T, across.T], [zero, second_inv.T]])


def exchange(x, my_col, n_col):
    chip, core = my_col // 2, my_col % 2
    chips = n_col // 2
    pairs = x
    got = []
    for step in range(chips):
        pair = lax.dynamic_index_in_dim(pairs, (chip + step) % chips, 0, keepdims=False)
        if step:
            pair = lax.ppermute(pair, "col", [(c, (c + 2 * step) % n_col) for c in range(n_col)])
        got.append(pair)

    def from_chips(wanted):
        ordered_by = [lax.dynamic_index_in_dim(p, wanted, 0, keepdims=False) for p in got]
        return jnp.stack(ordered_by)

    mine = from_chips(core)
    other = lax.ppermute(from_chips(1 - core), "col", [(c, c ^ 1) for c in range(n_col)])
    both = jnp.stack([jnp.where(core == 0, mine, other), jnp.where(core == 0, other, mine)], 1)
    placed = [
        lax.dynamic_index_in_dim(both, (chip + chips - k) % chips, 0, keepdims=False)
        for k in range(chips)
    ]
    return jnp.stack(placed).reshape((n_col,) + x.shape[2:])


def ordered(key, valid, span):
    count = key.shape[0]
    key = jnp.where(valid, key, span)
    index = jnp.arange(count, dtype=i32)
    ahead = (key[None, :] < key[:, None]) | (
        (key[None, :] == key[:, None]) & (index[None, :] < index[:, None])
    )
    rank = jnp.sum(ahead.astype(i32), axis=1)
    chosen = rank[None, :] == index[:, None]
    order = jnp.sum(jnp.where(chosen, index[None, :], 0), axis=1)
    return order, jnp.sum(jnp.where(chosen, key[None, :], 0), axis=1), key


def body(tiles, dest, block_row, block_col, rows_from, cols_from, initial, pattern):
    n_front = lax.axis_size("front")
    n_row = lax.axis_size("row")
    n_col = lax.axis_size("col")
    my_row = lax.axis_index("row")
    my_col = lax.axis_index("col")
    row_blocks = ORDER // n_row // BS
    col_blocks = ORDER // n_col // BS
    lead = PIV // BS
    slots = n_front * n_row * CAP
    target = dest[:, 0]
    owner_row = target % n_row
    local_row = jnp.where(owner_row == 0, lead + block_row % (row_blocks - lead), block_row)
    block_id = local_row * col_blocks + block_col
    same = (target[:, None] == target[None, :]).astype(i32)
    slot = target * CAP + jnp.sum(jnp.tril(same, -1), axis=1)
    choose = jnp.arange(slots, dtype=i32)[:, None] == slot[None, :]
    labels = jnp.where(
        jnp.any(choose, axis=1), jnp.sum(jnp.where(choose, block_id[None, :], 0), axis=1), -1
    )
    pivot = initial[0, :PIV]
    sent = [lax.ppermute(pivot, "row", [(0, to)]) for to in range(1, n_row)]
    pivot = jnp.where(my_row == 0, pivot, sent[0] + sent[1] + sent[2])
    row = jnp.zeros((1, pivot.shape[1]), f32).at[0, : slot.shape[0]].set(slot.astype(f32))
    near = jnp.concatenate([pivot, jnp.broadcast_to(row, (8, row.shape[1]))])
    near, slot = lax.optimization_barrier((near, slot))
    near = lax.all_gather(near, "col", axis=0)
    corner = near[:, :PIV].transpose(1, 0, 2).reshape(PIV, PIV)
    slot_meta = jnp.append(near[0, PIV, : slot.shape[0]].astype(i32), my_col)

    def send(part):
        return lax.all_to_all(part, ("front", "row"), split_axis=0, concat_axis=0, tiled=True)

    strips, parts = permute(slot, labels, tiles, rows_from, cols_from, slots)
    incoming = [send(parts[0])]
    got = [lax.ppermute(strips[k], "col", [(0, 2 * k)]) for k in range(1, NCHIP)]
    own = jnp.where(my_col == 0, strips[0], got[0] + got[1] + got[2])
    other = lax.ppermute(own[1], "col", [(2 * k, 2 * k + 1) for k in range(NCHIP)])
    first, first_inv = panel(corner[:BS, :BS])
    below = dot(corner[BS:, :BS], first_inv)
    below = jnp.where(pattern[0, 0, 1] == 1, below, jnp.zeros_like(below))
    rest = corner[BS:, BS:] - dot(below, below.T)
    second, second_inv = panel(rest)
    cross = dot(below.T, second_inv)
    other, first, second, first_inv, second_inv, cross = lax.optimization_barrier(
        (other, first, second, first_inv, second_inv, cross)
    )
    slotted = slot_strips(slot_meta, own, other, slots)
    slotted, incoming[0] = lax.optimization_barrier((slotted, incoming[0]))
    names = incoming[0][:, PARTS[0], 0]
    pivot_columns = initial[0].reshape(row_blocks, NSTRIP, STRIP, -1).transpose(1, 0, 2, 3)
    pivot_columns = pivot_columns.reshape(NCHIP, 2, row_blocks * STRIP, -1)
    extra = jnp.broadcast_to(names, (NCHIP, 2, 8, slots))
    got = exchange(jnp.concatenate([pivot_columns, extra], axis=2), my_col, n_col)
    pivot_columns = got[:, : row_blocks * STRIP].reshape(n_col, row_blocks, STRIP, -1)
    first_names = got[0, row_blocks * STRIP].astype(i32)
    names = names.astype(i32)

    valid = names >= 0
    order, sorted_id, key = ordered(names, valid, row_blocks * col_blocks)
    bounds = jnp.arange(row_blocks + 1, dtype=i32)[:, None] * col_blocks
    starts = jnp.sum((key[None, :] < bounds).astype(i32), axis=1)
    in_slab = (first_names >= 0) & (first_names % col_blocks < lead)
    slab_key = (first_names // col_blocks) * lead + first_names % col_blocks
    slab_order, slab_id, _ = ordered(slab_key, in_slab, row_blocks * lead)
    slab_meta = jnp.concatenate(
        [slab_order, slab_id, jnp.sum(in_slab.astype(i32))[None], my_col[None]]
    )

    meta = jnp.concatenate(
        [order, sorted_id % col_blocks, starts, (my_row == 0).astype(i32)[None], my_col[None]]
    )

    strip = slab_strip(slab_meta, pivot_columns, send(slotted))

    blocks = my_row * row_blocks + jnp.arange(row_blocks, dtype=i32)
    flags = lax.dynamic_slice_in_dim(pattern[0], my_row * row_blocks, row_blocks, 1)
    keep = (flags == 1) & (blocks[None, :] > jnp.arange(2, dtype=i32)[:, None])
    keep = jnp.repeat(keep, STRIP, axis=1)[:, :, None]
    strip = strip.reshape(row_blocks * STRIP, PIV)
    one = dot(strip[:, :BS], first_inv)
    one = jnp.where(keep[0], one, jnp.zeros_like(one))
    two = dot(strip[:, BS:], second_inv) - dot(one, cross)
    two = jnp.where(keep[1], two, jnp.zeros_like(two))
    solved = jnp.concatenate([one, two], axis=1).reshape(row_blocks, STRIP, PIV)

    part, solved = lax.optimization_barrier((parts[1], solved))
    rows = lax.all_gather(solved, "row", axis=0)
    incoming.append(send(part))
    part, rows, solved, incoming[1] = lax.optimization_barrier((parts[2], rows, solved, incoming[1]))
    incoming.append(send(part))
    slab = lax.all_gather(solved, "col", axis=0)
    across = exchange(rows.reshape(NCHIP, 2, col_blocks, STRIP, PIV), my_col, n_col)
    return final(meta, slab, across, (first, second), incoming, row_blocks, col_blocks)[None]


def solution(mesh):
    placed = (
        P(("front", "row", "col"), None, None),
        P(("front", "row", "col"), None),
        P(("front", "row", "col")),
        P(("front", "row", "col")),
        P(("front", "row", "col"), None),
        P(("front", "row", "col"), None),
        P("front", "row", "col"),
        P("front", None, None),
    )
    return jax.shard_map(
        body, mesh=mesh, in_specs=placed, out_specs=P("front", "row", "col"), check_vma=False
    )
```
